32 devices in a mesh: shard: 2 (over x), ctx: 4 (over y, core), tp: 4 (over z).
Axes of the slice: x: 2, y: 2, z: 4, core: 2. Of those that a mesh axis runs over, the one named last changes fastest.
Arguments:
- tokens: bfloat16 [2, 16, 196, 768], P('shard', 'ctx', 'tp'), may hold values from -6 to 6
- cotangent: bfloat16 [2, 16, 196, 768], P('shard', 'ctx', 'tp'), may hold values from -6 to 6
- norm_gains: bfloat16 [3, 768], P(None, 'shard'), may hold values from 0.099609375 to 1.8984375
- norm_shifts: bfloat16 [3, 768], P(None, 'shard'), may hold values from -1.5 to 1.5
- qkv_spatial: bfloat16 [3, 768, 768], P(None, 'shard', 'tp'), may hold values from -0.21875 to 0.21875
- proj_spatial: bfloat16 [768, 768], P('tp', 'shard'), may hold values from -0.75 to 0.75
- qkv_temporal: bfloat16 [3, 768, 768], P(None, 'shard', 'tp'), may hold values from -0.21875 to 0.21875
- proj_temporal: bfloat16 [768, 768], P('tp', 'shard'), may hold values from -0.4375 to 0.4375
- up_weight: bfloat16 [768, 3072], P('shard', 'tp'), may hold values from -0.21875 to 0.21875
- down_weight: bfloat16 [3072, 768], P('tp', 'shard'), may hold values from -0.109375 to 0.109375
- out_bias: bfloat16 [3, 768], P(None, 'shard'), may hold values from -1.5 to 1.5
- qv_bias: bfloat16 [2, 2, 768], P(None, None, 'shard'), may hold values from -1.5 to 1.5
- up_bias: bfloat16 [3072], P('shard'), may hold values from -1.5 to 1.5
Outputs:
- activations: bfloat16 [2, 16, 196, 768], P('shard', 'ctx', 'tp')
- token_grad: float32 [2, 16, 196, 768], P('shard', 'ctx', 'tp')
- norm_gains_grad: float32 [3, 768], P(None, ('shard', 'ctx', 'tp'))
- norm_shifts_grad: float32 [3, 768], P(None, ('shard', 'ctx', 'tp'))
- qkv_spatial_grad: float32 [3, 768, 768], P(None, ('shard', 'ctx'), 'tp')
- proj_spatial_grad: float32 [768, 768], P('tp', ('shard', 'ctx'))
- qkv_temporal_grad: float32 [3, 768, 768], P(None, ('shard', 'ctx'), 'tp')
- proj_temporal_grad: float32 [768, 768], P('tp', ('shard', 'ctx'))
- up_weight_grad: float32 [768, 3072], P(('shard', 'ctx'), 'tp')
- down_weight_grad: float32 [3072, 768], P('tp', ('shard', 'ctx'))
- out_bias_grad: float32 [3, 768], P(None, ('shard', 'ctx', 'tp'))
- qv_bias_grad: float32 [2, 2, 768], P(None, None, ('shard', 'ctx', 'tp'))
- up_bias_grad: float32 [3072], P(('shard', 'ctx', 'tp'))
The draws below stay inside these ranges and needn't reach their ends.
All inputs are finite; a program needn't handle non-finite values.
Results may differ from the reference program's by a relative error of at most 0.023.
Values may be sent and summed in bfloat16 or wider, within the bound.
No kernel may reach another device: no remote copies, remote signals or barrier semaphores. Data moves between devices by JAX's collectives and lax.ppermute only.
A program may use at most 128 MiB of HBM per device.

```python
import jax
import jax.numpy as jnp
from jax import lax

D = 768
HEADS = 12
HD = 64
FF = 3072
FRAMES = 16
PATCHES = 196
CLIPS = 2


def with_spikes(array, own_key, source, target, parts, factor):
    owner, partner = [(jnp.arange(array.shape[position]) // (array.shape[position] // parts)).reshape([-1 if axis == position else 1 for axis in range(array.ndim)]) for position in (source, target)]
    chosen = jax.random.permutation(own_key, parts)[partner]
    strong = (owner == chosen) | (owner == (partner + parts // 2) % parts)
    return jnp.where(strong, factor * array, array)


def steps_of(key, shape, shards, least, largest):
    def one(axis_at, shards_of):
        heights = jax.random.uniform(jax.random.fold_in(jax.random.fold_in(key, 6), axis_at), (shards_of,), jnp.float32, least / len(shards), largest / len(shards))
        return jnp.repeat(jnp.exp(heights), shape[axis_at] // shards_of).reshape((-1,) + (1,) * (len(shape) - axis_at - 1))

    level = one(*shards[0])
    for cut in shards[1:]:
        level = level * one(*cut)
    return level


def noise(own_key, dims, scale, most, split=(), held_as=jnp.bfloat16):
    entries = jax.random.normal(own_key, dims, jnp.float32) * scale
    if len(split) > 0:
        entries = steps_of(own_key, dims, split, -0.22, 0.18) * entries
    return jnp.clip(entries, min=-most, max=most).astype(held_as)


def bell_draw_with(stream_key, extent, spread, limit, cuts, heavy, dtype=jnp.bfloat16):
    array = spread * jax.random.normal(stream_key, extent, jnp.float32)
    if cuts:
        array = array * steps_of(stream_key, extent, cuts, -0.22, 0.18)
    return jnp.clip(with_spikes(array, jax.random.fold_in(stream_key, 3), *heavy), -limit, limit).astype(dtype)


def setup_inputs(seed: int = 0) -> dict:
    keys = jax.random.split(jax.random.key(seed), 14)
    return {
        "tokens": noise(keys[0], (CLIPS, FRAMES, PATCHES, D), 1.0, 6.0, ((0, 2), (1, 4), (2, 4))),
        "cotangent": bell_draw_with(keys[1], (CLIPS, FRAMES, PATCHES, D), 1.0, 6.0, ((0, 2), (1, 4), (2, 4)), (0, 3, 2, 2.0)),
        "norm_gains": jnp.clip(1.0 + 0.18 * jax.random.normal(keys[2], (3, D), jnp.float32), 0.099609375, 1.8984375).astype(jnp.bfloat16),
        "norm_shifts": noise(keys[3], (3, D), 0.3, 1.5, ((1, 2),)),
        "qkv_spatial": noise(keys[4], (3, D, D), D ** -0.5, 0.21875, ((1, 2), (2, 4))),
        "proj_spatial": noise(keys[5], (D, D), (D // 12) ** -0.5, 0.75, ((0, 4), (1, 2))),
        "qkv_temporal": noise(keys[6], (3, D, D), D ** -0.5, 0.21875, ((1, 2), (2, 4))),
        "proj_temporal": noise(keys[7], (D, D), (D // 4) ** -0.5, 0.4375, ((0, 4), (1, 2))),
        "up_weight": noise(keys[8], (D, FF), D ** -0.5, 0.21875, ((0, 2), (1, 4))),
        "down_weight": noise(keys[9], (FF, D), FF ** -0.5, 0.109375, ((0, 4), (1, 2))),
        "out_bias": noise(keys[10], (3, D), 0.3, 1.5, ((1, 2),)),
        "qv_bias": noise(keys[11], (2, 2, D), 0.3, 1.5, ((2, 2),)),
        "up_bias": noise(keys[12], (FF,), 0.3, 1.5, ((0, 2),)),
    }


@jax.custom_vjp
def low(v):
    return lax.optimization_barrier(v.astype(jnp.bfloat16)).astype(jnp.float32)

@jax.custom_vjp
def low_back(v):
    return v

def low_keep(v):
    return (low(v), None)

def low_pass(kept, grad):
    return (grad,)

def back_keep(v):
    return (v, None)

def back_low(kept, grad):
    return (low(grad),)
low.defvjp(low_keep, low_pass)
low_back.defvjp(back_keep, back_low)
highest = lax.Precision.HIGHEST
norm_eps = 1e-06

def round_both(features):
    return low(low_back(features))

def normalize(features, gain_row, shift_row):
    average = lax.optimization_barrier(jnp.mean(features, axis=-1, keepdims=True))
    centered = features - average
    variance = lax.optimization_barrier(jnp.mean(centered * centered, axis=-1, keepdims=True))
    return centered * lax.rsqrt(variance + norm_eps) * gain_row + shift_row

def heads_in(normed, weight_triple, query_bias, value_bias):
    projected = jnp.einsum('fpd,tde->tfpe', normed, weight_triple, precision=highest)
    biases = jnp.stack([query_bias, jnp.zeros_like(query_bias), value_bias])
    return round_both(projected + biases[:, None, None, :])

def attention(queries, key_rows, values, score_form, out_form):
    scores = low_back(jnp.einsum(score_form, queries, key_rows, precision=highest) * HD ** (-0.5))
    shifted = jnp.exp(scores - lax.optimization_barrier(jnp.max(scores, axis=-1, keepdims=True)))
    weights = low(shifted / lax.optimization_barrier(jnp.sum(shifted, axis=-1, keepdims=True)))
    return round_both(jnp.einsum(out_form, weights, values, precision=highest))

def block_forward(tokens_clip, params):
    gain_rows, shift_rows, qkv_spatial, proj_spatial, qkv_temporal, proj_temporal, up_weight, down_weight, out_bias, qv_bias, up_bias = params
    frames, patches, model_width = tokens_clip.shape
    split_shape = (frames, patches, HEADS, HD)
    flat_shape = (frames, patches, model_width)
    normed = low(normalize(tokens_clip, gain_rows[0], shift_rows[0]))
    triple = heads_in(normed, qkv_spatial, qv_bias[0, 0], qv_bias[0, 1])
    attended = attention(triple[0].reshape(split_shape), triple[1].reshape(split_shape), triple[2].reshape(split_shape), 'fqhd,fkhd->fhqk', 'fhqk,fkhd->fqhd')
    branch = jnp.einsum('fpc,cd->fpd', attended.reshape(flat_shape), proj_spatial, precision=highest)
    after_space = tokens_clip + low_back(branch + out_bias[0])
    normed = low(normalize(after_space, gain_rows[1], shift_rows[1]))
    triple = heads_in(normed, qkv_temporal, qv_bias[1, 0], qv_bias[1, 1])
    attended = attention(triple[0].reshape(split_shape), triple[1].reshape(split_shape), triple[2].reshape(split_shape), 'qphd,kphd->phqk', 'phqk,kphd->qphd')
    branch = jnp.einsum('fpc,cd->fpd', attended.reshape(flat_shape), proj_temporal, precision=highest)
    after_time = after_space + low_back(branch + out_bias[1])
    normed = low(normalize(after_time, gain_rows[2], shift_rows[2]))
    hidden_pre = low_back(jnp.einsum('fpd,dh->fph', normed, up_weight, precision=highest) + up_bias)
    activated = low(jax.nn.gelu(hidden_pre, approximate=False))
    branch = jnp.einsum('fph,hd->fpd', activated, down_weight, precision=highest)
    return after_time + low_back(branch + out_bias[2])

def reference(tokens, cotangent, norm_gains, norm_shifts, qkv_spatial, proj_spatial, qkv_temporal, proj_temporal, up_weight, down_weight, out_bias, qv_bias, up_bias):
    params = tuple((argument.astype(jnp.float32) for argument in (norm_gains, norm_shifts, qkv_spatial, proj_spatial, qkv_temporal, proj_temporal, up_weight, down_weight, out_bias, qv_bias, up_bias)))

    def one_clip(totals, pieces):
        tokens_clip, cot_clip = pieces
        result, pull_back = jax.vjp(block_forward, tokens_clip.astype(jnp.float32), params)
        grad_clip, grad_params = pull_back(cot_clip.astype(jnp.float32))
        totals = jax.tree.map(lambda left_term, right_term: left_term + right_term, totals, grad_params)
        return (totals, (result.astype(jnp.bfloat16), grad_clip))
    start_totals = jax.tree.map(jnp.zeros_like, params)
    totals, (activations, token_grad) = lax.scan(one_clip, start_totals, (tokens, cotangent))
    return (activations, token_grad, totals[0], totals[1], totals[2], totals[3], totals[4], totals[5], totals[6], totals[7], totals[8], totals[9], totals[10])
```

```python
import functools

import jax
import jax.numpy as jnp
from jax import lax
from jax.experimental import pallas as pl
from jax.experimental.pallas import tpu as pltpu
from jax.sharding import PartitionSpec as P

HD = 64
EPS = 1e-06
SCALE = HD ** (-0.5)
SLOT = 16
bf16 = jnp.bfloat16
f32 = jnp.float32
VMEM = pl.BlockSpec(memory_space=pltpu.VMEM)
ANY = pl.BlockSpec(memory_space=pl.ANY)
LIMIT = 50 * 1024 * 1024


def nn(a, b):
    return lax.dot_general(a, b, (((1,), (0,)), ((), ())), preferred_element_type=f32)


def nt(a, b):
    return lax.dot_general(a, b, (((1,), (1,)), ((), ())), preferred_element_type=f32)


def tn(a, b):
    return lax.dot_general(a, b, (((0,), (0,)), ((), ())), preferred_element_type=f32)


def standardize(v):
    c = v - jnp.mean(v, axis=-1, keepdims=True)
    r = lax.rsqrt(jnp.mean(c * c, axis=-1, keepdims=True) + EPS)
    return c * r, r


def norm_back(d, q, r, gain):
    e = d * gain
    return r * (e - jnp.mean(e, axis=-1, keepdims=True) - q * jnp.mean(e * q, axis=-1, keepdims=True))


def softmax(q, k, mask):
    s = nt(q * jnp.asarray(SCALE, bf16), k) + mask
    e = jnp.exp(s - jnp.max(s, axis=-1, keepdims=True))
    return e / jnp.sum(e, axis=-1, keepdims=True)


def rows_of(refs):
    return jnp.concatenate([r[...].reshape(-1, r.shape[-1]) for r in refs], axis=0)


def put_rows(refs, value):
    n = value.shape[0] // len(refs)
    for i, r in enumerate(refs):
        r[...] = value[i * n : (i + 1) * n].reshape(r.shape).astype(r.dtype)


class Plan:
    def __init__(self, mesh, model, wide):
        self.sizes = (mesh.shape["shard"], mesh.shape["ctx"], mesh.shape["tp"])
        self.paired = self.sizes == (2, 4, 4)
        self.model, self.wide, self.blocks = model, wide, self.sizes[2]
        self.strips = 8 if self.paired else 1

    def ranks(self):
        return lax.axis_index("shard"), lax.axis_index("ctx"), lax.axis_index("tp")

    def gather(self, local):
        if not self.paired:
            full = lax.all_gather(local, "shard", axis=0, tiled=True)
            return [lax.all_gather(full, "tp", axis=1, tiled=True)[None]]
        rows = local.shape[0] // 4
        own = lax.dynamic_slice_in_dim(local, lax.axis_index("ctx") * rows, rows, 0)
        a = jnp.stack([own] + [shift_z(own, k) for k in (1, 2, 3)])
        x, y = flip_x(a), flip_y(a)
        d1, d2 = flip_x(y[:2]), flip_y(x[2:])
        mine = [a, x, y, d1, d2]
        return mine + [flip_core(v) for v in mine]

    def places(self):
        if not self.paired:
            return [(0, 0, 0, 0)]
        x, q, z = self.ranks()
        out = []
        rows = self.model // 8
        for core in (0, 1):
            for i, (dx, dq, ks) in enumerate(
                ((0, 0, range(4)), (1, 0, range(4)), (0, 2, range(4)), (1, 2, (0, 1)), (1, 2, (2, 3)))
            ):
                for n, k in enumerate(ks):
                    row = ((x ^ dx) * 4 + (q ^ dq ^ core)) * rows
                    col = lax.rem(z + (4 - k), 4) * self.wide
                    out.append((5 * core + i, n, pl.multiple_of(row, rows), pl.multiple_of(col, self.wide)))
        return out

    def start_loads(self, refs, whole, sems):
        copies = []
        for n, (i, k, row, col) in enumerate(self.places()):
            shape = refs[i].shape
            copies.append(
                pltpu.make_async_copy(
                    refs[i].at[k], whole.at[pl.ds(row, shape[1]), pl.ds(col, shape[2])], sems.at[n]
                )
            )
        for c in copies:
            c.start()
        return copies

    def n_loads(self):
        return 32 if self.paired else 1

    def grad_shapes(self):
        rows = self.model // self.strips
        if self.paired:
            return [jax.ShapeDtypeStruct((2, 2, 4, rows, self.wide), bf16)] * 2
        return [jax.ShapeDtypeStruct((1, 1, self.blocks, rows, self.wide), bf16)]

    def grad_scratch(self):
        rows = self.model // self.strips
        if self.paired:
            return pltpu.VMEM((self.blocks, 2, 2, 2, rows, self.wide), bf16)
        return pltpu.VMEM((self.blocks, 1, 1, 1, rows, self.wide), bf16)

    def n_stores(self):
        return self.blocks * (2 if self.paired else 1)

    def start_stores(self, j, value, held, outs, sems):
        value = value.astype(bf16)
        if not self.paired:
            held[j, 0, 0, 0] = value
            c = pltpu.make_async_copy(held.at[j, 0], outs[0].at[:, :, j], sems.at[j])
            c.start()
            return [c]
        x, q, z = self.ranks()
        rows = self.model // 8
        for i in range(8):
            at = q ^ (i & 3)
            held[j, at & 1, at >> 1, x ^ (i >> 2)] = value[i * rows : (i + 1) * rows]
        slot = lax.rem(j + 4 - z, 4)
        copies = []
        for core in (0, 1):
            copies.append(
                pltpu.make_async_copy(held.at[j, core], outs[core].at[:, :, slot], sems.at[2 * j + core])
            )
            copies[-1].start()
        return copies

    def reduce(self, outs):
        if not self.paired:
            g = outs[0][0, 0].astype(f32)
            g = lax.psum_scatter(g, ("shard", "ctx"), scatter_dimension=1, tiled=True)
            return lax.psum_scatter(g, "tp", scatter_dimension=0, tiled=True)[0]
        keep, send = outs
        got = flip_core(send)

        def add(u, v):
            return (u.astype(f32) + v.astype(f32)).astype(bf16)

        send_a = add(keep[:, 1, :2], got[:, 1, :2])
        send_b = add(keep[1, :, 2:], got[1, :, 2:])
        got_a, got_b = flip_x(send_a), flip_y(send_b)
        keep_a = add(keep[:, 0, :2], got[:, 0, :2])
        keep_b = add(keep[0, :, 2:], got[0, :, 2:])
        next_a = add(keep_a[1], got_a[1])
        next_b = add(keep_b[1], got_b[1])
        last_a, last_b = flip_y(next_a), flip_x(next_b)

        def total(u, v, w):
            return u.astype(f32) + v.astype(f32) + w.astype(f32)

        parts = [total(keep_a[0, i], got_a[0, i], last_a[i]) for i in (0, 1)]
        parts += [total(keep_b[0, i], got_b[0, i], last_b[i]) for i in (0, 1)]
        out = parts[0]
        for k in (1, 2, 3):
            out = out + shift_z(parts[k].astype(bf16), k).astype(f32)
        return out


def flip_x(v):
    return lax.ppermute(v, "shard", [(i, i ^ 1) for i in range(2)])


def flip_ctx(v, e):
    return lax.ppermute(v, "ctx", [(i, i ^ e) for i in range(4)])


def flip_core(v):
    return flip_ctx(v, 1)


def flip_y(v):
    return flip_ctx(v, 2)


def shift_z(v, k):
    return lax.ppermute(v, "tp", [(i, (i + k) % 4) for i in range(4)])


def lay_out_kernel(x_ref, c_ref, *outs):
    z, q = lax.axis_index("tp"), lax.axis_index("ctx")
    xs, cs = outs
    for ref, out in ((x_ref, xs), (c_ref, cs)):
        patches = ref.shape[1]
        step = -(-patches // 4)
        for f in range(4):
            v = ref[f].astype(f32)
            for b in range(4):
                part = v[b * step : min((b + 1) * step, patches)]
                part = jnp.concatenate(
                    [part, jnp.zeros((SLOT - part.shape[0], part.shape[1]), f32)], axis=0
                )
                out[lax.rem(f + 4 - z, 4), b ^ q] = part.astype(out.dtype)


def lay_out(x, c):
    shape = jax.ShapeDtypeStruct((4, 4, SLOT, x.shape[-1]), bf16)
    return pl.pallas_call(
        lay_out_kernel,
        out_shape=[shape, shape],
        in_specs=[VMEM] * 2,
        out_specs=[VMEM] * 2,
        compiler_params=pltpu.CompilerParams(vmem_limit_bytes=LIMIT),
        name="lay_out",
    )(x, c)


def bring_back(parts, frames_first, patches, dtype):
    width = parts[0].shape[-1]

    def kernel(*refs):
        z, q = lax.axis_index("tp"), lax.axis_index("ctx")
        ins, out, held = refs[:4], refs[4], refs[5]
        step = -(-patches // 4)
        for i, r in enumerate(ins):
            if frames_first:
                held[i] = r[...].astype(f32)
            else:
                held[:, i] = r[...].astype(f32)
        for f in range(4):
            s = lax.rem(f + 4 - z, 4)
            rows = [held[s, b ^ q][: min(step, patches - b * step)] for b in range(4)]
            out[f] = jnp.concatenate(rows, axis=0).astype(out.dtype)

    return pl.pallas_call(
        kernel,
        out_shape=jax.ShapeDtypeStruct((4, patches, width), dtype),
        in_specs=[VMEM] * 4,
        out_specs=VMEM,
        scratch_shapes=[pltpu.VMEM((4, 4, SLOT, width), f32)],
        compiler_params=pltpu.CompilerParams(vmem_limit_bytes=LIMIT),
        name="bring_back",
    )(*parts)


def turn(parts):
    def kernel(*refs):
        for i in range(4):
            for k in range(4):
                refs[4 + k][i] = refs[i][k]

    shape = jax.ShapeDtypeStruct(parts[0].shape, parts[0].dtype)
    return pl.pallas_call(
        kernel,
        out_shape=[shape] * 4,
        in_specs=[VMEM] * 4,
        out_specs=[VMEM] * 4,
        compiler_params=pltpu.CompilerParams(vmem_limit_bytes=LIMIT),
        name="turn",
    )(*parts)


def swap_z_out(parts):
    return [parts[0]] + [shift_z(parts[k], k) for k in (1, 2, 3)]


def swap_z_back(parts):
    return [parts[0]] + [shift_z(parts[k], 4 - k) for k in (1, 2, 3)]


def swap_ctx(parts):
    return [parts[0]] + [flip_ctx(parts[e], e) for e in (1, 2, 3)]


def time_mask(rows):
    a = lax.broadcasted_iota(jnp.int32, (rows, rows), 0)
    b = lax.broadcasted_iota(jnp.int32, (rows, rows), 1)
    return jnp.where(((a ^ b) & (SLOT - 1)) == 0, 0.0, -1e30).astype(f32)


def attention_forward(plan, timed, head_cols):
    heads = head_cols // HD
    three = 3 * head_cols

    def kernel(*refs):
        refs = list(refs)

        def take(n):
            got, refs[:] = refs[:n], refs[n:]
            return got

        x_refs = take(4)
        b_refs = take(4) if timed else []
        (gain, shift, qv, mask_ref, bias_in) = take(5)
        w_refs = take(10 if plan.paired else 1)
        (p_ref, o_ref) = take(2)
        outs = take(2) if timed else take(4)
        whole, sems = take(2)
        loads = plan.start_loads(w_refs, whole, sems)
        x = rows_of(x_refs).astype(f32)
        if timed:
            x = x + rows_of(b_refs).astype(f32) + bias_in[0:1]
            outs[0][...] = x
            mask = time_mask(x.shape[0])
        else:
            mask = mask_ref[...]
        q, _ = standardize(x)
        n = (q * gain[...] + shift[...]).astype(bf16)
        for c in loads:
            c.wait()
        total = jnp.zeros(x.shape, f32)
        for j in range(plan.blocks):
            at = j * plan.wide
            p = (nn(n, whole[:, at : at + three]) + qv[j : j + 1]).astype(bf16)
            p_ref[j] = p
            attended = []
            for h in range(heads):
                qh = p[:, h * HD : (h + 1) * HD]
                kh = p[:, head_cols + h * HD : head_cols + (h + 1) * HD]
                vh = p[:, 2 * head_cols + h * HD : 2 * head_cols + (h + 1) * HD]
                attended.append(nn(softmax(qh, kh, mask).astype(bf16), vh))
            o = jnp.concatenate(attended, axis=-1).astype(bf16)
            o_ref[j] = o
            total = total + nt(o, whole[:, at + three : at + plan.wide])
        if timed:
            outs[1][...] = x + total + bias_in[1:2]
        else:
            put_rows(outs, total)

    return kernel


def attention_backward(plan, timed, head_cols):
    heads = head_cols // HD
    three = 3 * head_cols

    def kernel(*refs):
        refs = list(refs)

        def take(n):
            got, refs[:] = refs[:n], refs[n:]
            return got

        if timed:
            (x_ref, g_ref) = take(2)
        else:
            x_refs, g_refs = take(4), take(4)
        (gain, shift, mask_ref, p_ref, o_ref) = take(5)
        w_refs = take(10 if plan.paired else 1)
        grads = take(len(plan.grad_shapes()))
        sums, qv_sums = take(2)
        outs = take(4)
        whole, sems, held, out_sems = take(4)
        loads = plan.start_loads(w_refs, whole, sems)
        if timed:
            x, g = x_ref[...], g_ref[...]
            mask = time_mask(x.shape[0])
        else:
            x, g = rows_of(x_refs).astype(f32), rows_of(g_refs).astype(f32)
            mask = mask_ref[...]
        q, r = standardize(x)
        n_t = (q * gain[...] + shift[...]).T.astype(bf16)
        g_b = g.astype(bf16)
        g_t = g_b.astype(f32).T.astype(bf16)
        sums[2:3] = jnp.sum(g_b.astype(f32), axis=0, keepdims=True)
        for c in loads:
            c.wait()
        d_n = jnp.zeros(x.shape, f32)
        stores = []
        for j in range(plan.blocks):
            at = j * plan.wide
            p, o = p_ref[j], o_ref[j]
            d_o = nn(g_b, whole[:, at + three : at + plan.wide]).astype(bf16)
            d_q, d_k, d_v = [], [], []
            for h in range(heads):
                qh = p[:, h * HD : (h + 1) * HD]
                kh = p[:, head_cols + h * HD : head_cols + (h + 1) * HD]
                vh = p[:, 2 * head_cols + h * HD : 2 * head_cols + (h + 1) * HD]
                doh = d_o[:, h * HD : (h + 1) * HD]
                w = softmax(qh, kh, mask)
                d_v.append(tn(w.astype(bf16), doh))
                d_w = nt(doh, vh)
                inner = jnp.sum(d_w * w, axis=-1, keepdims=True)
                d_s = (w * (d_w - inner)).astype(bf16)
                d_q.append(nn(d_s, kh) * SCALE)
                d_k.append(tn(d_s, qh) * SCALE)
            d_p = jnp.concatenate(d_q + d_k + d_v, axis=-1).astype(bf16)
            qv_sums[j : j + 1] = jnp.sum(d_p.astype(f32), axis=0, keepdims=True)
            block = jnp.concatenate([nn(n_t, d_p), nn(g_t, o)], axis=-1)
            stores += plan.start_stores(j, block, held, grads, out_sems)
            d_n = d_n + nt(d_p, whole[:, at : at + three])
        sums[0:1] = jnp.sum(d_n * q, axis=0, keepdims=True)
        sums[1:2] = jnp.sum(d_n, axis=0, keepdims=True)
        put_rows(outs, g + norm_back(d_n, q, r, gain[...]))
        for c in stores:
            c.wait()

    return kernel


def mlp_kernel(plan):
    def kernel(*refs):
        refs = list(refs)

        def take(n):
            got, refs[:] = refs[:n], refs[n:]
            return got

        (x_ref,) = take(1)
        g_refs = take(4)
        gain, shift, up_bias, out_bias = take(4)
        n_w = 10 if plan.paired else 1
        up_refs, down_refs = take(n_w), take(n_w)
        n_g = len(plan.grad_shapes())
        up_grads, down_grads = take(n_g), take(n_g)
        sums, up_sums, back = take(3)
        outs = take(4)
        up, down, up_sem, down_sem, up_held, down_held, up_out, down_out = take(8)
        up_loads = plan.start_loads(up_refs, up, up_sem)
        down_loads = plan.start_loads(down_refs, down, down_sem)
        x = x_ref[...]
        g = rows_of(g_refs)
        g_t = g.astype(f32).T.astype(bf16)
        q, r = standardize(x)
        n32 = q * gain[...] + shift[...]
        n, n_t = n32.astype(bf16), n32.T.astype(bf16)
        for c in up_loads + down_loads:
            c.wait()
        total = jnp.zeros(x.shape, f32)
        d_n = jnp.zeros(x.shape, f32)
        stores = []
        for j in range(plan.blocks):
            cols = slice(j * plan.wide, (j + 1) * plan.wide)
            u = nn(n, up[:, cols]) + up_bias[j : j + 1]
            half = 0.5 * (1.0 + lax.erf(u * (0.5**0.5)))
            z = (u * half).astype(bf16)
            slope = half + u * (jnp.exp(-0.5 * u * u) * 0.3989422804014327)
            d_u = (nn(g, down[:, cols]) * slope).astype(bf16)
            stores += plan.start_stores(j, nn(g_t, z), down_held, down_grads, down_out)
            stores += plan.start_stores(j, nn(n_t, d_u), up_held, up_grads, up_out)
            total = total + nt(z, down[:, cols])
            d_n = d_n + nt(d_u, up[:, cols])
            up_sums[j : j + 1] = jnp.sum(d_u.astype(f32), axis=0, keepdims=True)
        put_rows(outs, x + total + out_bias[...])
        sums[0:1] = jnp.sum(d_n * q, axis=0, keepdims=True)
        sums[1:2] = jnp.sum(d_n, axis=0, keepdims=True)
        sums[2:3] = jnp.sum(g.astype(f32), axis=0, keepdims=True)
        back[...] = g.astype(f32) + norm_back(d_n, q, r, gain[...])
        for c in stores:
            c.wait()

    return kernel


def call(kernel, ins, n_any, outs, n_any_out, scratch, name, flops, any_first=False):
    moved = sum(v.size * v.dtype.itemsize for v in list(ins) + list(outs))
    return pl.pallas_call(
        kernel,
        out_shape=outs,
        in_specs=[VMEM] * (len(ins) - n_any) + [ANY] * n_any,
        out_specs=[ANY] * n_any_out + [VMEM] * (len(outs) - n_any_out),
        scratch_shapes=scratch,
        compiler_params=pltpu.CompilerParams(vmem_limit_bytes=LIMIT),
        cost_estimate=pl.CostEstimate(flops=flops, bytes_accessed=moved, transcendentals=0),
        name=name,
    )(*ins)


def on_device(
    mesh,
    tokens,
    cotangent,
    norm_gains,
    norm_shifts,
    qkv_spatial,
    proj_spatial,
    qkv_temporal,
    proj_temporal,
    up_weight,
    down_weight,
    out_bias,
    qv_bias,
    up_bias,
):
    shards = mesh.shape["shard"]
    blocks = mesh.shape["tp"]
    patches, model = tokens.shape[2:]
    head_cols = qkv_spatial.shape[2]
    wide = 4 * head_cols
    rows = 16 * SLOT
    plan = Plan(mesh, model, wide)
    x_rank, q_rank, z_rank = plan.ranks()

    part = norm_gains.shape[1]
    n_up = up_bias.shape[0] // part
    small = jnp.concatenate(
        [norm_gains, norm_shifts, out_bias, qv_bias.reshape(-1, part), up_bias.reshape(n_up, part)], axis=0
    )
    if plan.paired:
        other = flip_x(small)
        first = jnp.where(x_rank == 0, small, other)
        second = jnp.where(x_rank == 0, other, small)
        small = jnp.stack([first, second])
    else:
        small = lax.all_gather(small, "shard", axis=0, tiled=False)
    small = small.astype(f32)
    vectors = jnp.swapaxes(small[:, :13], 0, 1).reshape(13, model)
    gains, shifts, biases = vectors[0:3], vectors[3:6], vectors[6:9]
    qv = vectors[9:13].reshape(2, 2, blocks, head_cols)
    qv = jnp.concatenate([qv[:, 0], jnp.zeros_like(qv[:, 0]), qv[:, 1]], axis=-1)
    up_b = small[:, 13:].reshape(blocks, -1)

    def joined(qkv, proj):
        return jnp.concatenate([qkv[0], qkv[1], qkv[2], proj.T], axis=1)

    w_space = plan.gather(joined(qkv_spatial, proj_spatial))
    w_time = plan.gather(joined(qkv_temporal, proj_temporal))
    w_up = plan.gather(up_weight)
    w_down = plan.gather(down_weight.T)
    n_w = len(w_space)

    laid, cot = lay_out(tokens[0], cotangent[0])
    by_patch = [v.reshape(4 * SLOT, model) for v in swap_z_out([laid[s] for s in range(4)])]
    by_frame = swap_ctx([laid[:, e] for e in range(4)])
    cot_frame = swap_ctx([cot[:, e] for e in range(4)])

    step = -(-patches // 4)
    slot = jnp.arange(SLOT)[None, :]
    block = (jnp.arange(4) ^ q_rank)[:, None]
    valid = (slot < step) & (block * step + slot < patches)
    key_mask = jnp.where(valid, 0.0, -1e30).astype(f32).reshape(1, 4 * SLOT)
    key_mask = jnp.tile(key_mask, (1, 4))

    weight_scratch = [pltpu.VMEM((model, blocks * wide), bf16), pltpu.SemaphoreType.DMA((plan.n_loads(),))]
    grad_scratch = [plan.grad_scratch(), pltpu.SemaphoreType.DMA((plan.n_stores(),))]
    grads = plan.grad_shapes()
    p_shape = jax.ShapeDtypeStruct((blocks, rows, 3 * head_cols), bf16)
    o_shape = jax.ShapeDtypeStruct((blocks, rows, head_cols), bf16)
    full = jax.ShapeDtypeStruct((rows, model), f32)
    unit = jax.ShapeDtypeStruct((4, SLOT, model), bf16)
    unit32 = jax.ShapeDtypeStruct((4, SLOT, model), f32)
    sums = jax.ShapeDtypeStruct((3, model), f32)
    qv_sums = jax.ShapeDtypeStruct((blocks, 3 * head_cols), f32)
    proj_flops = 2 * rows * model * wide * blocks

    p1, o1, *branch = call(
        attention_forward(plan, False, head_cols),
        by_patch + [gains[0:1], shifts[0:1], qv[0], key_mask, biases[0:2]] + w_space,
        n_w,
        [p_shape, o_shape] + [unit] * 4,
        0,
        weight_scratch,
        "space_forward",
        2 * proj_flops,
    )
    branch = swap_ctx(turn(swap_z_back(branch)))
    p2, o2, x1, x2 = call(
        attention_forward(plan, True, head_cols),
        by_frame + branch + [gains[1:2], shifts[1:2], qv[1], key_mask, biases[0:2]] + w_time,
        n_w,
        [p_shape, o_shape, full, full],
        0,
        weight_scratch,
        "time_forward",
        2 * proj_flops,
    )
    n_g = len(grads)
    got = call(
        mlp_kernel(plan),
        [x2] + cot_frame + [gains[2:3], shifts[2:3], up_b, biases[2:3]] + w_up + w_down,
        2 * n_w,
        grads + grads + [sums, jax.ShapeDtypeStruct((blocks, wide), f32), full] + [unit] * 4,
        2 * n_g,
        weight_scratch[:1] * 2 + weight_scratch[1:] * 2 + grad_scratch[:1] * 2 + grad_scratch[1:] * 2,
        "mlp",
        6 * proj_flops,
    )
    g_up, g_down = got[:n_g], got[n_g : 2 * n_g]
    mlp_sums, up_sums, g2 = got[2 * n_g : 2 * n_g + 3]
    finished = bring_back(swap_ctx(got[2 * n_g + 3 :]), False, patches, bf16)
    sum_down = plan.reduce(g_down)
    sum_up = plan.reduce(g_up)

    got = call(
        attention_backward(plan, True, head_cols),
        [x1, g2, gains[1:2], shifts[1:2], key_mask, p2, o2] + w_time,
        n_w,
        grads + [sums, qv_sums] + [unit] * 4,
        n_g,
        weight_scratch + grad_scratch,
        "time_backward",
        3 * proj_flops,
    )
    g_time, time_sums, time_qv = got[:n_g], got[n_g], got[n_g + 1]
    g1 = swap_z_out(turn(swap_ctx(got[n_g + 2 :])))
    sum_time = plan.reduce(g_time)

    got = call(
        attention_backward(plan, False, head_cols),
        by_patch + g1 + [gains[0:1], shifts[0:1], key_mask, p1, o1] + w_space,
        n_w,
        grads + [sums, qv_sums] + [unit32] * 4,
        n_g,
        weight_scratch + grad_scratch,
        "space_backward",
        3 * proj_flops,
    )
    g_space, space_sums, space_qv = got[:n_g], got[n_g], got[n_g + 1]
    token_grad = bring_back(swap_z_back(got[n_g + 2 :]), True, patches, f32)
    sum_space = plan.reduce(g_space)

    stacked = jnp.stack([space_sums, time_sums, mlp_sums], axis=1).reshape(9, model)
    qv_all = jnp.stack([space_qv, time_qv]).reshape(2, blocks, 3, head_cols)
    qv_all = jnp.swapaxes(qv_all[:, :, ::2], 1, 2).reshape(4, model)
    vector = jnp.concatenate([stacked, qv_all, up_sums.reshape(-1, model)], axis=0)
    if plan.paired:
        for e in (1, 2):
            vector = vector + flip_ctx(vector, e)
        vector = vector + flip_x(vector)
        for e in (1, 2):
            vector = vector + lax.ppermute(vector, "tp", [(i, i ^ e) for i in range(4)])
    else:
        vector = lax.psum(vector, ("shard", "ctx", "tp"))
    place = (x_rank * mesh.shape["ctx"] + q_rank) * blocks + z_rank
    many = shards * mesh.shape["ctx"] * blocks
    mine = lax.dynamic_slice_in_dim(vector[:13], place * (model // many), model // many, 1)
    hidden = vector[13:].reshape(-1)
    hidden = lax.dynamic_slice_in_dim(hidden, place * (hidden.shape[0] // many), hidden.shape[0] // many, 0)

    def apart(total):
        three = total[:, : 3 * head_cols].reshape(-1, 3, head_cols)
        return jnp.swapaxes(three, 0, 1), total[:, 3 * head_cols :].T

    qkv_space, proj_space = apart(sum_space)
    qkv_time, proj_time = apart(sum_time)
    return (
        finished[None],
        token_grad[None],
        mine[0:3],
        mine[3:6],
        qkv_space,
        proj_space,
        qkv_time,
        proj_time,
        sum_up,
        sum_down.T,
        mine[6:9],
        mine[9:13].reshape(2, 2, -1),
        hidden,
    )


def solution(mesh):
    return jax.shard_map(
        functools.partial(on_device, mesh),
        mesh=mesh,
        in_specs=(
            P("shard", "ctx", "tp", None),
            P("shard", "ctx", "tp", None),
            P(None, "shard"),
            P(None, "shard"),
            P(None, "shard", "tp"),
            P("tp", "shard"),
            P(None, "shard", "tp"),
            P("tp", "shard"),
            P("shard", "tp"),
            P("tp", "shard"),
            P(None, "shard"),
            P(None, None, "shard"),
            P("shard"),
        ),
        out_specs=(
            P("shard", "ctx", "tp", None),
            P("shard", "ctx", "tp", None),
            P(None, ("shard", "ctx", "tp")),
            P(None, ("shard", "ctx", "tp")),
            P(None, ("shard", "ctx"), "tp"),
            P("tp", ("shard", "ctx")),
            P(None, ("shard", "ctx"), "tp"),
            P("tp", ("shard", "ctx")),
            P(("shard", "ctx"), "tp"),
            P("tp", ("shard", "ctx")),
            P(None, ("shard", "ctx", "tp")),
            P(None, None, ("shard", "ctx", "tp")),
            P(("shard", "ctx", "tp")),
        ),
        check_vma=False,
    )
```

```python
import functools

import jax
import jax.numpy as jnp
from jax import lax
from jax.experimental import pallas as pl
from jax.experimental.pallas import tpu as pltpu
from jax.sharding import PartitionSpec as P

HD = 64
EPS = 1e-06
SCALE = HD ** (-0.5)
SLOT = 16
bf16 = jnp.bfloat16
f32 = jnp.float32
VMEM = pl.BlockSpec(memory_space=pltpu.VMEM)
ANY = pl.BlockSpec(memory_space=pl.ANY)


def nn(a, b):
    return lax.dot_general(a, b, (((1,), (0,)), ((), ())), preferred_element_type=f32)


def nt(a, b):
    return lax.dot_general(a, b, (((1,), (1,)), ((), ())), preferred_element_type=f32)


def tn(a, b):
    return lax.dot_general(a, b, (((0,), (0,)), ((), ())), preferred_element_type=f32)


def turned(a):
    return a.astype(f32).T.astype(bf16)


def row_sum(v):
    return jnp.sum(v.astype(f32), axis=0, keepdims=True)


def standardize(v):
    c = v - jnp.mean(v, axis=-1, keepdims=True)
    r = lax.rsqrt(jnp.mean(c * c, axis=-1, keepdims=True) + EPS)
    return c * r, r


def norm_back(d, q, r, gain):
    e = d * gain
    return r * (e - jnp.mean(e, axis=-1, keepdims=True) - q * jnp.mean(e * q, axis=-1, keepdims=True))


def rows_of(parts):
    return jnp.concatenate([v[...].reshape(-1, v.shape[-1]) for v in parts], axis=0)


def put_rows(refs, value):
    n = value.shape[0] // len(refs)
    for i, r in enumerate(refs):
        r[...] = value[i * n : (i + 1) * n].reshape(r.shape).astype(r.dtype)


def put_ctx(refs, value):
    n = value.shape[0] // 4
    for i, to in enumerate((refs[0], refs[1], refs[2].at[0], refs[2].at[1])):
        to[...] = value[i * n : (i + 1) * n].reshape(to.shape).astype(to.dtype)


def like(shape, dtype=bf16):
    return jax.ShapeDtypeStruct(shape, dtype)


class Take:
    def __init__(self, refs):
        self.refs = list(refs)

    def __call__(self, n):
        got, self.refs = self.refs[:n], self.refs[n:]
        return got


def flip_x(v):
    return lax.ppermute(v, "shard", [(i, i ^ 1) for i in range(2)])


def flip_ctx(v, e):
    return lax.ppermute(v, "ctx", [(i, i ^ e) for i in range(4)])


def flip_core(v):
    return flip_ctx(v, 1)


def flip_y(v):
    return flip_ctx(v, 2)


def shift_z(v, k):
    return lax.ppermute(v, "tp", [(i, (i + k) % 4) for i in range(4)])


def swap_z_out(parts):
    return [parts[0]] + [shift_z(parts[k], k) for k in (1, 2, 3)]


def swap_z_back(parts):
    return [parts[0]] + [shift_z(parts[k], 4 - k) for k in (1, 2, 3)]


def swap_ctx(p0, p1, pair):
    far = flip_y(pair)
    return [p0, flip_core(p1), far, flip_core(far)]


def ctx_parts(refs):
    return [refs[0][...], refs[1][...], refs[2][0], refs[3][1]]


def after(value, *others):
    return lax.optimization_barrier((value, others))[0]


class Plan:
    def __init__(self, mesh, model, wide):
        self.sizes = (mesh.shape["shard"], mesh.shape["ctx"], mesh.shape["tp"])
        self.paired = self.sizes == (2, 4, 4)
        self.model, self.wide, self.blocks = model, wide, self.sizes[2]
        self.hidden = wide // 2 if self.paired else wide

    def ranks(self):
        q = lax.axis_index("ctx")
        return lax.axis_index("shard"), q >> 1, q & 1, lax.axis_index("tp")

    def block(self, r):
        if not self.paired:
            return r
        return lax.rem(lax.axis_index("tp") + r, self.blocks)

    def places(self):
        if not self.paired:
            return [(0, 0, 0, self.model, 0)]
        x, y, c, _ = self.ranks()
        rows = self.model // 8
        every = range(4)
        kinds = [(0, 0, every), (1, 0, every), (0, 1, every), (1, 1, every)]
        out = []
        for core in (0, 1):
            for i, (dx, dy, ks) in enumerate(kinds):
                row = (((x ^ dx) * 2 + (y ^ dy)) * 2 + (c ^ core)) * rows
                for n, k in enumerate(ks):
                    out.append((core * 4 + i, n, pl.multiple_of(row, rows), rows, (4 - k) % 4))
        return out

    def n_loads(self):
        return 32 if self.paired else 1

    def start_loads(self, refs, whole, sems):
        copies = []
        for n, (i, k, row, rows, slot) in enumerate(self.places()):
            to = whole.at[pl.ds(row, rows), pl.ds(slot * self.wide, refs[i].shape[-1])]
            copies.append(pltpu.make_async_copy(refs[i].at[k], to, sems.at[n]))
            copies[-1].start()
        return copies

    def start_hidden_loads(self, refs, slots, up, down, sems):
        copies = []
        if self.paired:
            x, y, _, _ = self.ranks()
            rows = self.model // 4
            kinds = [(0, 0, (0, 1)), (1, 0, (0, 1)), (0, 1, (0, 1)), (1, 1, (0,)), (1, 1, (1,))]
            places = []
            for ref, (dx, dy, ks) in zip(refs, kinds):
                row = pl.multiple_of(((x ^ dx) * 2 + (y ^ dy)) * rows, rows)
                places += [(ref.at[n], row, k) for n, k in enumerate(ks)]
        else:
            rows = self.model
            places = [(refs[0].at[r], 0, i) for i, r in enumerate(slots)]
        for n, (source, row, i) in enumerate(places):
            for part, whole in enumerate((up, down)):
                to = whole.at[pl.ds(row, rows), pl.ds(i * self.hidden, self.hidden)]
                copy = pltpu.make_async_copy(source.at[part * rows : (part + 1) * rows], to, sems.at[2 * n + part])
                copy.start()
                copies.append(copy)
        return copies

    def grad_shapes(self):
        if self.paired:
            return [like((2, 2, 4, self.model // 8, self.wide))] * 2
        return [like((self.blocks, self.model, self.wide))]

    def grad_scratch(self):
        if self.paired:
            held = pltpu.VMEM((4, 2, 2, 2, self.model // 8, self.wide), bf16)
            return [held, pltpu.SemaphoreType.DMA((8,))]
        return [
            pltpu.VMEM((self.blocks, self.model, self.wide), bf16),
            pltpu.SemaphoreType.DMA((self.blocks,)),
        ]

    def start_stores(self, r, value, held, outs, sems):
        value = value.astype(bf16)
        if not self.paired:
            held[r] = value
            copies = [pltpu.make_async_copy(held.at[r], outs[0].at[r], sems.at[r])]
        else:
            x, y, c, _ = self.ranks()
            rows = self.model // 8
            for i in range(8):
                held[r, (i & 1) ^ c, ((i >> 1) & 1) ^ y, (i >> 2) ^ x] = value[i * rows : (i + 1) * rows]
            copies = [
                pltpu.make_async_copy(held.at[r, core], outs[core].at[:, :, r], sems.at[2 * r + core])
                for core in (0, 1)
            ]
        for copy in copies:
            copy.start()
        return copies

    def hidden_grad_shapes(self):
        if self.paired:
            return [like((2, self.model // 2, self.hidden))] * 4
        return [like((2, 2 * self.model, self.hidden))]

    def hidden_grad_scratch(self):
        if self.paired:
            held = pltpu.VMEM((2, 2, 2, self.model // 2, self.hidden), bf16)
            return [held, pltpu.SemaphoreType.DMA((4,))]
        return [pltpu.VMEM((2, 2 * self.model, self.hidden), bf16), pltpu.SemaphoreType.DMA((2,))]

    def put_hidden(self, i, part, value, held):
        value = value.astype(bf16)
        if not self.paired:
            held[i, part * self.model : (part + 1) * self.model] = value
            return
        x, y, _, _ = self.ranks()
        rows = self.model // 4
        for n in range(4):
            to = held.at[i, (n & 1) ^ y, (n >> 1) ^ x]
            to[part * rows : (part + 1) * rows] = value[n * rows : (n + 1) * rows]

    def start_hidden(self, i, held, outs, sems):
        if not self.paired:
            copies = [pltpu.make_async_copy(held.at[i], outs[0].at[i], sems.at[i])]
        else:
            copies = []
            for side in (0, 1):
                source = held.at[i, side] if i == 0 else held.at[i, :, side]
                copies.append(pltpu.make_async_copy(source, outs[2 * i + side], sems.at[2 * i + side]))
        for copy in copies:
            copy.start()
        return copies


def call(kernel, ins, n_any, outs, n_any_out, scratch, name, limit, after=()):
    n_in, n_after = len(ins), len(after)

    def run(*refs):
        kernel(*refs[:n_in], *refs[n_in + n_after :])

    ins = list(ins)
    for i in range(n_in - n_any, n_in):
        ins[i] = pltpu.with_memory_space_constraint(ins[i], pltpu.HBM)
    got = pl.pallas_call(
        run,
        out_shape=outs,
        in_specs=[VMEM] * (n_in - n_any) + [ANY] * (n_any + n_after),
        out_specs=[ANY] * n_any_out + [VMEM] * (len(outs) - n_any_out),
        scratch_shapes=scratch,
        compiler_params=pltpu.CompilerParams(vmem_limit_bytes=limit * 2**20),
        name=name,
    )(*ins, *after)
    return list(got)


def add(u, v):
    return (u.astype(f32) + v.astype(f32)).astype(bf16)


def after_core(keep, got):
    rows, wide = keep.shape[-2:]
    cut = 3

    def kernel(k, g, keep_a, send_a, keep_b, send_b):
        for x in (0, 1):
            keep_a[x] = add(k[0, x, :2], g[0, x, :2])
            send_a[x] = add(k[1, x, :2], g[1, x, :2])
        for y in (0, 1):
            keep_b[y] = add(k[y, 0, 2:], g[y, 0, 2:])
            send_b[y] = add(k[y, 1, 2:], g[y, 1, 2:])

    whole = pl.BlockSpec((2, 2, 4, rows // cut, wide), lambda i: (0, 0, 0, i, 0))
    half = pl.BlockSpec((2, 2, rows // cut, wide), lambda i: (0, 0, i, 0))
    return pl.pallas_call(
        kernel,
        grid=(cut,),
        out_shape=[like((2, 2, rows, wide))] * 4,
        in_specs=[whole] * 2,
        out_specs=[half] * 4,
        compiler_params=pltpu.CompilerParams(vmem_limit_bytes=16 * 2**20),
        name="after_core",
    )(keep, got)


def after_side(*pairs):
    def kernel(*refs):
        n = len(pairs)
        for i in range(n):
            k, g = refs[2 * i], refs[2 * i + 1]
            refs[2 * n + 2 * i][...] = add(k[0], g[0])
            refs[2 * n + 2 * i + 1][...] = add(k[1], g[1])

    ins = [v for pair in pairs for v in pair]
    outs = [like(v.shape[1:]) for v in ins]
    return call(kernel, ins, 0, outs, 0, [], "after_side", 24)


def hidden_after_side(pairs):
    def kernel(*refs):
        for i in range(4):
            k, g = refs[2 * i], refs[2 * i + 1]
            rest, send = refs[8 + 2 * (i // 2)], refs[9 + 2 * (i // 2)]
            rest[i % 2] = add(k[0], g[0])
            send[i % 2] = add(k[1], g[1])

    ins = [v for pair in pairs for v in pair]
    return call(kernel, ins, 0, [like(ins[0].shape)] * 4, 0, [], "hidden_after_side", 24)


def after_corner(rest_a, got_a, rest_b, got_b, parts=1):
    rows = rest_a.shape[1] // parts

    def kernel(ra, ga, rb, gb, *outs):
        for p in range(parts):
            at = slice(p * rows, (p + 1) * rows)
            own, *sends = outs[4 * p : 4 * p + 4]
            own[...] = ra[0, at].astype(f32) + ga[0, at].astype(f32)
            sends[0][...] = add(ra[1, at], ga[1, at])
            sends[1][...] = add(rb[0, at], gb[0, at])
            sends[2][...] = add(rb[1, at], gb[1, at])

    shape = (rows,) + rest_a.shape[2:]
    outs = ([like(shape, f32)] + [like(shape)] * 3) * parts
    got = call(kernel, [rest_a, got_a, rest_b, got_b], 0, outs, 0, [], "after_corner", 12)
    return [got[4 * p : 4 * p + 4] for p in range(parts)]


def spread(sends):
    return [shift_z(v, k) for k, v in zip((1, 2, 3), sends)]


def attention_total(own, moved, head_cols):
    rows = own.shape[0]
    three = 3 * head_cols

    def kernel(o, a, b, c, qkv, proj):
        total = o[...] + a[...].astype(f32) + b[...].astype(f32) + c[...].astype(f32)
        for t in range(3):
            qkv[t] = total[:, t * head_cols : (t + 1) * head_cols]
        proj[...] = total[:, three:].T

    outs = [like((3, rows, head_cols), f32), like((head_cols, rows), f32)]
    return call(kernel, [own] + moved, 0, outs, 0, [], "attention_total", 8)


def hidden_total(up, down):
    rows, wide = up[0].shape[0] // 2, up[0].shape[1]

    def kernel(*refs):
        keep, send = refs[8:]
        core = lax.axis_index("ctx") & 1
        for part in (0, 1):
            o, a, b, c = refs[4 * part : 4 * part + 4]
            for half in (0, 1):
                at = slice(half * rows, (half + 1) * rows)
                total = o[at] + a[at].astype(f32) + b[at].astype(f32) + c[at].astype(f32)

                @pl.when(core == half)
                def _(total=total, part=part):
                    keep[part] = total

                @pl.when(core != half)
                def _(total=total, part=part):
                    send[part] = total.astype(bf16)

    outs = [like((2, rows, wide), f32), like((2, rows, wide))]
    return call(kernel, up + down, 0, outs, 0, [], "hidden_total", 8)


def hidden_join(keep, got):
    rows, wide = keep.shape[1:]

    def kernel(k, g, up, down):
        core = lax.axis_index("ctx") & 1
        here, there = pl.multiple_of(core * wide, wide), pl.multiple_of((1 - core) * wide, wide)
        for part, out in enumerate((up, down)):
            out[:, pl.ds(here, wide)] = k[part]
            out[:, pl.ds(there, wide)] = g[part].astype(f32)

    return call(kernel, [keep, got], 0, [like((rows, 2 * wide), f32)] * 2, 0, [], "hidden_join", 8)


def lay_out(x, c):
    frames, patches, width = x.shape
    step = -(-patches // 4)

    def kernel(x_ref, c_ref, *refs):
        by_patch, by_frame, held = refs[:4], refs[4:7], refs[7]
        z, q = lax.axis_index("tp"), lax.axis_index("ctx")
        for i, ref in enumerate((x_ref, c_ref)):
            for f in range(4):
                v = ref[f].astype(f32)
                for b in range(4):
                    part = v[b * step : min((b + 1) * step, patches)]
                    pad = jnp.zeros((SLOT - part.shape[0], width), f32)
                    held[i, f, b] = jnp.concatenate([part, pad], axis=0).astype(bf16)
        for s in range(4):
            f = lax.rem(z + s, 4)
            for e in range(4):
                by_patch[s][e * SLOT : (e + 1) * SLOT] = held[0, f, q ^ e]
                to = by_frame[e] if e < 2 else by_frame[2].at[e - 2]
                to[0, s] = held[0, f, q ^ e]
                to[1, s] = held[1, f, q ^ e]

    both = (2, 4, SLOT, width)
    outs = [like((4 * SLOT, width))] * 4 + [like(both)] * 2 + [like((2,) + both)]
    got = call(kernel, [x, c], 0, outs, 0, [pltpu.VMEM((2, 4, 4, SLOT, width), bf16)], "lay_out", 8)
    return got[:4], got[4:]


def bring_back(parts, frames_first, patches, dtype):
    width = parts[0].shape[-1]
    step = -(-patches // 4)

    def kernel(*refs):
        z, q = lax.axis_index("tp"), lax.axis_index("ctx")
        ins, out, held = refs[:4], refs[4], refs[5]
        for i, v in enumerate([r[...] for r in ins] if frames_first else ctx_parts(ins)):
            v = v.reshape(4, SLOT, width).astype(f32)
            if frames_first:
                held[i] = v
            else:
                held[:, i] = v
        for f in range(4):
            s = lax.rem(f + 4 - z, 4)
            rows = [held[s, b ^ q][: min(step, patches - b * step)] for b in range(4)]
            out[f] = jnp.concatenate(rows, axis=0).astype(out.dtype)

    scratch = [pltpu.VMEM((4, 4, SLOT, width), f32)]
    return call(kernel, parts, 0, [like((4, patches, width), dtype)], 0, scratch, "bring_back", 8)[0]


def to_ctx(parts):
    def kernel(*refs):
        for s in range(4):
            for e in range(4):
                to = refs[4 + e] if e < 2 else refs[6].at[e - 2]
                to[s] = refs[s][e]

    shape = parts[0].shape
    return call(kernel, parts, 0, [like(shape)] * 2 + [like((2,) + shape)], 0, [], "to_ctx", 4)


def to_frames(parts):
    def kernel(*refs):
        for e, v in enumerate(ctx_parts(refs[:4])):
            for s in range(4):
                refs[4 + s][e] = v[s]

    return call(kernel, parts, 0, [like(parts[0].shape)] * 4, 0, [], "to_frames", 4)


def time_mask(rows):
    a = lax.broadcasted_iota(jnp.int32, (rows, rows), 0)
    b = lax.broadcasted_iota(jnp.int32, (rows, rows), 1)
    return jnp.where(((a ^ b) & (SLOT - 1)) == 0, 0.0, -1e30).astype(f32)


def head_slices(p, h, head_cols):
    return [p[:, t * head_cols + h * HD : t * head_cols + (h + 1) * HD] for t in range(3)]


def attention_forward(plan, timed, head_cols, n_w):
    heads = head_cols // HD
    three = 3 * head_cols

    def kernel(*refs):
        take = Take(refs)
        x_refs = take(4)
        b_refs = take(4) if timed else []
        gain, shift, qv, mask_ref, bias_in = take(5)
        next_norm = take(2) if timed else []
        w_refs = take(n_w)
        p_ref, o_ref, log_ref = take(3)
        outs = take(3) if timed else take(4)
        whole, sems = take(2)
        loads = plan.start_loads(w_refs, whole, sems)
        if timed:
            x = rows_of([v[0] for v in ctx_parts(x_refs)]).astype(f32)
            x = x + rows_of(ctx_parts(b_refs)).astype(f32) + bias_in[0:1]
            outs[0][...] = x
            mask = time_mask(x.shape[0])
        else:
            x = rows_of(x_refs).astype(f32)
            mask = mask_ref[...]
        q, _ = standardize(x)
        n = (q * gain[...] + shift[...]).astype(bf16)
        for copy in loads:
            copy.wait()
        total = jnp.zeros(x.shape, f32)
        for r in range(plan.blocks):
            at = r * plan.wide
            p = (nn(n, whole[:, at : at + three]) + qv[plan.block(r)]).astype(bf16)
            p_ref[r] = p
            attended = []
            for h in range(heads):
                qh, kh, vh = head_slices(p, h, head_cols)
                s = nt(qh * jnp.asarray(SCALE, bf16), kh) + mask
                top = jnp.max(s, axis=-1, keepdims=True)
                e = jnp.exp(s - top)
                total_e = jnp.sum(e, axis=-1, keepdims=True)
                log_ref[:, r * heads + h : r * heads + h + 1] = top + jnp.log(total_e)
                attended.append(nn((e / total_e).astype(bf16), vh))
            o = jnp.concatenate(attended, axis=-1).astype(bf16)
            o_ref[r] = o
            total = total + nt(o, whole[:, at + three : at + plan.wide])
        if timed:
            x = x + total + bias_in[1:2]
            outs[1][...] = x
            q, _ = standardize(x)
            outs[2][...] = (q * next_norm[0][...] + next_norm[1][...]).astype(bf16)
        else:
            put_rows(outs, total)

    return kernel


def mlp(plan, slots, groups, rows, first):
    def kernel(*refs):
        take = Take(refs)
        n_refs, g_refs = take(groups), take(groups)
        (up_bias,) = take(1)
        before = [] if first else take(2 * groups + 1)
        w_refs = take(5 if plan.paired else 1)
        grads = take(len(plan.hidden_grad_shapes()))
        outs = take(groups)
        backs = take(groups)
        (up_sums,) = take(1)
        up, down, load_sems, held, out_sems = take(5)
        loads = plan.start_hidden_loads(w_refs, slots, up, down, load_sems)
        n = jnp.concatenate([v[...] for v in n_refs], axis=0)
        g = jnp.concatenate([v[...].reshape(-1, v.shape[-1]) for v in g_refs], axis=0)
        n_t, g_t = turned(n), turned(g)
        if first:
            total = jnp.zeros(n.shape, f32)
            back = jnp.zeros(n.shape, f32)
            up_sums[...] = jnp.zeros(up_sums.shape, f32)
        else:
            total = jnp.concatenate([v[...] for v in before[:groups]], axis=0)
            back = jnp.concatenate([v[...] for v in before[groups : 2 * groups]], axis=0)
            up_sums[...] = before[2 * groups][...]
        side = lax.axis_index("ctx") & 1 if plan.paired else 0
        here = pl.multiple_of(side * plan.hidden, plan.hidden)
        for copy in loads:
            copy.wait()
        stores = []
        for i, r in enumerate(slots):
            cols = slice(i * plan.hidden, (i + 1) * plan.hidden)
            at = plan.block(r)
            u = nn(n, up[:, cols]) + up_bias[at, :, pl.ds(here, plan.hidden)]
            half = 0.5 * (1.0 + lax.erf(u * (0.5**0.5)))
            z = (u * half).astype(bf16)
            slope = half + u * (jnp.exp(-0.5 * u * u) * 0.3989422804014327)
            d_u = (nn(g, down[:, cols]) * slope).astype(bf16)
            plan.put_hidden(i, 0, nn(n_t, d_u), held)
            plan.put_hidden(i, 1, nn(g_t, z), held)
            stores += plan.start_hidden(i, held, grads, out_sems)
            total = total + nt(z, down[:, cols])
            back = back + nt(d_u, up[:, cols])
            up_sums[at, :, pl.ds(here, plan.hidden)] = row_sum(d_u)
        for i in range(groups):
            outs[i][...] = total[i * rows : (i + 1) * rows].astype(outs[i].dtype)
            backs[i][...] = back[i * rows : (i + 1) * rows].astype(backs[i].dtype)
        for copy in stores:
            copy.wait()

    return kernel


def attention_backward(plan, timed, head_cols, n_w, n_back):
    heads = head_cols // HD
    three = 3 * head_cols

    def kernel(*refs):
        take = Take(refs)
        if timed:
            x_ref, next_x = take(2)
            g_refs, back_refs = take(4), take(n_back)
            (next_gain,) = take(1)
        else:
            x_refs, g_refs = take(4), take(4)
            time_vec, up_sums = take(2)
        gain, shift, mask_ref, p_ref, o_ref, log_ref = take(6)
        w_refs = take(n_w)
        grads = take(len(plan.grad_shapes()))
        (vec,) = take(1)
        outs = take(3 if timed else 4)
        whole, sems, held, out_sems, qv_held = take(5)
        loads = plan.start_loads(w_refs, whole, sems)
        g = rows_of(g_refs).astype(f32)
        if timed:
            vec[...] = jnp.zeros(vec.shape, f32)
            x = x_ref[...]
            mask = time_mask(x.shape[0])
            q3, r3 = standardize(next_x[...])
            d = back_refs[0][...].astype(f32)
            for ref in back_refs[1:]:
                d = d + ref[...].astype(f32)
            vec[2:3] = row_sum(d * q3)
            vec[5:6] = row_sum(d)
            vec[8:9] = row_sum(g)
            g = g + norm_back(d, q3, r3, next_gain[...])
            layer = 1
        else:
            x = rows_of(x_refs).astype(f32)
            mask = mask_ref[...]
            vec[...] = time_vec[...]
            for j in range(up_sums.shape[0]):
                vec[13 + j : 14 + j] = up_sums[j]
            layer = 0
        q, r_x = standardize(x)
        n_t = (q * gain[...] + shift[...]).T.astype(bf16)
        g_b = g.astype(bf16)
        g_t = turned(g_b)
        vec[6 + layer : 7 + layer] = row_sum(g_b)
        for copy in loads:
            copy.wait()
        d_n = jnp.zeros(x.shape, f32)
        stores = []
        for r in range(plan.blocks):
            at = r * plan.wide
            p, o = p_ref[r], o_ref[r]
            d_o = nn(g_b, whole[:, at + three : at + plan.wide]).astype(bf16)
            d_q, d_k, d_v = [], [], []
            for h in range(heads):
                qh, kh, vh = head_slices(p, h, head_cols)
                doh = d_o[:, h * HD : (h + 1) * HD]
                s = nt(qh * jnp.asarray(SCALE, bf16), kh) + mask
                w = jnp.exp(s - log_ref[:, r * heads + h : r * heads + h + 1])
                d_v.append(tn(w.astype(bf16), doh))
                d_w = nt(doh, vh)
                inner = jnp.sum(d_w * w, axis=-1, keepdims=True)
                d_s = (w * (d_w - inner)).astype(bf16)
                d_q.append(nn(d_s, kh) * SCALE)
                d_k.append(tn(d_s, qh) * SCALE)
            d_p = jnp.concatenate(d_q + d_k + d_v, axis=-1).astype(bf16)
            qv_held[plan.block(r)] = row_sum(d_p)
            block = jnp.concatenate([nn(n_t, d_p), nn(g_t, o)], axis=-1)
            stores += plan.start_stores(r, block, held, grads, out_sems)
            d_n = d_n + nt(d_p, whole[:, at : at + three])
        vec[layer : layer + 1] = row_sum(d_n * q)
        vec[3 + layer : 4 + layer] = row_sum(d_n)
        for i, t in enumerate((0, 2)):
            whole_row = [qv_held[j][:, t * head_cols : (t + 1) * head_cols] for j in range(plan.blocks)]
            vec[9 + 2 * layer + i : 10 + 2 * layer + i] = jnp.concatenate(whole_row, axis=-1)
        put = put_ctx if timed else put_rows
        put(outs, g + norm_back(d_n, q, r_x, gain[...]))
        for copy in stores:
            copy.wait()

    return kernel


def on_device(
    mesh,
    tokens,
    cotangent,
    norm_gains,
    norm_shifts,
    qkv_spatial,
    proj_spatial,
    qkv_temporal,
    proj_temporal,
    up_weight,
    down_weight,
    out_bias,
    qv_bias,
    up_bias,
):
    shards, _, blocks = mesh.shape["shard"], mesh.shape["ctx"], mesh.shape["tp"]
    patches, model = tokens.shape[2:]
    head_cols = qkv_spatial.shape[2]
    wide = 4 * head_cols
    rows = 16 * SLOT
    plan = Plan(mesh, model, wide)
    paired = plan.paired
    x_rank, z_rank = lax.axis_index("shard"), lax.axis_index("tp")
    q_rank = lax.axis_index("ctx")

    def cut(v, axis, size, at):
        return lax.dynamic_slice_in_dim(v, at * size, size, axis)

    def joined(qkv, proj):
        if paired:
            part = model // 8
            qkv, proj = cut(qkv, 1, part, q_rank), cut(proj, 1, part, q_rank)
        return jnp.concatenate([qkv[0], qkv[1], qkv[2], proj.T], axis=1)

    own_space = joined(qkv_spatial, proj_spatial)
    own_time = joined(qkv_temporal, proj_temporal)
    own_up, own_down = up_weight, down_weight
    if paired:
        part = model // 4
        own_up = cut(cut(own_up, 0, part, q_rank >> 1), 1, plan.hidden, q_rank & 1)
        own_down = cut(cut(own_down, 0, plan.hidden, q_rank & 1), 1, part, q_rank >> 1)
    own_down = own_down.T
    part = norm_gains.shape[1]
    small = [norm_gains, norm_shifts, out_bias, qv_bias.reshape(-1, part), up_bias.reshape(-1, part)]
    small = jnp.concatenate(small, axis=0)
    msg_patch, msg_frame = lay_out(tokens[0], cotangent[0])
    own_hidden = jnp.concatenate([own_up, own_down], axis=0)

    if paired:

        def line(own, m):
            with jax.named_scope(f"line{m}"):
                return [own] + [shift_z(own, k) for k in (1, 2, 3)]

        def sides(a, m):
            with jax.named_scope(f"side{m}"):
                return a, flip_x(a), flip_y(a)

        def corners(x, y, m):
            with jax.named_scope(f"corner{m}"):
                return flip_x(y), flip_y(x)

        def cores(parts, m):
            with jax.named_scope(f"core{m}"):
                return [flip_core(v) for v in parts]

        l0 = line(own_space, 0)
        with jax.named_scope("small"):
            other = flip_x(small)
        with jax.named_scope("frames"):
            frames = swap_ctx(*msg_frame)
        a0, x0, y0 = sides(jnp.stack(after(l0, other)), 0)
        l1 = line(after(own_time, l0), 1)
        a1, x1, y1 = sides(jnp.stack(after(l1, x0, y0, frames[2])), 1)
        with jax.named_scope("line2"):
            l2 = shift_z(after(own_hidden, l1), 2)
        core0 = cores(after([a0, x0, y0], l1), 0)
        with jax.named_scope("corner0"):
            c0 = flip_x(after(y0, x1, y1))
        with jax.named_scope("corner1"):
            c1 = flip_y(x1)
        with jax.named_scope("patches"):
            by_patch = swap_z_out(after(list(msg_patch), l2, core0))
        a2, x2, y2 = sides(jnp.stack(after([own_hidden, l2], c0, c1)), 2)
        core0 += cores([c0], 0)
        with jax.named_scope("line3"):
            own = after(own_hidden, by_patch)
            l3 = [shift_z(own, 3), shift_z(own, 1)]
        w_space = [a0, x0, y0, c0] + core0
        first = jnp.where(x_rank == 0, small, other)
        second = jnp.where(x_rank == 0, other, small)
        small = jnp.stack([first, second])
    else:

        def gathered(v):
            v = lax.all_gather(v, "shard", axis=0, tiled=True)
            return [lax.all_gather(v, "tp", axis=1, tiled=True)[None]]

        w_space, w_time = gathered(own_space), gathered(own_time)
        w_hidden = lax.all_gather(own_hidden.reshape(2, -1, wide), "shard", axis=1, tiled=True)
        w_first = w_second = [lax.all_gather(w_hidden.reshape(1, 2 * model, wide), "tp", axis=0, tiled=True)]
        small = lax.all_gather(small, "shard", axis=0, tiled=False)
        frames = swap_ctx(*msg_frame)
        by_patch = swap_z_out(msg_patch)

    cot = jnp.stack([frames[0][1], frames[1][1], frames[2][0, 1], frames[3][1, 1]])
    small = small.astype(f32)
    vectors = jnp.swapaxes(small[:, :13], 0, 1).reshape(13, model)
    gains, shifts, biases = vectors[0:3], vectors[3:6], vectors[6:9]
    qv = vectors[9:13].reshape(2, 2, blocks, head_cols)
    qv = jnp.concatenate([qv[:, 0], jnp.zeros_like(qv[:, 0]), qv[:, 1]], axis=-1)[:, :, None]
    up_b = small[:, 13:].reshape(blocks, 1, -1)

    step = -(-patches // 4)
    slot = jnp.arange(SLOT)[None, :]
    block = (jnp.arange(4) ^ q_rank)[:, None]
    valid = (slot < step) & (block * step + slot < patches)
    key_mask = jnp.where(valid, 0.0, -1e30).astype(f32).reshape(1, 4 * SLOT)
    key_mask = jnp.tile(key_mask, (1, 4))

    weight_scratch = [
        pltpu.VMEM((model, blocks * wide), bf16),
        pltpu.SemaphoreType.DMA((plan.n_loads(),)),
    ]
    p_shape = like((blocks, rows, 3 * head_cols))
    o_shape = like((blocks, rows, head_cols))
    log_shape = like((rows, 128), f32)
    full = like((rows, model), f32)
    unit = like((4, SLOT, model))

    p1, o1, log1, *branch = call(
        attention_forward(plan, False, head_cols, len(w_space)),
        by_patch + [gains[0:1], shifts[0:1], qv[0], key_mask, biases[0:2]] + w_space,
        len(w_space),
        [p_shape, o_shape, log_shape] + [unit] * 4,
        0,
        weight_scratch,
        "space_forward",
        24,
    )
    if paired:
        a3, x3, y3 = sides(jnp.stack(after(l3, x2, y2)), 3)
        core1 = cores(after([a1, x1, y1, c1], l3), 1)
    with jax.named_scope("branch_z"):
        branch = swap_z_back(branch)
    if paired:
        c2 = corners(*after((x2[1:], y2[:1]), branch, x3, y3), 2)
    with jax.named_scope("branch_ctx"):
        branch = swap_ctx(*to_ctx(branch))
    if paired:
        w_time = [a1, x1, y1, c1] + core1
        c3 = corners(*after((x3[1:], y3[:1]), branch[2], c2), 3)
        w_first, w_second = [a2, x2, y2, *c2], [a3, x3, y3, *c3]
        with jax.named_scope("cot_core"):
            cots = [cot, flip_core(after(cot, w_space))]
    else:
        cots = [cot]

    p2, o2, log2, mid, stream, n3 = call(
        attention_forward(plan, True, head_cols, len(w_time)),
        frames
        + branch
        + [gains[1:2], shifts[1:2], qv[1], key_mask, biases[0:2], gains[2:3], shifts[2:3]]
        + w_time,
        len(w_time),
        [p_shape, o_shape, log_shape, full, full, like((rows, model))],
        0,
        weight_scratch,
        "time_forward",
        24,
    )
    norms = [n3]
    if paired:
        with jax.named_scope("norm_core"):
            norms.append(flip_core(n3))

    groups = len(norms)
    hidden_whole = pltpu.VMEM((model, 2 * plan.hidden), bf16)
    hidden_scratch = [hidden_whole, hidden_whole, pltpu.SemaphoreType.DMA((16,))]
    hidden_scratch += plan.hidden_grad_scratch()
    hidden_grads = plan.hidden_grad_shapes()
    n_g = len(hidden_grads)
    up_shape = like((blocks, 1, wide), f32)
    got = call(
        mlp(plan, (0, 2), groups, rows, True),
        norms + cots + [up_b] + w_first,
        len(w_first),
        hidden_grads + [full] * (2 * groups) + [up_shape],
        n_g,
        hidden_scratch,
        "mlp_first",
        40,
    )
    first_grads, partial = got[:n_g], got[n_g:]
    got = call(
        mlp(plan, (1, 3), groups, rows, False),
        norms + cots + [up_b] + partial + w_second,
        len(w_second),
        hidden_grads + ([full] + [like((rows, model))] * (groups - 1)) * 2 + [up_shape],
        n_g,
        hidden_scratch,
        "mlp_second",
        40,
    )
    second_grads, results, backs, up_sums = got[:n_g], got[n_g : n_g + groups], got[n_g + groups : -1], got[-1]
    if paired:
        with jax.named_scope("hidden_side"):
            first_moved = [flip_y(first_grads[1]), flip_x(first_grads[3])]
            second_moved = [flip_y(second_grads[1]), flip_x(second_grads[3])]
        with jax.named_scope("back_core"):
            backs = [backs[0], flip_core(backs[1])]

    grads = plan.grad_shapes()
    n_g = len(grads)
    grad_scratch = plan.grad_scratch() + [pltpu.VMEM((blocks, 1, 3 * head_cols), f32)]
    vec_shape = like((24, model), f32)
    got = call(
        attention_backward(plan, True, head_cols, len(w_time), groups),
        [mid, stream]
        + [cot[e] for e in range(4)]
        + backs
        + [gains[2:3], gains[1:2], shifts[1:2], key_mask, p2, o2, log2]
        + w_time,
        len(w_time),
        grads + [vec_shape] + [unit] * 2 + [like((2,) + unit.shape)],
        n_g,
        weight_scratch + grad_scratch,
        "time_backward",
        28,
    )
    if paired:
        got, first_moved, second_moved = after((got, first_moved, second_moved))
    g_time, time_vec, g1 = got[:n_g], got[n_g], got[n_g + 1 :]
    with jax.named_scope("g1_ctx"):
        g1 = swap_ctx(*g1)
    if paired:
        with jax.named_scope("time_core"):
            got_time = flip_core(g_time[1])
        pairs = [(first_grads[0], first_moved[0]), (second_grads[0], second_moved[0])]
        pairs += [(first_grads[2], first_moved[1]), (second_grads[2], second_moved[1])]
        hidden_rest_a, send_a, hidden_rest_b, send_b = hidden_after_side(pairs)
        with jax.named_scope("hidden_corner"):
            corner_a, corner_b = flip_x(send_a), flip_y(after(send_b, g1[2]))
    with jax.named_scope("g1_z"):
        g1 = swap_z_out(to_frames(g1))
    if paired:
        keep_ta, send_ta, keep_tb, send_tb = after_core(g_time[0], got_time)
        with jax.named_scope("time_side"):
            side_ta, side_tb = flip_y(after(send_ta, g1)), flip_x(after(send_tb, g1))
        up_parts, down_parts = after_corner(hidden_rest_a, corner_a, hidden_rest_b, corner_b, 2)
        with jax.named_scope("up_line"):
            up_moved = spread(after(up_parts[1:], send_ta))

    got = call(
        attention_backward(plan, False, head_cols, len(w_space), 0),
        by_patch + g1 + [time_vec, up_sums, gains[0:1], shifts[0:1], key_mask, p1, o1, log1] + w_space,
        len(w_space),
        grads + [vec_shape] + [unit] * 4,
        n_g,
        weight_scratch + grad_scratch,
        "space_backward",
        28,
        after=(up_parts[1], send_ta) if paired else (),
    )
    if paired:
        got, side_ta, side_tb, up_moved = after((got, side_ta, side_tb, up_moved))
    g_space, vector, back = got[:n_g], got[n_g], got[n_g + 1 :]

    if paired:
        with jax.named_scope("space_core"):
            got_space = flip_core(g_space[1])
        with jax.named_scope("vectors"):
            vector = vector + flip_core(vector)
        with jax.named_scope("token_grad"):
            back = swap_z_back(back)
        rest_ta, send_ta, rest_tb, send_tb = after_side((keep_ta, side_ta), (keep_tb, side_tb))
        with jax.named_scope("time_corner"):
            corner_ta, corner_tb = flip_x(send_ta), flip_y(send_tb)

        keep_a, send_a, keep_b, send_b = after_core(g_space[0], got_space)
        send_a, send_b = after((send_a, send_b), corner_ta, corner_tb)
        with jax.named_scope("space_side"):
            side_a, side_b = flip_y(send_a), flip_x(send_b)
        with jax.named_scope("down_line"):
            down_moved = spread(after(down_parts[1:], back))
        with jax.named_scope("vectors"):
            vector = vector + flip_y(after(vector, send_a))
        ((own_time_sum, *sends),) = after_corner(rest_ta, corner_ta, rest_tb, corner_tb)

        side_a, side_b, down_moved = after((side_a, side_b, down_moved))
        rest_a, send_a, rest_b, send_b = after_side((keep_a, side_a), (keep_b, side_b))
        with jax.named_scope("space_corner"):
            corner_a, corner_b = flip_x(send_a), flip_y(send_b)
        with jax.named_scope("time_line"):
            time_moved = spread(after(sends, send_a))
        with jax.named_scope("vectors"):
            vector = vector + flip_x(after(vector, send_a))
        hidden_keep, hidden_send = hidden_total(up_parts[:1] + up_moved, down_parts[:1] + down_moved)
        with jax.named_scope("hidden_core"):
            hidden_got = flip_core(hidden_send)

        corner_a, corner_b, time_moved = after((corner_a, corner_b, time_moved))
        ((own, *sends),) = after_corner(rest_a, corner_a, rest_b, corner_b)
        with jax.named_scope("space_line"):
            moved = spread(sends)
        qkv_time, proj_time = attention_total(own_time_sum, time_moved, head_cols)
        grad_up, grad_down = hidden_join(hidden_keep, hidden_got)
        qkv_space, proj_space = attention_total(own, moved, head_cols)
    else:

        def summed(g):
            g = lax.psum_scatter(g.astype(f32), ("shard", "ctx"), scatter_dimension=1, tiled=True)
            return lax.psum_scatter(g, "tp", scatter_dimension=0, tiled=True)[0]

        def apart(total):
            three = total[:, : 3 * head_cols].reshape(-1, 3, head_cols)
            return jnp.swapaxes(three, 0, 1), total[:, 3 * head_cols :].T

        hidden_grad = jnp.concatenate([v[i : i + 1] for i in (0, 1) for v in (first_grads[0], second_grads[0])])
        grad_up, grad_down = summed(hidden_grad[:, :model]), summed(hidden_grad[:, model:])
        qkv_time, proj_time = apart(summed(g_time[0]))
        qkv_space, proj_space = apart(summed(g_space[0]))

    with jax.named_scope("finished"):
        if paired:
            results = [results[0], flip_core(after(results[1], g_space))]

        def finish(*refs):
            total = refs[0][...] + refs[1][...]
            for ref in refs[2 : 1 + groups]:
                total = total + ref[...].astype(f32)
            put_ctx(refs[1 + groups :], total)

        outs = [unit] * 2 + [like((2,) + unit.shape)]
        parts = call(finish, [stream + biases[2:3]] + list(results), 0, outs, 0, [], "finish", 8)
        finished = bring_back(swap_ctx(*parts), False, patches, bf16)
    with jax.named_scope("token_grad"):
        token_grad = bring_back(back if paired else swap_z_back(back), True, patches, f32)

    if paired:
        with jax.named_scope("vectors"):
            vector = after(vector, sends)
            vector = vector + shift_z(vector, 1) + shift_z(vector, 2) + shift_z(vector, 3)
    else:
        vector = lax.psum(vector, ("shard", "ctx", "tp"))
    place = (x_rank * mesh.shape["ctx"] + q_rank) * blocks + z_rank
    many = shards * mesh.shape["ctx"] * blocks
    mine = lax.dynamic_slice_in_dim(vector[:13], place * (model // many), model // many, 1)
    hidden = vector[13 : 13 + blocks * wide // model].reshape(-1)
    hidden = lax.dynamic_slice_in_dim(hidden, place * (hidden.shape[0] // many), hidden.shape[0] // many, 0)
    return (
        finished[None],
        token_grad[None],
        mine[0:3],
        mine[3:6],
        qkv_space,
        proj_space,
        qkv_time,
        proj_time,
        grad_up,
        grad_down.T,
        mine[6:9],
        mine[9:13].reshape(2, 2, -1),
        hidden,
    )


def solution(mesh):
    return jax.shard_map(
        functools.partial(on_device, mesh),
        mesh=mesh,
        in_specs=(
            P("shard", "ctx", "tp", None),
            P("shard", "ctx", "tp", None),
            P(None, "shard"),
            P(None, "shard"),
            P(None, "shard", "tp"),
            P("tp", "shard"),
            P(None, "shard", "tp"),
            P("tp", "shard"),
            P("shard", "tp"),
            P("tp", "shard"),
            P(None, "shard"),
            P(None, None, "shard"),
            P("shard"),
        ),
        out_specs=(
            P("shard", "ctx", "tp", None),
            P("shard", "ctx", "tp", None),
            P(None, ("shard", "ctx", "tp")),
            P(None, ("shard", "ctx", "tp")),
            P(None, ("shard", "ctx"), "tp"),
            P("tp", ("shard", "ctx")),
            P(None, ("shard", "ctx"), "tp"),
            P("tp", ("shard", "ctx")),
            P(("shard", "ctx"), "tp"),
            P("tp", ("shard", "ctx")),
            P(None, ("shard", "ctx", "tp")),
            P(None, None, ("shard", "ctx", "tp")),
            P(("shard", "ctx", "tp")),
        ),
        check_vma=False,
    )
```

```python
import functools

import jax
import jax.numpy as jnp
from jax import lax
from jax.experimental import pallas as pl
from jax.experimental.pallas import tpu as pltpu
from jax.sharding import PartitionSpec as P

HD = 64
EPS = 1e-06
SCALE = HD ** (-0.5)
SLOT = 16
bf16 = jnp.bfloat16
f32 = jnp.float32
VMEM = pl.BlockSpec(memory_space=pltpu.VMEM)
ANY = pl.BlockSpec(memory_space=pl.ANY)


def nn(a, b):
    return lax.dot_general(a, b, (((1,), (0,)), ((), ())), preferred_element_type=f32)


def nt(a, b):
    return lax.dot_general(a, b, (((1,), (1,)), ((), ())), preferred_element_type=f32)


def tn(a, b):
    return lax.dot_general(a, b, (((0,), (0,)), ((), ())), preferred_element_type=f32)


def turned(a):
    return a.astype(f32).T.astype(bf16)


def row_sum(v):
    return jnp.sum(v.astype(f32), axis=0, keepdims=True)


def standardize(v):
    c = v - jnp.mean(v, axis=-1, keepdims=True)
    r = lax.rsqrt(jnp.mean(c * c, axis=-1, keepdims=True) + EPS)
    return c * r, r


def norm_back(d, q, r, gain):
    e = d * gain
    return r * (e - jnp.mean(e, axis=-1, keepdims=True) - q * jnp.mean(e * q, axis=-1, keepdims=True))


def rows_of(parts):
    return jnp.concatenate([v[...].reshape(-1, v.shape[-1]) for v in parts], axis=0)


def put_rows(refs, value):
    n = value.shape[0] // len(refs)
    for i, r in enumerate(refs):
        r[...] = value[i * n : (i + 1) * n].reshape(r.shape).astype(r.dtype)


def put_ctx(refs, value):
    n = value.shape[0] // 4
    for i, to in enumerate((refs[0], refs[1], refs[2].at[0], refs[2].at[1])):
        to[...] = value[i * n : (i + 1) * n].reshape(to.shape).astype(to.dtype)


def like(shape, dtype=bf16):
    return jax.ShapeDtypeStruct(shape, dtype)


class Take:
    def __init__(self, refs):
        self.refs = list(refs)

    def __call__(self, n):
        got, self.refs = self.refs[:n], self.refs[n:]
        return got


def flip_x(v):
    return lax.ppermute(v, "shard", [(i, i ^ 1) for i in range(2)])


def flip_ctx(v, e):
    return lax.ppermute(v, "ctx", [(i, i ^ e) for i in range(4)])


def flip_core(v):
    return flip_ctx(v, 1)


def flip_y(v):
    return flip_ctx(v, 2)


def shift_z(v, k):
    return lax.ppermute(v, "tp", [(i, (i + k) % 4) for i in range(4)])


def swap_z_out(parts):
    return [parts[0]] + [shift_z(parts[k], k) for k in (1, 2, 3)]


def swap_z_back(parts):
    return [parts[0]] + [shift_z(parts[k], 4 - k) for k in (1, 2, 3)]


def swap_ctx(p0, p1, pair):
    far = flip_y(pair)
    return [p0, flip_core(p1), far, flip_core(far)]


def ctx_parts(refs):
    return [refs[0][...], refs[1][...], refs[2][0], refs[3][1]]


def after(value, *others):
    return lax.optimization_barrier((value, others))[0]


class Plan:
    def __init__(self, mesh, model, wide):
        self.sizes = (mesh.shape["shard"], mesh.shape["ctx"], mesh.shape["tp"])
        self.paired = self.sizes == (2, 4, 4)
        self.model, self.wide, self.blocks = model, wide, self.sizes[2]
        self.hidden = wide // 2 if self.paired else wide

    def ranks(self):
        q = lax.axis_index("ctx")
        return lax.axis_index("shard"), q >> 1, q & 1, lax.axis_index("tp")

    def block(self, r):
        if not self.paired:
            return r
        return lax.rem(lax.axis_index("tp") + r, self.blocks)

    def places(self):
        if not self.paired:
            return [(0, 0, 0, self.model, 0)]
        x, y, c, _ = self.ranks()
        rows = self.model // 8
        every = range(4)
        kinds = [(0, 0, every), (1, 0, every), (0, 1, every), (1, 1, every)]
        out = []
        for core in (0, 1):
            for i, (dx, dy, ks) in enumerate(kinds):
                row = (((x ^ dx) * 2 + (y ^ dy)) * 2 + (c ^ core)) * rows
                for n, k in enumerate(ks):
                    out.append((core * 4 + i, n, pl.multiple_of(row, rows), rows, (4 - k) % 4))
        return out

    def n_loads(self):
        return 32 if self.paired else 1

    def start_loads(self, refs, whole, sems):
        by_slot = [[] for _ in range(self.blocks)]
        for n, (i, k, row, rows, slot) in enumerate(self.places()):
            to = whole.at[pl.ds(row, rows), pl.ds(slot * self.wide, refs[i].shape[-1])]
            by_slot[slot].append(pltpu.make_async_copy(refs[i].at[k], to, sems.at[n]))
        for copies in by_slot:
            for copy in copies:
                copy.start()
        return by_slot

    def start_hidden_loads(self, refs, slots, up, down, sems):
        by_slot = [[], []]
        if self.paired:
            x, y, _, _ = self.ranks()
            rows = self.model // 4
            kinds = [(0, 0, (0, 1)), (1, 0, (0, 1)), (0, 1, (0, 1))]
            kinds += [(1, 1, (0, 1))] if len(refs) == 4 else [(1, 1, (0,)), (1, 1, (1,))]
            places = []
            for ref, (dx, dy, ks) in zip(refs, kinds):
                row = pl.multiple_of(((x ^ dx) * 2 + (y ^ dy)) * rows, rows)
                places += [(ref.at[n], row, k) for n, k in enumerate(ks)]
        else:
            rows = self.model
            places = [(refs[0].at[r], 0, i) for i, r in enumerate(slots)]
        for n, (source, row, i) in enumerate(places):
            for part, whole in enumerate((up, down)):
                to = whole.at[pl.ds(row, rows), pl.ds(i * self.hidden, self.hidden)]
                copy = pltpu.make_async_copy(source.at[part * rows : (part + 1) * rows], to, sems.at[2 * n + part])
                by_slot[i].append(copy)
        for copies in by_slot:
            for copy in copies:
                copy.start()
        return by_slot

    def grad_shapes(self):
        if self.paired:
            return [like((2, 2, 4, self.model // 8, self.wide))] * 2
        return [like((self.blocks, self.model, self.wide))]

    def grad_scratch(self):
        if self.paired:
            held = pltpu.VMEM((4, 2, 2, 2, self.model // 8, self.wide), bf16)
            return [held, pltpu.SemaphoreType.DMA((8,))]
        return [
            pltpu.VMEM((self.blocks, self.model, self.wide), bf16),
            pltpu.SemaphoreType.DMA((self.blocks,)),
        ]

    def hold(self, r, value, held):
        value = value.astype(bf16)
        if not self.paired:
            held[r] = value
            return
        x, y, c, _ = self.ranks()
        rows = self.model // 8
        for i in range(8):
            held[r, (i & 1) ^ c, ((i >> 1) & 1) ^ y, (i >> 2) ^ x] = value[i * rows : (i + 1) * rows]

    def store(self, held, outs, sems):
        copies = []
        for r in range(self.blocks):
            if not self.paired:
                copies.append(pltpu.make_async_copy(held.at[r], outs[0].at[r], sems.at[r]))
                continue
            for core in (1, 0):
                to = outs[core].at[:, :, r]
                copies.append(pltpu.make_async_copy(held.at[r, core], to, sems.at[2 * r + core]))
        for copy in copies:
            copy.start()
        for copy in copies:
            copy.wait()

    def hidden_grad_shapes(self):
        if self.paired:
            return [like((2, self.model // 2, self.hidden))] * 4
        return [like((2, 2 * self.model, self.hidden))]

    def hidden_grad_scratch(self):
        if self.paired:
            held = pltpu.VMEM((2, 2, 2, self.model // 2, self.hidden), bf16)
            return [held, pltpu.SemaphoreType.DMA((4,))]
        return [pltpu.VMEM((2, 2 * self.model, self.hidden), bf16), pltpu.SemaphoreType.DMA((2,))]

    def put_hidden(self, i, part, value, held):
        value = value.astype(bf16)
        if not self.paired:
            held[i, part * self.model : (part + 1) * self.model] = value
            return
        x, y, _, _ = self.ranks()
        rows = self.model // 4
        for n in range(4):
            to = held.at[i, (n & 1) ^ y, (n >> 1) ^ x]
            to[part * rows : (part + 1) * rows] = value[n * rows : (n + 1) * rows]

    def start_hidden(self, i, held, outs, sems):
        if not self.paired:
            copies = [pltpu.make_async_copy(held.at[i], outs[0].at[i], sems.at[i])]
        else:
            copies = []
            for side in (0, 1):
                source = held.at[i, side] if i == 0 else held.at[i, :, side]
                copies.append(pltpu.make_async_copy(source, outs[2 * i + side], sems.at[2 * i + side]))
        for copy in copies:
            copy.start()
        return copies


def call(kernel, ins, n_any, outs, n_any_out, scratch, name, limit, after=(), far=None):
    n_in, n_after = len(ins), len(after)

    def run(*refs):
        kernel(*refs[:n_in], *refs[n_in + n_after :])

    ins = list(ins)
    for i, v in enumerate(ins):
        if i >= n_in - n_any or (far is not None and v.size >= far):
            ins[i] = pltpu.with_memory_space_constraint(v, pltpu.HBM)
    got = pl.pallas_call(
        run,
        out_shape=outs,
        in_specs=[VMEM] * (n_in - n_any) + [ANY] * (n_any + n_after),
        out_specs=[ANY] * n_any_out + [VMEM] * (len(outs) - n_any_out),
        scratch_shapes=scratch,
        compiler_params=pltpu.CompilerParams(vmem_limit_bytes=limit * 2**20),
        cost_estimate=pl.CostEstimate(flops=0, bytes_accessed=0, transcendentals=0),
        name=name,
    )(*ins, *after)
    return list(got)


def add(u, v):
    return (u.astype(f32) + v.astype(f32)).astype(bf16)


def after_core(keep, got):
    rows, wide = keep.shape[-2:]
    cut = 3

    def kernel(k, g, keep_a, send_a, keep_b, send_b):
        for x in (0, 1):
            keep_a[x] = add(k[0, x, :2], g[0, x, :2])
            send_a[x] = add(k[1, x, :2], g[1, x, :2])
        for y in (0, 1):
            keep_b[y] = add(k[y, 0, 2:], g[y, 0, 2:])
            send_b[y] = add(k[y, 1, 2:], g[y, 1, 2:])

    whole = pl.BlockSpec((2, 2, 4, rows // cut, wide), lambda i: (0, 0, 0, i, 0))
    half = pl.BlockSpec((2, 2, rows // cut, wide), lambda i: (0, 0, i, 0))
    return pl.pallas_call(
        kernel,
        grid=(cut,),
        out_shape=[like((2, 2, rows, wide))] * 4,
        in_specs=[whole] * 2,
        out_specs=[half] * 4,
        compiler_params=pltpu.CompilerParams(vmem_limit_bytes=16 * 2**20),
        name="after_core",
    )(keep, got)


def after_side(*pairs):
    def kernel(*refs):
        n = len(pairs)
        for i in range(n):
            k, g = refs[2 * i], refs[2 * i + 1]
            refs[2 * n + 2 * i][...] = add(k[0], g[0])
            refs[2 * n + 2 * i + 1][...] = add(k[1], g[1])

    ins = [v for pair in pairs for v in pair]
    outs = [like(v.shape[1:]) for v in ins]
    return call(kernel, ins, 0, outs, 0, [], "after_side", 24)


def hidden_after_side(pairs):
    def kernel(*refs):
        for i in range(4):
            k, g = refs[2 * i], refs[2 * i + 1]
            rest, send = refs[8 + 2 * (i // 2)], refs[9 + 2 * (i // 2)]
            rest[i % 2] = add(k[0], g[0])
            send[i % 2] = add(k[1], g[1])

    ins = [v for pair in pairs for v in pair]
    return call(kernel, ins, 0, [like(ins[0].shape)] * 4, 0, [], "hidden_after_side", 24)


def after_corner(rest_a, got_a, rest_b, got_b, parts=1):
    rows = rest_a.shape[1] // parts

    def kernel(ra, ga, rb, gb, *outs):
        for p in range(parts):
            at = slice(p * rows, (p + 1) * rows)
            own, *sends = outs[4 * p : 4 * p + 4]
            own[...] = ra[0, at].astype(f32) + ga[0, at].astype(f32)
            sends[0][...] = add(ra[1, at], ga[1, at])
            sends[1][...] = add(rb[0, at], gb[0, at])
            sends[2][...] = add(rb[1, at], gb[1, at])

    shape = (rows,) + rest_a.shape[2:]
    outs = ([like(shape, f32)] + [like(shape)] * 3) * parts
    got = call(kernel, [rest_a, got_a, rest_b, got_b], 0, outs, 0, [], "after_corner", 12)
    return [got[4 * p : 4 * p + 4] for p in range(parts)]


def spread(sends):
    return [shift_z(v, k) for k, v in zip((1, 2, 3), sends)]


def attention_total(own, moved, head_cols):
    rows = own.shape[0]
    three = 3 * head_cols

    def kernel(o, a, b, c, qkv, proj):
        total = o[...] + a[...].astype(f32) + b[...].astype(f32) + c[...].astype(f32)
        for t in range(3):
            qkv[t] = total[:, t * head_cols : (t + 1) * head_cols]
        proj[...] = total[:, three:].T

    outs = [like((3, rows, head_cols), f32), like((head_cols, rows), f32)]
    return call(kernel, [own] + moved, 0, outs, 0, [], "attention_total", 8, far=2**15)


def hidden_total(up, down):
    rows, wide = up[0].shape[0] // 2, up[0].shape[1]

    def kernel(*refs):
        keep, send = refs[8:]
        core = lax.axis_index("ctx") & 1
        for part in (0, 1):
            o, a, b, c = refs[4 * part : 4 * part + 4]
            for half in (0, 1):
                at = slice(half * rows, (half + 1) * rows)
                total = o[at] + a[at].astype(f32) + b[at].astype(f32) + c[at].astype(f32)

                @pl.when(core == half)
                def _(total=total, part=part):
                    keep[part] = total

                @pl.when(core != half)
                def _(total=total, part=part):
                    send[part] = total.astype(bf16)

    outs = [like((2, rows, wide), f32), like((2, rows, wide))]
    return call(kernel, up + down, 0, outs, 0, [], "hidden_total", 8)


def hidden_join(keep, got):
    rows, wide = keep.shape[1:]

    def kernel(k, g, up, down):
        core = lax.axis_index("ctx") & 1
        here, there = pl.multiple_of(core * wide, wide), pl.multiple_of((1 - core) * wide, wide)
        for part, out in enumerate((up, down)):
            out[:, pl.ds(here, wide)] = k[part]
            out[:, pl.ds(there, wide)] = g[part].astype(f32)

    return call(kernel, [keep, got], 0, [like((rows, 2 * wide), f32)] * 2, 0, [], "hidden_join", 8)


def lay_out(x, c):
    frames, patches, width = x.shape
    step = -(-patches // 4)

    def kernel(x_ref, c_ref, *refs):
        by_patch, by_frame, held = refs[:4], refs[4:7], refs[7]
        z, q = lax.axis_index("tp"), lax.axis_index("ctx")
        for i, ref in enumerate((x_ref, c_ref)):
            for f in range(4):
                v = ref[f].astype(f32)
                for b in range(4):
                    part = v[b * step : min((b + 1) * step, patches)]
                    pad = jnp.zeros((SLOT - part.shape[0], width), f32)
                    held[i, f, b] = jnp.concatenate([part, pad], axis=0).astype(bf16)
        for s in range(4):
            f = lax.rem(z + s, 4)
            for e in range(4):
                by_patch[s][e * SLOT : (e + 1) * SLOT] = held[0, f, q ^ e]
                to = by_frame[e] if e < 2 else by_frame[2].at[e - 2]
                to[0, s] = held[0, f, q ^ e]
                to[1, s] = held[1, f, q ^ e]

    both = (2, 4, SLOT, width)
    outs = [like((4 * SLOT, width))] * 4 + [like(both)] * 2 + [like((2,) + both)]
    got = call(kernel, [x, c], 0, outs, 0, [pltpu.VMEM((2, 4, 4, SLOT, width), bf16)], "lay_out", 8)
    return got[:4], got[4:]


def put_tokens(values, frames_first, held, out):
    z, q = lax.axis_index("tp"), lax.axis_index("ctx")
    patches, width = out.shape[0], out.shape[-1]
    step = -(-patches // 4)
    for i, v in enumerate(values):
        v = v.reshape(4, SLOT, width).astype(f32)
        if frames_first:
            held[i] = v
        else:
            held[:, i] = v
    for f in range(4):
        s = lax.rem(f + 4 - z, 4)
        rows = [held[s, b ^ q][: min(step, patches - b * step)] for b in range(4)]
        out[:, f] = jnp.concatenate(rows, axis=0).astype(out.dtype)


def bring_back(parts, frames_first, patches, dtype):
    width = parts[0].shape[-1]

    def kernel(*refs):
        ins, out, held = refs[:4], refs[4], refs[5]
        put_tokens([r[...] for r in ins] if frames_first else ctx_parts(ins), frames_first, held, out)

    scratch = [pltpu.VMEM((4, 4, SLOT, width), f32)]
    got = call(kernel, parts, 0, [like((patches, 4, width), dtype)], 0, scratch, "bring_back", 8)
    return jnp.swapaxes(got[0], 0, 1)


def pack(parts, vector):
    rows, width = 4 * SLOT, parts[0].shape[-1]
    extra = vector.shape[0]

    def kernel(*refs):
        v = refs[3][...]
        high = v.astype(bf16)
        low = (v - high.astype(f32)).astype(bf16)
        below = jnp.concatenate([high.astype(f32), low.astype(f32)], axis=0).astype(bf16)
        for i in range(3):
            refs[4 + i][:rows] = refs[i][...].reshape(rows, width)
            refs[4 + i][rows:] = below

    return call(kernel, parts + [vector], 0, [like((rows + 2 * extra, width))] * 3, 0, [], "pack", 8)


def unpack(own, vector, moved, patches):
    rows, width = 4 * SLOT, own.shape[-1]
    extra = vector.shape[0]

    def kernel(*refs):
        own_ref, vec, ins = refs[0], refs[1], refs[2:5]
        out, total, held = refs[5:]
        put_tokens([own_ref[...]] + [r[:rows] for r in ins], True, held, out)
        v = vec[...]
        for r in ins:
            below = r[rows:].astype(f32)
            v = v + (below[:extra] + below[extra:])
        total[...] = v

    scratch = [pltpu.VMEM((4, 4, SLOT, width), f32)]
    outs = [like((patches, 4, width), f32), like(vector.shape, f32)]
    token_grad, total = call(kernel, [own, vector] + moved, 0, outs, 0, scratch, "unpack", 8, far=2**15)
    return jnp.swapaxes(token_grad, 0, 1), total


def to_ctx(parts):
    def kernel(*refs):
        for s in range(4):
            for e in range(4):
                to = refs[4 + e] if e < 2 else refs[6].at[e - 2]
                to[s] = refs[s][e]

    shape = parts[0].shape
    return call(kernel, parts, 0, [like(shape)] * 2 + [like((2,) + shape)], 0, [], "to_ctx", 4)


def to_frames(parts):
    def kernel(*refs):
        for e, v in enumerate(ctx_parts(refs[:4])):
            for s in range(4):
                refs[4 + s][e] = v[s]

    return call(kernel, parts, 0, [like(parts[0].shape)] * 4, 0, [], "to_frames", 4)


def turn_rows(rows):
    a = lax.broadcasted_iota(jnp.int32, (rows, rows), 0)
    b = lax.broadcasted_iota(jnp.int32, (rows, rows), 1)
    bits = SLOT.bit_length() - 1
    return jnp.where(b == ((a & (SLOT - 1)) << bits) + (a >> bits), 1.0, 0.0).astype(bf16)


def masks_of(timed, rows, mask_ref):
    if not timed:
        return [slice(0, rows)], mask_ref[...]
    half = rows // 2
    a = lax.broadcasted_iota(jnp.int32, (half, half), 0)
    b = lax.broadcasted_iota(jnp.int32, (half, half), 1)
    return [slice(0, half), slice(half, rows)], jnp.where((a ^ b) < SLOT, 0.0, -1e30).astype(f32)


def head_slices(p, h, head_cols):
    return [p[:, t * head_cols + h * HD : t * head_cols + (h + 1) * HD] for t in range(3)]


def attention_forward(plan, timed, head_cols, n_w):
    heads = head_cols // HD
    three = 3 * head_cols

    def kernel(*refs):
        take = Take(refs)
        x_refs = take(4)
        b_refs = take(4) if timed else []
        gain, shift, qv, mask_ref, bias_in = take(5)
        next_norm = take(2) if timed else []
        w_refs = take(n_w)
        p_ref, o_ref, log_ref = take(3)
        outs = take(3) if timed else take(4)
        whole, sems = take(2)
        loads = plan.start_loads(w_refs, whole, sems)
        if timed:
            parts = ctx_parts(x_refs)
            swap = turn_rows(log_ref.shape[0])
            x = nn(swap, rows_of([v[0] for v in parts]))
            x = x + nn(swap, rows_of(ctx_parts(b_refs))) + bias_in[0:1]
            outs[0][...] = x
            outs[2][1] = nn(swap, rows_of([v[1] for v in parts])).astype(bf16)
        else:
            x = rows_of(x_refs).astype(f32)
        ranges, mask = masks_of(timed, x.shape[0], mask_ref)
        q, _ = standardize(x)
        n = (q * gain[...] + shift[...]).astype(bf16)
        total = jnp.zeros(x.shape, f32)
        scale = jnp.where(lax.broadcasted_iota(jnp.int32, (1, three), 1) < head_cols, SCALE, 1.0).astype(f32)
        rows = x.shape[0]
        for r in range(plan.blocks):
            at = r * plan.wide
            for copy in loads[r]:
                copy.wait()
            p = ((nn(n, whole[:, at : at + three]) + qv[plan.block(r)]) * scale).astype(bf16)
            p_ref[r] = p
            cells = [[v[m] for v in head_slices(p, h, head_cols)] for h in range(heads) for m in ranges]
            s = jnp.concatenate([nt(qh, kh) + mask for qh, kh, _ in cells], axis=0)
            top = jnp.max(s, axis=-1, keepdims=True)
            e = jnp.exp(s - top)
            total_e = jnp.sum(e, axis=-1, keepdims=True)
            log = top + jnp.log(total_e)
            w = (e / total_e).astype(bf16)
            size = mask.shape[-1]
            o = [nn(w[i * size : (i + 1) * size], vh) for i, (_, _, vh) in enumerate(cells)]
            for h in range(heads):
                log_ref[:, r * heads + h : r * heads + h + 1] = log[h * rows : (h + 1) * rows]
            n_m = len(ranges)
            o = jnp.concatenate(
                [jnp.concatenate(o[h * n_m : (h + 1) * n_m], axis=0) for h in range(heads)], axis=-1
            ).astype(bf16)
            o_ref[r] = o
            total = total + nt(o, whole[:, at + three : at + plan.wide])
        if timed:
            x = x + total + bias_in[1:2]
            outs[1][...] = x
            q, _ = standardize(x)
            outs[2][0] = (q * next_norm[0][...] + next_norm[1][...]).astype(bf16)
        else:
            put_rows(outs, total)

    return kernel


def heads_backward(p, d_o, log, ranges, mask, head_cols):
    heads, n_m, size = head_cols // HD, len(ranges), mask.shape[-1]
    cells = []
    for h in range(heads):
        parts = head_slices(p, h, head_cols) + [d_o[:, h * HD : (h + 1) * HD], log[:, h : h + 1]]
        cells += [[v[m] for v in parts] for m in ranges]
    s = jnp.concatenate([nt(qh, kh) + (mask - lh) for qh, kh, _, _, lh in cells], axis=0)
    d_w = jnp.concatenate([nt(doh, vh) for _, _, vh, doh, _ in cells], axis=0)
    w = jnp.exp(s)
    d_s = (w * (d_w - jnp.sum(d_w * w, axis=-1, keepdims=True))).astype(bf16)
    w = w.astype(bf16)
    at = [slice(i * size, (i + 1) * size) for i in range(len(cells))]
    d_q = [nn(d_s[m], cell[1]) * SCALE for m, cell in zip(at, cells)]
    d_k = [tn(d_s[m], cell[0]) for m, cell in zip(at, cells)]
    d_v = [tn(w[m], cell[3]) for m, cell in zip(at, cells)]
    columns = [jnp.concatenate(v[h * n_m : (h + 1) * n_m], axis=0) for v in (d_q, d_k, d_v) for h in range(heads)]
    return jnp.concatenate(columns, axis=-1).astype(bf16)


def put_qv(vec, layer, qv_held, head_cols):
    for i, t in enumerate((0, 2)):
        row = [qv_held[j][:, t * head_cols : (t + 1) * head_cols] for j in range(qv_held.shape[0])]
        vec[9 + 2 * layer + i : 10 + 2 * layer + i] = jnp.concatenate(row, axis=-1)


def time_backward(plan, head_cols, n_w, n_back):
    heads = head_cols // HD
    three = 3 * head_cols

    def kernel(*refs):
        take = Take(refs)
        x_ref, next_x, pair = take(3)
        back_refs = take(n_back)
        next_gain, gain, log_ref = take(3)
        (p_ref,) = take(1)
        w_refs = take(n_w)
        d_ref, vec, g_out = take(3)
        outs = take(3)
        whole, sems, qv_held = take(3)
        loads = plan.start_loads(w_refs, whole, sems)
        vec[...] = jnp.zeros(vec.shape, f32)
        x = x_ref[...]
        rows = x.shape[0]
        ranges, mask = masks_of(True, rows, None)
        g = pair[1].astype(f32)
        q3, r3 = standardize(next_x[...])
        d = back_refs[0][...].astype(f32)
        for ref in back_refs[1:]:
            d = d + ref[...].astype(f32)
        vec[2:3] = row_sum(d * q3)
        vec[5:6] = row_sum(d)
        vec[8:9] = row_sum(g)
        g = g + norm_back(d, q3, r3, next_gain[...])
        g_b = g.astype(bf16)
        g_out[...] = g_b
        vec[7:8] = row_sum(g_b)
        q, r_x = standardize(x)
        d_n = jnp.zeros(x.shape, f32)
        for r in range(plan.blocks):
            at = r * plan.wide
            for copy in loads[r]:
                copy.wait()
            d_o = nn(g_b, whole[:, at + three : at + plan.wide]).astype(bf16)
            log = log_ref[:, r * heads : (r + 1) * heads]
            d_p = heads_backward(p_ref[r], d_o, log, ranges, mask, head_cols)
            d_ref[r] = d_p
            qv_held[plan.block(r)] = row_sum(d_p)
            d_n = d_n + nt(d_p, whole[:, at : at + three])
        vec[1:2] = row_sum(d_n * q)
        vec[4:5] = row_sum(d_n)
        put_qv(vec, 1, qv_held, head_cols)
        g = g + norm_back(d_n, q, r_x, gain[...])
        put_ctx(outs, nn(turn_rows(rows), g.astype(bf16)))

    return kernel


def time_weights(plan):
    def kernel(*refs):
        take = Take(refs)
        x_ref, g_ref, gain, shift = take(4)
        d_ref, o_ref = take(2)
        grads = take(len(plan.grad_shapes()))
        held, out_sems = take(2)
        q, _ = standardize(x_ref[...])
        n_t = (q * gain[...] + shift[...]).T.astype(bf16)
        g_t = turned(g_ref[...])
        for r in range(plan.blocks):
            block = jnp.concatenate([nn(n_t, d_ref[r]), nn(g_t, o_ref[r])], axis=-1)
            plan.hold(r, block, held)
        plan.store(held, grads, out_sems)

    return kernel


def space_weights(plan, head_cols, n_w):
    heads = head_cols // HD
    three = 3 * head_cols

    def kernel(*refs):
        take = Take(refs)
        x_refs, g_refs = take(4), take(4)
        gain, shift, mask_ref, log_ref = take(4)
        p_ref, o_ref = take(2)
        w_refs = take(n_w)
        grads = take(len(plan.grad_shapes()))
        (d_ref,) = take(1)
        whole, sems, held, out_sems = take(4)
        loads = plan.start_loads(w_refs, whole, sems)
        x = rows_of(x_refs).astype(f32)
        g_b = rows_of(g_refs)
        g_t = turned(g_b)
        ranges, mask = masks_of(False, x.shape[0], mask_ref)
        q, _ = standardize(x)
        n_t = (q * gain[...] + shift[...]).T.astype(bf16)
        for r in range(plan.blocks):
            at = r * plan.wide
            for copy in loads[r]:
                copy.wait()
            d_o = nn(g_b, whole[:, at + three : at + plan.wide]).astype(bf16)
            log = log_ref[:, r * heads : (r + 1) * heads]
            d_p = heads_backward(p_ref[r], d_o, log, ranges, mask, head_cols)
            d_ref[r] = d_p
            block = jnp.concatenate([nn(n_t, d_p), nn(g_t, o_ref[r])], axis=-1)
            plan.hold(r, block, held)
        plan.store(held, grads, out_sems)

    return kernel


def space_backward(plan, head_cols, n_w):
    three = 3 * head_cols

    def kernel(*refs):
        take = Take(refs)
        x_refs, g_refs = take(4), take(4)
        time_vec, up_sums, gain = take(3)
        (d_ref,) = take(1)
        w_refs = take(n_w)
        (vec,) = take(1)
        outs = take(4)
        whole, sems, qv_held = take(3)
        loads = plan.start_loads(w_refs, whole, sems)
        x, g = rows_of(x_refs).astype(f32), rows_of(g_refs).astype(f32)
        vec[...] = time_vec[...]
        for j in range(up_sums.shape[0]):
            vec[13 + j : 14 + j] = up_sums[j]
        vec[6:7] = row_sum(g)
        q, r_x = standardize(x)
        d_n = jnp.zeros(x.shape, f32)
        for r in range(plan.blocks):
            at = r * plan.wide
            for copy in loads[r]:
                copy.wait()
            d_p = d_ref[r]
            qv_held[plan.block(r)] = row_sum(d_p)
            d_n = d_n + nt(d_p, whole[:, at : at + three])
        vec[0:1] = row_sum(d_n * q)
        vec[3:4] = row_sum(d_n)
        put_qv(vec, 0, qv_held, head_cols)
        put_rows(outs, g + norm_back(d_n, q, r_x, gain[...]))

    return kernel


def mlp(plan, slots, n_w, groups, rows, first):
    def kernel(*refs):
        take = Take(refs)
        pairs = take(groups)
        (up_bias,) = take(1)
        before = [] if first else take(2 * groups + 1)
        w_refs = take(n_w)
        grads = take(len(plan.hidden_grad_shapes()))
        outs = take(groups)
        backs = take(groups)
        (up_sums,) = take(1)
        up, down, load_sems, held, out_sems = take(5)
        loads = plan.start_hidden_loads(w_refs, slots, up, down, load_sems)
        n = jnp.concatenate([v[0] for v in pairs], axis=0)
        g = jnp.concatenate([v[1] for v in pairs], axis=0)
        n_t, g_t = turned(n), turned(g)
        if first:
            total = jnp.zeros(n.shape, f32)
            back = jnp.zeros(n.shape, f32)
            up_sums[...] = jnp.zeros(up_sums.shape, f32)
        else:
            total = jnp.concatenate([v[...] for v in before[:groups]], axis=0)
            back = jnp.concatenate([v[...] for v in before[groups : 2 * groups]], axis=0)
            up_sums[...] = before[2 * groups][...]
        side = lax.axis_index("ctx") & 1 if plan.paired else 0
        here = pl.multiple_of(side * plan.hidden, plan.hidden)
        stores = []
        for i, r in enumerate(slots):
            for copy in loads[i]:
                copy.wait()
            cols = slice(i * plan.hidden, (i + 1) * plan.hidden)
            at = plan.block(r)
            u = nn(n, up[:, cols]) + up_bias[at, :, pl.ds(here, plan.hidden)]
            half = 0.5 * (1.0 + lax.erf(u * (0.5**0.5)))
            z = (u * half).astype(bf16)
            slope = half + u * (jnp.exp(-0.5 * u * u) * 0.3989422804014327)
            d_u = (nn(g, down[:, cols]) * slope).astype(bf16)
            plan.put_hidden(i, 0, nn(n_t, d_u), held)
            plan.put_hidden(i, 1, nn(g_t, z), held)
            stores += plan.start_hidden(i, held, grads, out_sems)
            total = total + nt(z, down[:, cols])
            back = back + nt(d_u, up[:, cols])
            up_sums[at, :, pl.ds(here, plan.hidden)] = row_sum(d_u)
        for i in range(groups):
            outs[i][...] = total[i * rows : (i + 1) * rows].astype(outs[i].dtype)
            backs[i][...] = back[i * rows : (i + 1) * rows].astype(backs[i].dtype)
        for copy in stores:
            copy.wait()

    return kernel


def on_device(
    mesh,
    tokens,
    cotangent,
    norm_gains,
    norm_shifts,
    qkv_spatial,
    proj_spatial,
    qkv_temporal,
    proj_temporal,
    up_weight,
    down_weight,
    out_bias,
    qv_bias,
    up_bias,
):
    shards, _, blocks = mesh.shape["shard"], mesh.shape["ctx"], mesh.shape["tp"]
    patches, model = tokens.shape[2:]
    head_cols = qkv_spatial.shape[2]
    wide = 4 * head_cols
    rows = 16 * SLOT
    plan = Plan(mesh, model, wide)
    paired = plan.paired
    x_rank, z_rank = lax.axis_index("shard"), lax.axis_index("tp")
    q_rank = lax.axis_index("ctx")

    def cut(v, axis, size, at):
        return lax.dynamic_slice_in_dim(v, at * size, size, axis)

    def joined(qkv, proj):
        if paired:
            part = model // 8
            qkv, proj = cut(qkv, 1, part, q_rank), cut(proj, 1, part, q_rank)
        return jnp.concatenate([qkv[0], qkv[1], qkv[2], proj.T], axis=1)

    own_space = joined(qkv_spatial, proj_spatial)
    own_time = joined(qkv_temporal, proj_temporal)
    own_up, own_down = up_weight, down_weight
    if paired:
        part = model // 4
        own_up = cut(cut(own_up, 0, part, q_rank >> 1), 1, plan.hidden, q_rank & 1)
        own_down = cut(cut(own_down, 0, plan.hidden, q_rank & 1), 1, part, q_rank >> 1)
    own_down = own_down.T
    part = norm_gains.shape[1]
    small = [norm_gains, norm_shifts, out_bias, qv_bias.reshape(-1, part), up_bias.reshape(-1, part)]
    small = jnp.concatenate(small, axis=0)
    msg_patch, msg_frame = lay_out(tokens[0], cotangent[0])
    own_hidden = jnp.concatenate([own_up, own_down], axis=0)

    if paired:

        def line(own, m):
            with jax.named_scope(f"line{m}"):
                return [own] + [shift_z(own, k) for k in (1, 2, 3)]

        def sides(a, m):
            with jax.named_scope(f"side{m}"):
                return a, flip_x(a), flip_y(a)

        def cores(parts, m):
            with jax.named_scope(f"core{m}"):
                return [flip_core(v) for v in parts]

        l0 = line(own_space, 0)
        with jax.named_scope("small"):
            other = flip_x(small)
        with jax.named_scope("frames"):
            frames = swap_ctx(*msg_frame)
        l0, other, frames[2], own_time, own_hidden = after((l0, other, frames[2], own_time, own_hidden))

        a0, x0, y0 = sides(jnp.stack(l0), 0)
        l1 = line(own_time, 1)
        x0, y0, l1 = after((x0, y0, l1))

        a1, x1, y1 = sides(jnp.stack(l1), 1)
        with jax.named_scope("line2"):
            l2 = shift_z(after(own_hidden, l1), 2)
        core0 = cores(after([a0, x0], l1), 0)
        x1, y1, l2, core0 = after((x1, y1, l2, core0))

        with jax.named_scope("corner0"):
            c0 = flip_x(after(y0, x1))
        with jax.named_scope("corner1"):
            c1 = flip_y(x1)
        with jax.named_scope("patches"):
            by_patch = swap_z_out(after(list(msg_patch), l2))
        c0, c1, by_patch = after((c0, c1, by_patch))

        a2, x2, y2 = sides(jnp.stack(after([own_hidden, l2], c0)), 2)
        core0 += cores([y0, c0], 0)
        with jax.named_scope("line3"):
            own = after(own_hidden, core0)
            l3 = [shift_z(own, 3), shift_z(own, 1)]
        w_space = [a0, x0, y0, c0] + core0
        first = jnp.where(x_rank == 0, small, other)
        second = jnp.where(x_rank == 0, other, small)
        small = jnp.stack([first, second])
    else:

        def gathered(v):
            v = lax.all_gather(v, "shard", axis=0, tiled=True)
            return [lax.all_gather(v, "tp", axis=1, tiled=True)[None]]

        w_space, w_time = gathered(own_space), gathered(own_time)
        w_hidden = lax.all_gather(own_hidden.reshape(2, -1, wide), "shard", axis=1, tiled=True)
        w_first = w_second = [lax.all_gather(w_hidden.reshape(1, 2 * model, wide), "tp", axis=0, tiled=True)]
        small = lax.all_gather(small, "shard", axis=0, tiled=False)
        frames = swap_ctx(*msg_frame)
        by_patch = swap_z_out(msg_patch)

    small = small.astype(f32)
    vectors = jnp.swapaxes(small[:, :13], 0, 1).reshape(13, model)
    gains, shifts, biases = vectors[0:3], vectors[3:6], vectors[6:9]
    qv = vectors[9:13].reshape(2, 2, blocks, head_cols)
    qv = jnp.concatenate([qv[:, 0], jnp.zeros_like(qv[:, 0]), qv[:, 1]], axis=-1)[:, :, None]
    up_b = small[:, 13:].reshape(blocks, 1, -1)

    step = -(-patches // 4)
    slot = jnp.arange(SLOT)[None, :]
    block = (jnp.arange(4) ^ q_rank)[:, None]
    valid = (slot < step) & (block * step + slot < patches)
    key_mask = jnp.where(valid, 0.0, -1e30).astype(f32).reshape(1, 4 * SLOT)
    key_mask = jnp.tile(key_mask, (1, 4))

    weight_scratch = [
        pltpu.VMEM((model, blocks * wide), bf16),
        pltpu.SemaphoreType.DMA((plan.n_loads(),)),
    ]
    p_shape = like((blocks, rows, 3 * head_cols))
    o_shape = like((blocks, rows, head_cols))
    log_shape = like((rows, 128), f32)
    full = like((rows, model), f32)
    unit = like((4, SLOT, model))

    p1, o1, log1, *branch = call(
        attention_forward(plan, False, head_cols, len(w_space)),
        by_patch + [gains[0:1], shifts[0:1], qv[0], key_mask, biases[0:2]] + w_space,
        len(w_space),
        [p_shape, o_shape, log_shape] + [unit] * 4,
        0,
        weight_scratch,
        "space_forward",
        20,
    )
    if paired:
        x2, y2, l3, branch = after((x2, y2, l3, branch))
        a3, x3, y3 = sides(jnp.stack(l3), 3)
    with jax.named_scope("branch_z"):
        branch = swap_z_back(branch)
    if paired:
        x3, y3, branch = after((x3, y3, branch))
        with jax.named_scope("corner2"):
            c2 = flip_x(after(y2, x3))
    with jax.named_scope("branch_ctx"):
        near, beside, beyond = to_ctx(branch)
        far = flip_y(beyond)
    if paired:
        core1 = cores(after([a1, x1, y1, c1], far), 1)
        with jax.named_scope("corner3"):
            c3 = [flip_x(y3[:1]), flip_y(after(x3[1:], far))]
        w_time = [a1, x1, y1, c1] + core1
    with jax.named_scope("branch_ctx"):
        branch = [near, flip_core(beside), far, flip_core(far)]
    if paired:
        branch, c2, c3[1] = after((branch, c2, c3[1]))
        w_first, w_second = [a2, x2, y2, c2], [a3, x3, y3, *c3]

    p2, o2, log2, mid, stream, pair = call(
        attention_forward(plan, True, head_cols, len(w_time)),
        frames
        + branch
        + [gains[1:2], shifts[1:2], qv[1], key_mask, biases[0:2], gains[2:3], shifts[2:3]]
        + w_time,
        len(w_time),
        [p_shape, o_shape, log_shape, full, full, like((2, rows, model))],
        0,
        weight_scratch,
        "time_forward",
        20,
    )
    pairs = [pair]
    if paired:
        with jax.named_scope("pair_core"):
            pairs.append(flip_core(pair))

    groups = len(pairs)
    hidden_whole = pltpu.VMEM((model, 2 * plan.hidden), bf16)
    hidden_scratch = [hidden_whole, hidden_whole, pltpu.SemaphoreType.DMA((16,))]
    hidden_scratch += plan.hidden_grad_scratch()
    hidden_grads = plan.hidden_grad_shapes()
    n_g = len(hidden_grads)
    up_shape = like((blocks, 1, wide), f32)
    got = call(
        mlp(plan, (0, 2), len(w_first), groups, rows, True),
        pairs + [up_b] + w_first,
        len(w_first),
        hidden_grads + [full] * (2 * groups) + [up_shape],
        n_g,
        hidden_scratch,
        "mlp_first",
        26,
    )
    first_grads, partial = got[:n_g], got[n_g:]
    got = call(
        mlp(plan, (1, 3), len(w_second), groups, rows, False),
        pairs + [up_b] + partial + w_second,
        len(w_second),
        hidden_grads + ([full] + [like((rows, model))] * (groups - 1)) * 2 + [up_shape],
        n_g,
        hidden_scratch,
        "mlp_second",
        26,
    )
    second_grads, results, backs, up_sums = got[:n_g], got[n_g : n_g + groups], got[n_g + groups : -1], got[-1]
    if paired:
        with jax.named_scope("hidden_side"):
            first_moved = [flip_y(first_grads[1]), flip_x(first_grads[3])]
            second_moved = [flip_y(second_grads[1]), flip_x(second_grads[3])]
        with jax.named_scope("back_core"):
            backs = [backs[0], flip_core(backs[1])]

    grads = plan.grad_shapes()
    n_g = len(grads)
    vec_shape = like((24, model), f32)
    qv_held = pltpu.VMEM((blocks, 1, 3 * head_cols), f32)
    d_time, time_vec, time_g, *g1 = call(
        time_backward(plan, head_cols, len(w_time), groups),
        [mid, stream, pair] + backs + [gains[2:3], gains[1:2], log2, p2] + w_time,
        len(w_time),
        [p_shape, vec_shape, like((rows, model))] + [unit] * 2 + [like((2,) + unit.shape)],
        0,
        weight_scratch + [qv_held],
        "time_backward",
        20,
    )
    if paired:
        g1, first_moved = after((g1, first_moved))
    with jax.named_scope("g1_ctx"):
        far = flip_y(g1[2])
    g_time = call(
        time_weights(plan),
        [mid, time_g, gains[1:2], shifts[1:2], d_time, o2],
        0,
        grads,
        n_g,
        plan.grad_scratch(),
        "time_weights",
        16,
    )
    if paired:
        g_time, far, second_moved = after((g_time, far, second_moved))
    with jax.named_scope("g1_ctx"):
        g1 = [g1[0], flip_core(g1[1]), far, flip_core(far)]
    if paired:
        with jax.named_scope("time_core"):
            got_time = flip_core(g_time[1])
        pairs = [(first_grads[0], first_moved[0]), (second_grads[0], second_moved[0])]
        pairs += [(first_grads[2], first_moved[1]), (second_grads[2], second_moved[1])]
        hidden_rest_a, send_a, hidden_rest_b, send_b = hidden_after_side(pairs)
        with jax.named_scope("hidden_corner"):
            corner_a, corner_b = flip_x(send_a), flip_y(send_b)
    with jax.named_scope("g1_z"):
        g1 = swap_z_out(to_frames(g1))
    if paired:
        keep_ta, send_ta, keep_tb, send_tb = after_core(g_time[0], got_time)
        with jax.named_scope("time_side"):
            side_ta, side_tb = flip_y(after(send_ta, g1)), flip_x(after(send_tb, g1))
        up_parts, down_parts = after_corner(hidden_rest_a, corner_a, hidden_rest_b, corner_b, 2)
        with jax.named_scope("up_line"):
            up_moved = spread(after(up_parts[1:], send_ta))

    got = call(
        space_weights(plan, head_cols, len(w_space)),
        by_patch + g1 + [gains[0:1], shifts[0:1], key_mask, log1, p1, o1] + w_space,
        len(w_space),
        grads + [p_shape],
        n_g,
        weight_scratch + plan.grad_scratch(),
        "space_weights",
        24,
        after=(up_parts[1], send_ta) if paired else (),
    )
    if paired:
        got, side_ta, side_tb, up_moved = after((got, side_ta, side_tb, up_moved))
    g_space, d_space = got[:n_g], got[n_g]
    vector, *back = call(
        space_backward(plan, head_cols, len(w_space)),
        by_patch + g1 + [time_vec, up_sums, gains[0:1], d_space] + w_space,
        len(w_space),
        [vec_shape] + [unit] * 4,
        0,
        weight_scratch + [qv_held],
        "space_backward",
        16,
    )

    if paired:
        with jax.named_scope("space_core"):
            got_space = flip_core(g_space[1])
        rest_ta, send_ta, rest_tb, send_tb = after_side((keep_ta, side_ta), (keep_tb, side_tb))
        with jax.named_scope("time_corner"):
            corner_ta, corner_tb = flip_x(send_ta), flip_y(send_tb)
        with jax.named_scope("down_line"):
            down_moved = spread(after(down_parts[1:], up_moved))
        got_space, vector, back, corner_ta, corner_tb, down_moved[:2] = after(
            (got_space, vector, back, corner_ta, corner_tb, down_moved[:2])
        )

        keep_a, send_a, keep_b, send_b = after_core(g_space[0], got_space)
        with jax.named_scope("space_side"):
            side_a, side_b = flip_y(send_a), flip_x(send_b)
        ((own_time_sum, *sends),) = after_corner(rest_ta, corner_ta, rest_tb, corner_tb)
        with jax.named_scope("time_line"):
            time_moved = spread(sends)
        hidden_keep, hidden_send = hidden_total(up_parts[:1] + up_moved, down_parts[:1] + down_moved)
        with jax.named_scope("hidden_core"):
            hidden_got = flip_core(hidden_send)
        side_a, side_b = after((side_a, side_b))

        rest_a, send_a, rest_b, send_b = after_side((keep_a, side_a), (keep_b, side_b))
        with jax.named_scope("space_corner"):
            corner_a, corner_b = flip_x(send_a), flip_y(send_b)
        with jax.named_scope("token_grad"):
            messages = pack(after(back[1:], send_a), vector)
            moved = [shift_z(v, 4 - k) for k, v in zip((1, 2, 3), messages)]
        qkv_time, proj_time = attention_total(own_time_sum, time_moved, head_cols)
        grad_up, grad_down = hidden_join(hidden_keep, hidden_got)
        corner_a, corner_b, moved, qkv_time, proj_time, grad_up, grad_down = after(
            (corner_a, corner_b, moved, qkv_time, proj_time, grad_up, grad_down)
        )
        token_parts = (back[0], vector, moved)

        ((own, *sends),) = after_corner(rest_a, corner_a, rest_b, corner_b)
        with jax.named_scope("space_line"):
            moved = spread(sends)
        qkv_space, proj_space = attention_total(own, moved, head_cols)
    else:

        def summed(g):
            g = lax.psum_scatter(g.astype(f32), ("shard", "ctx"), scatter_dimension=1, tiled=True)
            return lax.psum_scatter(g, "tp", scatter_dimension=0, tiled=True)[0]

        def apart(total):
            three = total[:, : 3 * head_cols].reshape(-1, 3, head_cols)
            return jnp.swapaxes(three, 0, 1), total[:, 3 * head_cols :].T

        hidden_grad = jnp.concatenate([v[i : i + 1] for i in (0, 1) for v in (first_grads[0], second_grads[0])])
        grad_up, grad_down = summed(hidden_grad[:, :model]), summed(hidden_grad[:, model:])
        qkv_time, proj_time = apart(summed(g_time[0]))
        qkv_space, proj_space = apart(summed(g_space[0]))

    with jax.named_scope("finished"):
        if paired:
            results = [results[0], flip_core(after(results[1], far))]

        def finish(*refs):
            total = refs[0][...] + refs[1][...]
            for ref in refs[2 : 1 + groups]:
                total = total + ref[...].astype(f32)
            put_ctx(refs[1 + groups :], nn(turn_rows(total.shape[0]), total.astype(bf16)))

        outs = [unit] * 2 + [like((2,) + unit.shape)]
        parts = call(finish, [stream + biases[2:3]] + list(results), 0, outs, 0, [], "finish", 8)
        if paired:
            parts = after(parts, moved[0])
        finished = bring_back(swap_ctx(*parts), False, patches, bf16)
    with jax.named_scope("token_grad"):
        if paired:
            token_grad, vector = unpack(*token_parts, patches)
            for flip in (flip_core, flip_y, flip_x):
                vector = vector + flip(vector)
        else:
            token_grad = bring_back(swap_z_back(back), True, patches, f32)

    if not paired:
        vector = lax.psum(vector, ("shard", "ctx", "tp"))
    place = (x_rank * mesh.shape["ctx"] + q_rank) * blocks + z_rank
    many = shards * mesh.shape["ctx"] * blocks
    mine = lax.dynamic_slice_in_dim(vector[:13], place * (model // many), model // many, 1)
    hidden = vector[13 : 13 + blocks * wide // model].reshape(-1)
    hidden = lax.dynamic_slice_in_dim(hidden, place * (hidden.shape[0] // many), hidden.shape[0] // many, 0)
    return (
        finished[None],
        token_grad[None],
        mine[0:3],
        mine[3:6],
        qkv_space,
        proj_space,
        qkv_time,
        proj_time,
        grad_up,
        grad_down.T,
        mine[6:9],
        mine[9:13].reshape(2, 2, -1),
        hidden,
    )


def solution(mesh):
    return jax.shard_map(
        functools.partial(on_device, mesh),
        mesh=mesh,
        in_specs=(
            P("shard", "ctx", "tp", None),
            P("shard", "ctx", "tp", None),
            P(None, "shard"),
            P(None, "shard"),
            P(None, "shard", "tp"),
            P("tp", "shard"),
            P(None, "shard", "tp"),
            P("tp", "shard"),
            P("shard", "tp"),
            P("tp", "shard"),
            P(None, "shard"),
            P(None, None, "shard"),
            P("shard"),
        ),
        out_specs=(
            P("shard", "ctx", "tp", None),
            P("shard", "ctx", "tp", None),
            P(None, ("shard", "ctx", "tp")),
            P(None, ("shard", "ctx", "tp")),
            P(None, ("shard", "ctx"), "tp"),
            P("tp", ("shard", "ctx")),
            P(None, ("shard", "ctx"), "tp"),
            P("tp", ("shard", "ctx")),
            P(("shard", "ctx"), "tp"),
            P("tp", ("shard", "ctx")),
            P(None, ("shard", "ctx", "tp")),
            P(None, None, ("shard", "ctx", "tp")),
            P(("shard", "ctx", "tp")),
        ),
        check_vma=False,
    )
```

```python
import functools

import jax
import jax.numpy as jnp
from jax import lax
from jax.experimental import pallas as pl
from jax.experimental.pallas import tpu as pltpu
from jax.sharding import PartitionSpec as P

HD = 64
EPS = 1e-06
SCALE = HD ** (-0.5)
SLOT = 16
bf16 = jnp.bfloat16
f32 = jnp.float32
VMEM = pl.BlockSpec(memory_space=pltpu.VMEM)
ANY = pl.BlockSpec(memory_space=pl.ANY)


def nn(a, b):
    return lax.dot_general(a, b, (((1,), (0,)), ((), ())), preferred_element_type=f32)


def nt(a, b):
    return lax.dot_general(a, b, (((1,), (1,)), ((), ())), preferred_element_type=f32)


def tn(a, b):
    return lax.dot_general(a, b, (((0,), (0,)), ((), ())), preferred_element_type=f32)


def turned(a):
    return a.astype(f32).T.astype(bf16)


def row_sum(v):
    return jnp.sum(v.astype(f32), axis=0, keepdims=True)


def standardize(v):
    c = v - jnp.mean(v, axis=-1, keepdims=True)
    r = lax.rsqrt(jnp.mean(c * c, axis=-1, keepdims=True) + EPS)
    return c * r, r


def norm_back(d, q, r, gain):
    e = d * gain
    return r * (e - jnp.mean(e, axis=-1, keepdims=True) - q * jnp.mean(e * q, axis=-1, keepdims=True))


def rows_of(parts):
    return jnp.concatenate([v[...].reshape(-1, v.shape[-1]) for v in parts], axis=0)


def put_rows(refs, value):
    n = value.shape[0] // len(refs)
    for i, r in enumerate(refs):
        r[...] = value[i * n : (i + 1) * n].reshape(r.shape).astype(r.dtype)


def put_ctx(refs, value):
    n = value.shape[0] // 4
    for i, to in enumerate((refs[0], refs[1], refs[2].at[0], refs[2].at[1])):
        to[...] = value[i * n : (i + 1) * n].reshape(to.shape).astype(to.dtype)


def like(shape, dtype=bf16):
    return jax.ShapeDtypeStruct(shape, dtype)


class Take:
    def __init__(self, refs):
        self.refs = list(refs)

    def __call__(self, n):
        got, self.refs = self.refs[:n], self.refs[n:]
        return got


def flip_x(v):
    return lax.ppermute(v, "shard", [(i, i ^ 1) for i in range(2)])


def flip_ctx(v, e):
    return lax.ppermute(v, "ctx", [(i, i ^ e) for i in range(4)])


def flip_core(v):
    return flip_ctx(v, 1)


def flip_y(v):
    return flip_ctx(v, 2)


def shift_z(v, k):
    return lax.ppermute(v, "tp", [(i, (i + k) % 4) for i in range(4)])


def swap_z_out(parts):
    return [parts[0]] + [shift_z(parts[k], k) for k in (1, 2, 3)]


def swap_z_back(parts):
    return [parts[0]] + [shift_z(parts[k], 4 - k) for k in (1, 2, 3)]


def swap_ctx(p0, p1, pair):
    far = flip_y(pair)
    return [p0, flip_core(p1), far, flip_core(far)]


def ctx_parts(refs):
    return [refs[0][...], refs[1][...], refs[2][0], refs[3][1]]


def after(value, *others):
    return lax.optimization_barrier((value, others))[0]


class Plan:
    def __init__(self, mesh, model, wide):
        self.sizes = (mesh.shape["shard"], mesh.shape["ctx"], mesh.shape["tp"])
        self.paired = self.sizes == (2, 4, 4)
        self.model, self.wide, self.blocks = model, wide, self.sizes[2]
        self.hidden = wide // 2 if self.paired else wide

    def ranks(self):
        q = lax.axis_index("ctx")
        return lax.axis_index("shard"), q >> 1, q & 1, lax.axis_index("tp")

    def block(self, r):
        if not self.paired:
            return r
        return lax.rem(lax.axis_index("tp") + r, self.blocks)

    def places(self):
        if not self.paired:
            return [(0, 0, 0, self.model, 0)]
        x, y, c, _ = self.ranks()
        rows = self.model // 8
        every = range(4)
        kinds = [(0, 0, every), (1, 0, every), (0, 1, every), (1, 1, every)]
        out = []
        for core in (0, 1):
            for i, (dx, dy, ks) in enumerate(kinds):
                row = (((x ^ dx) * 2 + (y ^ dy)) * 2 + (c ^ core)) * rows
                for n, k in enumerate(ks):
                    out.append((core * 4 + i, n, pl.multiple_of(row, rows), rows, (4 - k) % 4))
        return out

    def n_loads(self):
        return 32 if self.paired else 1

    def start_loads(self, refs, whole, sems):
        by_slot = [[] for _ in range(self.blocks)]
        for n, (i, k, row, rows, slot) in enumerate(self.places()):
            to = whole.at[pl.ds(row, rows), pl.ds(slot * self.wide, refs[i].shape[-1])]
            by_slot[slot].append(pltpu.make_async_copy(refs[i].at[k], to, sems.at[n]))
        for copies in by_slot:
            for copy in copies:
                copy.start()
        return by_slot

    def start_hidden_loads(self, refs, slots, up, down, sems):
        by_slot = [[], []]
        if self.paired:
            x, y, _, _ = self.ranks()
            rows = self.model // 4
            kinds = [(0, 0, (0, 1)), (1, 0, (0, 1)), (0, 1, (0, 1))]
            kinds += [(1, 1, (0, 1))] if len(refs) == 4 else [(1, 1, (0,)), (1, 1, (1,))]
            places = []
            for ref, (dx, dy, ks) in zip(refs, kinds):
                row = pl.multiple_of(((x ^ dx) * 2 + (y ^ dy)) * rows, rows)
                places += [(ref.at[n], row, k) for n, k in enumerate(ks)]
        else:
            rows = self.model
            places = [(refs[0].at[r], 0, i) for i, r in enumerate(slots)]
        for n, (source, row, i) in enumerate(places):
            for part, whole in enumerate((up, down)):
                to = whole.at[pl.ds(row, rows), pl.ds(i * self.hidden, self.hidden)]
                copy = pltpu.make_async_copy(source.at[part * rows : (part + 1) * rows], to, sems.at[2 * n + part])
                by_slot[i].append(copy)
        for copies in by_slot:
            for copy in copies:
                copy.start()
        return by_slot

    def grad_shapes(self):
        if self.paired:
            return [like((2, 2, 4, self.model // 8, self.wide))] * 2
        return [like((self.blocks, self.model, self.wide))]

    def grad_scratch(self):
        if self.paired:
            held = pltpu.VMEM((4, 2, 2, 2, self.model // 8, self.wide), bf16)
            return [held, pltpu.SemaphoreType.DMA((8,))]
        return [
            pltpu.VMEM((self.blocks, self.model, self.wide), bf16),
            pltpu.SemaphoreType.DMA((self.blocks,)),
        ]

    def hold(self, r, value, held):
        value = value.astype(bf16)
        if not self.paired:
            held[r] = value
            return
        x, y, c, _ = self.ranks()
        rows = self.model // 8
        for i in range(8):
            held[r, (i & 1) ^ c, ((i >> 1) & 1) ^ y, (i >> 2) ^ x] = value[i * rows : (i + 1) * rows]

    def store(self, held, outs, sems):
        copies = []
        for r in range(self.blocks):
            if not self.paired:
                copies.append(pltpu.make_async_copy(held.at[r], outs[0].at[r], sems.at[r]))
                continue
            for core in (1, 0):
                to = outs[core].at[:, :, r]
                copies.append(pltpu.make_async_copy(held.at[r, core], to, sems.at[2 * r + core]))
        for copy in copies:
            copy.start()
        for copy in copies:
            copy.wait()

    def hidden_grad_shapes(self):
        if self.paired:
            return [like((2, self.model // 2, self.hidden))] * 4
        return [like((2, 2 * self.model, self.hidden))]

    def hidden_grad_scratch(self):
        if self.paired:
            held = pltpu.VMEM((2, 2, 2, self.model // 2, self.hidden), bf16)
            return [held, pltpu.SemaphoreType.DMA((4,))]
        return [pltpu.VMEM((2, 2 * self.model, self.hidden), bf16), pltpu.SemaphoreType.DMA((2,))]

    def put_hidden(self, i, part, value, held):
        value = value.astype(bf16)
        if not self.paired:
            held[i, part * self.model : (part + 1) * self.model] = value
            return
        x, y, _, _ = self.ranks()
        rows = self.model // 4
        for n in range(4):
            to = held.at[i, (n & 1) ^ y, (n >> 1) ^ x]
            to[part * rows : (part + 1) * rows] = value[n * rows : (n + 1) * rows]

    def start_hidden(self, i, held, outs, sems):
        if not self.paired:
            copies = [pltpu.make_async_copy(held.at[i], outs[0].at[i], sems.at[i])]
        else:
            copies = []
            for side in (0, 1):
                source = held.at[i, side] if i == 0 else held.at[i, :, side]
                copies.append(pltpu.make_async_copy(source, outs[2 * i + side], sems.at[2 * i + side]))
        for copy in copies:
            copy.start()
        return copies


def call(kernel, ins, n_any, outs, n_any_out, scratch, name, limit, after=(), far=None, wait=()):
    n_in, n_after = len(ins), len(after)

    def run(*refs):
        kernel(*refs[:n_in], *refs[n_in + n_after :])

    ins = list(ins)
    for i, v in enumerate(ins):
        if i >= n_in - n_any or (far is not None and v.size >= far):
            ins[i] = pltpu.with_memory_space_constraint(v, pltpu.HBM)
    outs = [pltpu.HBM(v.shape, v.dtype) if i in wait else v for i, v in enumerate(outs)]
    got = pl.pallas_call(
        run,
        out_shape=outs,
        in_specs=[VMEM] * (n_in - n_any) + [ANY] * (n_any + n_after),
        out_specs=[ANY] * n_any_out + [VMEM] * (len(outs) - n_any_out),
        scratch_shapes=scratch,
        compiler_params=pltpu.CompilerParams(vmem_limit_bytes=limit * 2**20),
        cost_estimate=pl.CostEstimate(flops=0, bytes_accessed=0, transcendentals=0),
        name=name,
    )(*ins, *after)
    return list(got)


def add(u, v):
    return (u.astype(f32) + v.astype(f32)).astype(bf16)


def after_core(keep, got):
    rows, wide = keep.shape[-2:]
    cut = 3

    def kernel(k, g, keep_a, send_a, keep_b, send_b):
        for x in (0, 1):
            keep_a[x] = add(k[0, x, :2], g[0, x, :2])
            send_a[x] = add(k[1, x, :2], g[1, x, :2])
        for y in (0, 1):
            keep_b[y] = add(k[y, 0, 2:], g[y, 0, 2:])
            send_b[y] = add(k[y, 1, 2:], g[y, 1, 2:])

    whole = pl.BlockSpec((2, 2, 4, rows // cut, wide), lambda i: (0, 0, 0, i, 0))
    half = pl.BlockSpec((2, 2, rows // cut, wide), lambda i: (0, 0, i, 0))
    return pl.pallas_call(
        kernel,
        grid=(cut,),
        out_shape=[like((2, 2, rows, wide))] * 4,
        in_specs=[whole] * 2,
        out_specs=[half] * 4,
        compiler_params=pltpu.CompilerParams(vmem_limit_bytes=16 * 2**20),
        name="after_core",
    )(keep, got)


def after_side(*pairs):
    def kernel(*refs):
        n = len(pairs)
        for i in range(n):
            k, g = refs[2 * i], refs[2 * i + 1]
            refs[2 * n + 2 * i][...] = add(k[0], g[0])
            refs[2 * n + 2 * i + 1][...] = add(k[1], g[1])

    ins = [v for pair in pairs for v in pair]
    outs = [like(v.shape[1:]) for v in ins]
    return call(kernel, ins, 0, outs, 0, [], "after_side", 24, wait=range(0, 2 * len(pairs), 2))


def hidden_after_side(pairs):
    def kernel(*refs):
        for i in range(4):
            k, g = refs[2 * i], refs[2 * i + 1]
            rest, send = refs[8 + 2 * (i // 2)], refs[9 + 2 * (i // 2)]
            rest[i % 2] = add(k[0], g[0])
            send[i % 2] = add(k[1], g[1])

    ins = [v for pair in pairs for v in pair]
    return call(kernel, ins, 0, [like(ins[0].shape)] * 4, 0, [], "hidden_after_side", 24)


def after_corner(rest_a, got_a, rest_b, got_b):
    def kernel(ra, ga, rb, gb, own, *sends):
        own[...] = ra[0].astype(f32) + ga[0].astype(f32)
        sends[0][...] = add(ra[1], ga[1])
        sends[1][...] = add(rb[0], gb[0])
        sends[2][...] = add(rb[1], gb[1])

    shape = rest_a.shape[1:]
    outs = [like(shape, f32)] + [like(shape)] * 3
    return call(kernel, [rest_a, got_a, rest_b, got_b], 0, outs, 0, [], "after_corner", 12)


def hidden_after_corner(rest_a, got_a, rest_b, got_b):
    rows = rest_a.shape[1] // 2

    def kernel(ra, ga, rb, gb, own, *sends):
        own[...] = ra[0].astype(f32) + ga[0].astype(f32)
        for part in (0, 1):
            at = slice(part * rows, (part + 1) * rows)
            sends[2 * part][...] = add(ra[1, at], ga[1, at])
            sends[2 * part + 1][...] = add(rb[0, at], gb[0, at])
        sends[4][...] = add(rb[1], gb[1])

    shape = rest_a.shape[1:]
    half = (rows,) + shape[1:]
    outs = [like(shape, f32)] + [like(half)] * 4 + [like(shape)]
    return call(kernel, [rest_a, got_a, rest_b, got_b], 0, outs, 0, [], "hidden_after_corner", 12)


def spread(sends):
    return [shift_z(v, k) for k, v in zip((1, 2, 3), sends)]


def attention_total(own, moved, head_cols, far):
    rows = own.shape[0]
    three = 3 * head_cols

    def kernel(o, a, b, c, qkv, proj):
        total = o[...] + a[...].astype(f32) + b[...].astype(f32) + c[...].astype(f32)
        for t in range(3):
            qkv[t] = total[:, t * head_cols : (t + 1) * head_cols]
        proj[...] = total[:, three:].T

    outs = [like((3, rows, head_cols), f32), like((head_cols, rows), f32)]
    return call(kernel, [own] + moved, 0, outs, 0, [], "attention_total", 8, far=far)


def hidden_total(own, moved):
    rows, wide = own.shape[0] // 4, own.shape[1]

    def kernel(o, up_1, up_2, down_1, down_2, both, keep, send):
        core = lax.axis_index("ctx") & 1
        for part, pair in enumerate(((up_1, up_2), (down_1, down_2))):
            for half in (0, 1):
                at = slice(half * rows, (half + 1) * rows)
                of = slice((2 * part + half) * rows, (2 * part + half + 1) * rows)
                total = o[of] + both[of].astype(f32) + pair[0][at].astype(f32) + pair[1][at].astype(f32)

                @pl.when(core == half)
                def _(total=total, part=part):
                    keep[part] = total

                @pl.when(core != half)
                def _(total=total, part=part):
                    send[part] = total.astype(bf16)

    outs = [like((2, rows, wide), f32), like((2, rows, wide))]
    return call(kernel, [own] + moved, 0, outs, 0, [], "hidden_total", 8)


def hidden_join(keep, got):
    rows, wide = keep.shape[1:]

    def kernel(k, g, up, down):
        core = lax.axis_index("ctx") & 1
        here, there = pl.multiple_of(core * wide, wide), pl.multiple_of((1 - core) * wide, wide)
        for part, out in enumerate((up, down)):
            out[:, pl.ds(here, wide)] = k[part]
            out[:, pl.ds(there, wide)] = g[part].astype(f32)

    return call(kernel, [keep, got], 0, [like((rows, 2 * wide), f32)] * 2, 0, [], "hidden_join", 8)


def lay_out(x, c):
    frames, patches, width = x.shape
    step = -(-patches // 4)

    def kernel(x_ref, c_ref, *refs):
        by_patch, by_frame, held = refs[:4], refs[4:7], refs[7]
        z, q = lax.axis_index("tp"), lax.axis_index("ctx")
        for i, ref in enumerate((x_ref, c_ref)):
            for f in range(4):
                v = ref[f].astype(f32)
                for b in range(4):
                    part = v[b * step : min((b + 1) * step, patches)]
                    pad = jnp.zeros((SLOT - part.shape[0], width), f32)
                    held[i, f, b] = jnp.concatenate([part, pad], axis=0).astype(bf16)
        for s in range(4):
            f = lax.rem(z + s, 4)
            for e in range(4):
                by_patch[s][e * SLOT : (e + 1) * SLOT] = held[0, f, q ^ e]
                to = by_frame[e] if e < 2 else by_frame[2].at[e - 2]
                to[0, s] = held[0, f, q ^ e]
                to[1, s] = held[1, f, q ^ e]

    both = (2, 4, SLOT, width)
    outs = [like((4 * SLOT, width))] * 4 + [like(both)] * 2 + [like((2,) + both)]
    got = call(kernel, [x, c], 0, outs, 0, [pltpu.VMEM((2, 4, 4, SLOT, width), bf16)], "lay_out", 8)
    return got[:4], got[4:]


def put_tokens(values, frames_first, held, out):
    z, q = lax.axis_index("tp"), lax.axis_index("ctx")
    patches, width = out.shape[0], out.shape[-1]
    step = -(-patches // 4)
    for i, v in enumerate(values):
        v = v.reshape(4, SLOT, width).astype(f32)
        if frames_first:
            held[i] = v
        else:
            held[:, i] = v
    for f in range(4):
        s = lax.rem(f + 4 - z, 4)
        rows = [held[s, b ^ q][: min(step, patches - b * step)] for b in range(4)]
        out[:, f] = jnp.concatenate(rows, axis=0).astype(out.dtype)


def bring_back(parts, frames_first, patches, dtype):
    width = parts[0].shape[-1]

    def kernel(*refs):
        ins, out, held = refs[:4], refs[4], refs[5]
        put_tokens([r[...] for r in ins] if frames_first else ctx_parts(ins), frames_first, held, out)

    scratch = [pltpu.VMEM((4, 4, SLOT, width), f32)]
    got = call(kernel, parts, 0, [like((patches, 4, width), dtype)], 0, scratch, "bring_back", 8)
    return jnp.swapaxes(got[0], 0, 1)


def pack(parts, vector, other):
    rows, width = 4 * SLOT, parts[0].shape[-1]
    extra = vector.shape[0]

    def kernel(a, b, c, vec, far, total, *outs):
        v = vec[...] + far[...]
        total[...] = v
        high = v.astype(bf16)
        low = (v - high.astype(f32)).astype(bf16)
        below = jnp.concatenate([high.astype(f32), low.astype(f32)], axis=0).astype(bf16)
        for part, out in zip((a, b, c), outs):
            out[:rows] = part[...].reshape(rows, width)
            out[rows:] = below

    outs = [like(vector.shape, f32)] + [like((rows + 2 * extra, width))] * 3
    return call(kernel, parts + [vector, other], 0, outs, 0, [], "pack", 8)


def own_vectors(mesh, vector, other):
    blocks, model = mesh.shape["tp"], vector.shape[-1]
    many = mesh.size
    size, hidden = model // many, 4 * model // many

    def kernel(vec, far, gains, shifts, biases, qv, up):
        place = (lax.axis_index("shard") * mesh.shape["ctx"] + lax.axis_index("ctx")) * blocks + lax.axis_index("tp")
        total = vec[...] + far[...]
        mine = pltpu.roll(total, lax.rem(model - place * size, model), 1)[:, :size]
        gains[...] = mine[0:3]
        shifts[...] = mine[3:6]
        biases[...] = mine[6:9]
        qv[...] = mine[9:13]
        at = place * hidden
        for row in range(4):

            @pl.when(lax.div(at, model) == row)
            def _(row=row):
                here = total[13 + row : 14 + row]
                up[...] = pltpu.roll(here, lax.rem(model - lax.rem(at, model), model), 1)[:, :hidden]

    outs = [like((3, size), f32)] * 3 + [like((4, size), f32), like((1, hidden), f32)]
    return call(kernel, [vector, other], 0, outs, 0, [], "own_vectors", 4)


def unpack(own, vector, moved, patches):
    rows, width = 4 * SLOT, own.shape[-1]
    extra = vector.shape[0]

    def kernel(*refs):
        own_ref, vec, ins = refs[0], refs[1], refs[2:5]
        out, total, held = refs[5:]
        put_tokens([own_ref[...]] + [r[:rows] for r in ins], True, held, out)
        v = vec[...]
        for r in ins:
            below = r[rows:].astype(f32)
            v = v + (below[:extra] + below[extra:])
        total[...] = v

    scratch = [pltpu.VMEM((4, 4, SLOT, width), f32)]
    outs = [like((patches, 4, width), f32), like(vector.shape, f32)]
    token_grad, total = call(kernel, [own, vector] + moved, 0, outs, 0, scratch, "unpack", 8, far=2**15)
    return jnp.swapaxes(token_grad, 0, 1), total


def to_ctx(parts):
    def kernel(*refs):
        for s in range(4):
            for e in range(4):
                to = refs[4 + e] if e < 2 else refs[6].at[e - 2]
                to[s] = refs[s][e]

    shape = parts[0].shape
    return call(kernel, parts, 0, [like(shape)] * 2 + [like((2,) + shape)], 0, [], "to_ctx", 4)


def to_frames(parts):
    def kernel(*refs):
        for e, v in enumerate(ctx_parts(refs[:4])):
            for s in range(4):
                refs[4 + s][e] = v[s]

    return call(kernel, parts, 0, [like(parts[0].shape)] * 4, 0, [], "to_frames", 4)


def turn_rows(rows):
    a = lax.broadcasted_iota(jnp.int32, (rows, rows), 0)
    b = lax.broadcasted_iota(jnp.int32, (rows, rows), 1)
    bits = SLOT.bit_length() - 1
    return jnp.where(b == ((a & (SLOT - 1)) << bits) + (a >> bits), 1.0, 0.0).astype(bf16)


def masks_of(timed, rows, mask_ref):
    if not timed:
        return [slice(0, rows)], mask_ref[...]
    half = rows // 2
    a = lax.broadcasted_iota(jnp.int32, (half, half), 0)
    b = lax.broadcasted_iota(jnp.int32, (half, half), 1)
    return [slice(0, half), slice(half, rows)], jnp.where((a ^ b) < SLOT, 0.0, -1e30).astype(f32)


def head_slices(p, h, head_cols):
    return [p[:, t * head_cols + h * HD : t * head_cols + (h + 1) * HD] for t in range(3)]


def attention_forward(plan, timed, head_cols, n_w):
    heads = head_cols // HD
    three = 3 * head_cols

    def kernel(*refs):
        take = Take(refs)
        x_refs = take(4)
        b_refs = take(4) if timed else []
        gain, shift, qv, mask_ref, bias_in = take(5)
        next_norm = take(2) if timed else []
        w_refs = take(n_w)
        p_ref, o_ref, log_ref = take(3)
        outs = take(3) if timed else take(4)
        whole, sems = take(2)
        loads = plan.start_loads(w_refs, whole, sems)
        if timed:
            parts = ctx_parts(x_refs)
            swap = turn_rows(log_ref.shape[0])
            x = nn(swap, rows_of([v[0] for v in parts]))
            x = x + nn(swap, rows_of(ctx_parts(b_refs))) + bias_in[0:1]
            outs[0][...] = x
            outs[2][1] = nn(swap, rows_of([v[1] for v in parts])).astype(bf16)
        else:
            x = rows_of(x_refs).astype(f32)
        ranges, mask = masks_of(timed, x.shape[0], mask_ref)
        q, _ = standardize(x)
        n = (q * gain[...] + shift[...]).astype(bf16)
        total = jnp.zeros(x.shape, f32)
        scale = jnp.where(lax.broadcasted_iota(jnp.int32, (1, three), 1) < head_cols, SCALE, 1.0).astype(f32)
        rows = x.shape[0]
        for r in range(plan.blocks):
            at = r * plan.wide
            for copy in loads[r]:
                copy.wait()
            p = ((nn(n, whole[:, at : at + three]) + qv[plan.block(r)]) * scale).astype(bf16)
            p_ref[r] = p
            cells = [[v[m] for v in head_slices(p, h, head_cols)] for h in range(heads) for m in ranges]
            s = jnp.concatenate([nt(qh, kh) + mask for qh, kh, _ in cells], axis=0)
            top = jnp.max(s, axis=-1, keepdims=True)
            e = jnp.exp(s - top)
            total_e = jnp.sum(e, axis=-1, keepdims=True)
            log = top + jnp.log(total_e)
            w = (e / total_e).astype(bf16)
            size = mask.shape[-1]
            o = [nn(w[i * size : (i + 1) * size], vh) for i, (_, _, vh) in enumerate(cells)]
            for h in range(heads):
                log_ref[:, r * heads + h : r * heads + h + 1] = log[h * rows : (h + 1) * rows]
            n_m = len(ranges)
            o = jnp.concatenate(
                [jnp.concatenate(o[h * n_m : (h + 1) * n_m], axis=0) for h in range(heads)], axis=-1
            ).astype(bf16)
            o_ref[r] = o
            total = total + nt(o, whole[:, at + three : at + plan.wide])
        if timed:
            x = x + total + bias_in[1:2]
            outs[1][...] = x
            q, _ = standardize(x)
            outs[2][0] = (q * next_norm[0][...] + next_norm[1][...]).astype(bf16)
        else:
            put_rows(outs, total)

    return kernel


def heads_backward(p, d_o, log, ranges, mask, head_cols):
    heads, n_m, size = head_cols // HD, len(ranges), mask.shape[-1]
    cells = []
    for h in range(heads):
        parts = head_slices(p, h, head_cols) + [d_o[:, h * HD : (h + 1) * HD], log[:, h : h + 1]]
        cells += [[v[m] for v in parts] for m in ranges]
    s = jnp.concatenate([nt(qh, kh) + (mask - lh) for qh, kh, _, _, lh in cells], axis=0)
    d_w = jnp.concatenate([nt(doh, vh) for _, _, vh, doh, _ in cells], axis=0)
    w = jnp.exp(s)
    d_s = (w * (d_w - jnp.sum(d_w * w, axis=-1, keepdims=True))).astype(bf16)
    w = w.astype(bf16)
    at = [slice(i * size, (i + 1) * size) for i in range(len(cells))]
    d_q = [nn(d_s[m], cell[1]) * SCALE for m, cell in zip(at, cells)]
    d_k = [tn(d_s[m], cell[0]) for m, cell in zip(at, cells)]
    d_v = [tn(w[m], cell[3]) for m, cell in zip(at, cells)]
    columns = [jnp.concatenate(v[h * n_m : (h + 1) * n_m], axis=0) for v in (d_q, d_k, d_v) for h in range(heads)]
    return jnp.concatenate(columns, axis=-1).astype(bf16)


def put_qv(vec, layer, qv_held, head_cols):
    for i, t in enumerate((0, 2)):
        row = [qv_held[j][:, t * head_cols : (t + 1) * head_cols] for j in range(qv_held.shape[0])]
        vec[9 + 2 * layer + i : 10 + 2 * layer + i] = jnp.concatenate(row, axis=-1)


def time_backward(plan, head_cols, n_w, n_back):
    heads = head_cols // HD
    three = 3 * head_cols

    def kernel(*refs):
        take = Take(refs)
        x_ref, next_x, pair = take(3)
        back_refs = take(n_back)
        next_gain, gain, log_ref = take(3)
        (p_ref,) = take(1)
        w_refs = take(n_w)
        d_ref, vec, g_out = take(3)
        outs = take(3)
        whole, sems, qv_held = take(3)
        loads = plan.start_loads(w_refs, whole, sems)
        vec[...] = jnp.zeros(vec.shape, f32)
        x = x_ref[...]
        rows = x.shape[0]
        ranges, mask = masks_of(True, rows, None)
        g = pair[1].astype(f32)
        q3, r3 = standardize(next_x[...])
        d = back_refs[0][...].astype(f32)
        for ref in back_refs[1:]:
            d = d + ref[...].astype(f32)
        vec[2:3] = row_sum(d * q3)
        vec[5:6] = row_sum(d)
        vec[8:9] = row_sum(g)
        g = g + norm_back(d, q3, r3, next_gain[...])
        g_b = g.astype(bf16)
        g_out[...] = g_b
        vec[7:8] = row_sum(g_b)
        q, r_x = standardize(x)
        d_n = jnp.zeros(x.shape, f32)
        for r in range(plan.blocks):
            at = r * plan.wide
            for copy in loads[r]:
                copy.wait()
            d_o = nn(g_b, whole[:, at + three : at + plan.wide]).astype(bf16)
            log = log_ref[:, r * heads : (r + 1) * heads]
            d_p = heads_backward(p_ref[r], d_o, log, ranges, mask, head_cols)
            d_ref[r] = d_p
            qv_held[plan.block(r)] = row_sum(d_p)
            d_n = d_n + nt(d_p, whole[:, at : at + three])
        vec[1:2] = row_sum(d_n * q)
        vec[4:5] = row_sum(d_n)
        put_qv(vec, 1, qv_held, head_cols)
        g = g + norm_back(d_n, q, r_x, gain[...])
        put_ctx(outs, nn(turn_rows(rows), g.astype(bf16)))

    return kernel


def time_weights(plan):
    def kernel(*refs):
        take = Take(refs)
        x_ref, g_ref, gain, shift = take(4)
        d_ref, o_ref = take(2)
        grads = take(len(plan.grad_shapes()))
        held, out_sems = take(2)
        q, _ = standardize(x_ref[...])
        n_t = (q * gain[...] + shift[...]).T.astype(bf16)
        g_t = turned(g_ref[...])
        for r in range(plan.blocks):
            block = jnp.concatenate([nn(n_t, d_ref[r]), nn(g_t, o_ref[r])], axis=-1)
            plan.hold(r, block, held)
        plan.store(held, grads, out_sems)

    return kernel


def space_weights(plan, head_cols, n_w):
    heads = head_cols // HD
    three = 3 * head_cols

    def kernel(*refs):
        take = Take(refs)
        x_refs, g_refs = take(4), take(4)
        gain, shift, mask_ref, log_ref = take(4)
        p_ref, o_ref = take(2)
        w_refs = take(n_w)
        grads = take(len(plan.grad_shapes()))
        (d_ref,) = take(1)
        whole, sems, held, out_sems = take(4)
        loads = plan.start_loads(w_refs, whole, sems)
        x = rows_of(x_refs).astype(f32)
        g_b = rows_of(g_refs)
        g_t = turned(g_b)
        ranges, mask = masks_of(False, x.shape[0], mask_ref)
        q, _ = standardize(x)
        n_t = (q * gain[...] + shift[...]).T.astype(bf16)
        for r in range(plan.blocks):
            at = r * plan.wide
            for copy in loads[r]:
                copy.wait()
            d_o = nn(g_b, whole[:, at + three : at + plan.wide]).astype(bf16)
            log = log_ref[:, r * heads : (r + 1) * heads]
            d_p = heads_backward(p_ref[r], d_o, log, ranges, mask, head_cols)
            d_ref[r] = d_p
            block = jnp.concatenate([nn(n_t, d_p), nn(g_t, o_ref[r])], axis=-1)
            plan.hold(r, block, held)
        plan.store(held, grads, out_sems)

    return kernel


def space_backward(plan, head_cols, n_w):
    three = 3 * head_cols

    def kernel(*refs):
        take = Take(refs)
        x_refs, g_refs = take(4), take(4)
        time_vec, up_sums, gain = take(3)
        (d_ref,) = take(1)
        w_refs = take(n_w)
        (vec,) = take(1)
        outs = take(4)
        whole, sems, qv_held = take(3)
        loads = plan.start_loads(w_refs, whole, sems)
        x, g = rows_of(x_refs).astype(f32), rows_of(g_refs).astype(f32)
        vec[...] = time_vec[...]
        for j in range(up_sums.shape[0]):
            vec[13 + j : 14 + j] = up_sums[j]
        vec[6:7] = row_sum(g)
        q, r_x = standardize(x)
        d_n = jnp.zeros(x.shape, f32)
        for r in range(plan.blocks):
            at = r * plan.wide
            for copy in loads[r]:
                copy.wait()
            d_p = d_ref[r]
            qv_held[plan.block(r)] = row_sum(d_p)
            d_n = d_n + nt(d_p, whole[:, at : at + three])
        vec[0:1] = row_sum(d_n * q)
        vec[3:4] = row_sum(d_n)
        put_qv(vec, 0, qv_held, head_cols)
        put_rows(outs, g + norm_back(d_n, q, r_x, gain[...]))

    return kernel


def mlp(plan, slots, n_w, groups, rows, first):
    def kernel(*refs):
        take = Take(refs)
        pairs = take(groups)
        (up_bias,) = take(1)
        before = [] if first else take(2 * groups + 1)
        w_refs = take(n_w)
        grads = take(len(plan.hidden_grad_shapes()))
        outs = take(groups)
        backs = take(groups)
        (up_sums,) = take(1)
        up, down, load_sems, held, out_sems = take(5)
        loads = plan.start_hidden_loads(w_refs, slots, up, down, load_sems)
        n = jnp.concatenate([v[0] for v in pairs], axis=0)
        g = jnp.concatenate([v[1] for v in pairs], axis=0)
        n_t, g_t = turned(n), turned(g)
        if first:
            total = jnp.zeros(n.shape, f32)
            back = jnp.zeros(n.shape, f32)
            up_sums[...] = jnp.zeros(up_sums.shape, f32)
        else:
            total = jnp.concatenate([v[...] for v in before[:groups]], axis=0)
            back = jnp.concatenate([v[...] for v in before[groups : 2 * groups]], axis=0)
            up_sums[...] = before[2 * groups][...]
        side = lax.axis_index("ctx") & 1 if plan.paired else 0
        here = pl.multiple_of(side * plan.hidden, plan.hidden)
        stores = []
        for i, r in enumerate(slots):
            for copy in loads[i]:
                copy.wait()
            cols = slice(i * plan.hidden, (i + 1) * plan.hidden)
            at = plan.block(r)
            u = nn(n, up[:, cols]) + up_bias[at, :, pl.ds(here, plan.hidden)]
            half = 0.5 * (1.0 + lax.erf(u * (0.5**0.5)))
            z = (u * half).astype(bf16)
            slope = half + u * (jnp.exp(-0.5 * u * u) * 0.3989422804014327)
            d_u = (nn(g, down[:, cols]) * slope).astype(bf16)
            plan.put_hidden(i, 0, nn(n_t, d_u), held)
            plan.put_hidden(i, 1, nn(g_t, z), held)
            stores += plan.start_hidden(i, held, grads, out_sems)
            total = total + nt(z, down[:, cols])
            back = back + nt(d_u, up[:, cols])
            up_sums[at, :, pl.ds(here, plan.hidden)] = row_sum(d_u)
        for i in range(groups):
            outs[i][...] = total[i * rows : (i + 1) * rows].astype(outs[i].dtype)
            backs[i][...] = back[i * rows : (i + 1) * rows].astype(backs[i].dtype)
        for copy in stores:
            copy.wait()

    return kernel


def on_device(
    mesh,
    tokens,
    cotangent,
    norm_gains,
    norm_shifts,
    qkv_spatial,
    proj_spatial,
    qkv_temporal,
    proj_temporal,
    up_weight,
    down_weight,
    out_bias,
    qv_bias,
    up_bias,
):
    shards, _, blocks = mesh.shape["shard"], mesh.shape["ctx"], mesh.shape["tp"]
    patches, model = tokens.shape[2:]
    head_cols = qkv_spatial.shape[2]
    wide = 4 * head_cols
    rows = 16 * SLOT
    plan = Plan(mesh, model, wide)
    paired = plan.paired
    x_rank, z_rank = lax.axis_index("shard"), lax.axis_index("tp")
    q_rank = lax.axis_index("ctx")

    def cut(v, axis, size, at):
        return lax.dynamic_slice_in_dim(v, at * size, size, axis)

    def joined(qkv, proj):
        if paired:
            part = model // 8
            qkv, proj = cut(qkv, 1, part, q_rank), cut(proj, 1, part, q_rank)
        return jnp.concatenate([qkv[0], qkv[1], qkv[2], proj.T], axis=1)

    own_space = joined(qkv_spatial, proj_spatial)
    own_time = joined(qkv_temporal, proj_temporal)
    own_up, own_down = up_weight, down_weight
    if paired:
        part = model // 4
        own_up = cut(cut(own_up, 0, part, q_rank >> 1), 1, plan.hidden, q_rank & 1)
        own_down = cut(cut(own_down, 0, plan.hidden, q_rank & 1), 1, part, q_rank >> 1)
    own_down = own_down.T
    part = norm_gains.shape[1]
    small = [norm_gains, norm_shifts, out_bias, qv_bias.reshape(-1, part), up_bias.reshape(-1, part)]
    small = jnp.concatenate(small, axis=0)
    msg_patch, msg_frame = lay_out(*after((tokens[0], cotangent[0]), own_space))
    own_hidden = jnp.concatenate([own_up, own_down], axis=0)

    if paired:

        def line(own, m):
            with jax.named_scope(f"line{m}"):
                return [own] + [shift_z(own, k) for k in (1, 2, 3)]

        def sides(a, m):
            with jax.named_scope(f"side{m}"):
                return a, flip_x(a), flip_y(a)

        def cores(parts, m):
            with jax.named_scope(f"core{m}"):
                return [flip_core(v) for v in parts]

        l0 = line(own_space, 0)
        with jax.named_scope("small"):
            other = flip_x(small)
        with jax.named_scope("frames"):
            frames = swap_ctx(*msg_frame)
        l0, other, frames[2], own_time, own_hidden = after((l0, other, frames[2], own_time, own_hidden))

        a0, x0, y0 = sides(jnp.stack(l0), 0)
        l1 = line(own_time, 1)
        x0, y0, l1 = after((x0, y0, l1))

        a1, x1, y1 = sides(jnp.stack(l1), 1)
        with jax.named_scope("line2"):
            l2 = shift_z(after(own_hidden, l1), 2)
        core0 = cores(after([a0, x0], l1), 0)
        x1, y1, l2, core0 = after((x1, y1, l2, core0))

        with jax.named_scope("corner0"):
            c0 = flip_x(after(y0, x1))
        with jax.named_scope("corner1"):
            c1 = flip_y(x1)
        with jax.named_scope("patches"):
            by_patch = swap_z_out(after(list(msg_patch), l2))
        c0, c1, by_patch = after((c0, c1, by_patch))

        a2, x2, y2 = sides(jnp.stack(after([own_hidden, l2], c0)), 2)
        core0 += cores([y0, c0], 0)
        with jax.named_scope("line3"):
            own = after(own_hidden, core0)
            l3 = [shift_z(own, 3), shift_z(own, 1)]
        w_space = [a0, x0, y0, c0] + core0
        first = jnp.where(x_rank == 0, small, other)
        second = jnp.where(x_rank == 0, other, small)
        small = jnp.stack([first, second])
    else:

        def gathered(v):
            v = lax.all_gather(v, "shard", axis=0, tiled=True)
            return [lax.all_gather(v, "tp", axis=1, tiled=True)[None]]

        w_space, w_time = gathered(own_space), gathered(own_time)
        w_hidden = lax.all_gather(own_hidden.reshape(2, -1, wide), "shard", axis=1, tiled=True)
        w_first = w_second = [lax.all_gather(w_hidden.reshape(1, 2 * model, wide), "tp", axis=0, tiled=True)]
        small = lax.all_gather(small, "shard", axis=0, tiled=False)
        frames = swap_ctx(*msg_frame)
        by_patch = swap_z_out(msg_patch)

    small = small.astype(f32)
    vectors = jnp.swapaxes(small[:, :13], 0, 1).reshape(13, model)
    gains, shifts, biases = vectors[0:3], vectors[3:6], vectors[6:9]
    qv = vectors[9:13].reshape(2, 2, blocks, head_cols)
    qv = jnp.concatenate([qv[:, 0], jnp.zeros_like(qv[:, 0]), qv[:, 1]], axis=-1)[:, :, None]
    up_b = small[:, 13:].reshape(blocks, 1, -1)

    step = -(-patches // 4)
    slot = jnp.arange(SLOT)[None, :]
    block = (jnp.arange(4) ^ q_rank)[:, None]
    valid = (slot < step) & (block * step + slot < patches)
    key_mask = jnp.where(valid, 0.0, -1e30).astype(f32).reshape(1, 4 * SLOT)
    key_mask = jnp.tile(key_mask, (1, 4))

    weight_scratch = [
        pltpu.VMEM((model, blocks * wide), bf16),
        pltpu.SemaphoreType.DMA((plan.n_loads(),)),
    ]
    p_shape = like((blocks, rows, 3 * head_cols))
    o_shape = like((blocks, rows, head_cols))
    log_shape = like((rows, 128), f32)
    full = like((rows, model), f32)
    unit = like((4, SLOT, model))

    p1, o1, log1, *branch = call(
        attention_forward(plan, False, head_cols, len(w_space)),
        by_patch + [gains[0:1], shifts[0:1], qv[0], key_mask, biases[0:2]] + w_space,
        len(w_space),
        [p_shape, o_shape, log_shape] + [unit] * 4,
        0,
        weight_scratch,
        "space_forward",
        20,
        wait=(0, 1, 2),
    )
    if paired:
        x2, y2, l3, branch = after((x2, y2, l3, branch))
        a3, x3, y3 = sides(jnp.stack(l3), 3)
    with jax.named_scope("branch_z"):
        branch = swap_z_back(branch)
    if paired:
        x3, y3, branch = after((x3, y3, branch))
        with jax.named_scope("corner2"):
            c2 = flip_x(after(y2, x3))
    with jax.named_scope("branch_ctx"):
        near, beside, beyond = to_ctx(branch)
        far = flip_y(beyond)
    if paired:
        core1 = cores(after([a1, x1, y1, c1], far), 1)
        with jax.named_scope("corner3"):
            c3 = [flip_x(y3[:1]), flip_y(after(x3[1:], far))]
        w_time = [a1, x1, y1, c1] + core1
    with jax.named_scope("branch_ctx"):
        branch = [near, flip_core(beside), far, flip_core(far)]
    if paired:
        branch, c2, c3[1] = after((branch, c2, c3[1]))
        w_first, w_second = [a2, x2, y2, c2], [a3, x3, y3, *c3]

    p2, o2, log2, mid, stream, pair = call(
        attention_forward(plan, True, head_cols, len(w_time)),
        frames
        + branch
        + [gains[1:2], shifts[1:2], qv[1], key_mask, biases[0:2], gains[2:3], shifts[2:3]]
        + w_time,
        len(w_time),
        [p_shape, o_shape, log_shape, full, full, like((2, rows, model))],
        0,
        weight_scratch,
        "time_forward",
        20,
        wait=(0, 1, 2, 3, 4),
    )
    pairs = [pair]
    if paired:
        with jax.named_scope("pair_core"):
            pairs.append(flip_core(pair))

    groups = len(pairs)
    hidden_whole = pltpu.VMEM((model, 2 * plan.hidden), bf16)
    hidden_scratch = [hidden_whole, hidden_whole, pltpu.SemaphoreType.DMA((16,))]
    hidden_scratch += plan.hidden_grad_scratch()
    hidden_grads = plan.hidden_grad_shapes()
    n_g = len(hidden_grads)
    up_shape = like((blocks, 1, wide), f32)
    got = call(
        mlp(plan, (0, 2), len(w_first), groups, rows, True),
        pairs + [up_b] + w_first,
        len(w_first),
        hidden_grads + [full] * (2 * groups) + [up_shape],
        n_g,
        hidden_scratch,
        "mlp_first",
        26,
    )
    first_grads, partial = got[:n_g], got[n_g:]
    got = call(
        mlp(plan, (1, 3), len(w_second), groups, rows, False),
        pairs + [up_b] + partial + w_second,
        len(w_second),
        hidden_grads + ([full] + [like((rows, model))] * (groups - 1)) * 2 + [up_shape],
        n_g,
        hidden_scratch,
        "mlp_second",
        26,
    )
    second_grads, results, backs, up_sums = got[:n_g], got[n_g : n_g + groups], got[n_g + groups : -1], got[-1]
    if paired:
        with jax.named_scope("hidden_side"):
            first_moved = [flip_y(first_grads[1]), flip_x(first_grads[3])]
            second_moved = [flip_y(second_grads[1]), flip_x(second_grads[3])]
        with jax.named_scope("back_core"):
            backs = [backs[0], flip_core(backs[1])]

    grads = plan.grad_shapes()
    n_g = len(grads)
    vec_shape = like((24, model), f32)
    qv_held = pltpu.VMEM((blocks, 1, 3 * head_cols), f32)
    d_time, time_vec, time_g, *g1 = call(
        time_backward(plan, head_cols, len(w_time), groups),
        [mid, stream, pair] + backs + [gains[2:3], gains[1:2], log2, p2] + w_time,
        len(w_time),
        [p_shape, vec_shape, like((rows, model))] + [unit] * 2 + [like((2,) + unit.shape)],
        0,
        weight_scratch + [qv_held],
        "time_backward",
        20,
    )
    if paired:
        g1, first_moved = after((g1, first_moved))
    with jax.named_scope("g1_ctx"):
        far = flip_y(g1[2])
    g_time = call(
        time_weights(plan),
        [mid, time_g, gains[1:2], shifts[1:2], d_time, o2],
        0,
        grads,
        n_g,
        plan.grad_scratch(),
        "time_weights",
        16,
    )
    if paired:
        g_time, far, second_moved = after((g_time, far, second_moved))
    with jax.named_scope("g1_ctx"):
        g1 = [g1[0], flip_core(g1[1]), far, flip_core(far)]
    with jax.named_scope("finished"):
        if paired:
            results = [results[0], flip_core(after(results[1], far))]

        def finish(*refs):
            total = refs[0][...] + refs[1][...] + refs[2][...]
            for ref in refs[3 : 2 + groups]:
                total = total + ref[...].astype(f32)
            put_ctx(refs[2 + groups :], nn(turn_rows(total.shape[0]), total.astype(bf16)))

        outs = [unit] * 2 + [like((2,) + unit.shape)]
        finished = call(finish, [biases[2:3], stream] + list(results), 0, outs, 0, [], "finish", 8)
    if paired:
        with jax.named_scope("time_core"):
            got_time = flip_core(g_time[1])
        pairs = [(first_grads[0], first_moved[0]), (second_grads[0], second_moved[0])]
        pairs += [(first_grads[2], first_moved[1]), (second_grads[2], second_moved[1])]
        hidden_rest_a, send_a, hidden_rest_b, send_b = hidden_after_side(pairs)
        with jax.named_scope("hidden_corner"):
            corner_a, corner_b = flip_x(send_a), flip_y(send_b)
    with jax.named_scope("g1_z"):
        g1 = swap_z_out(to_frames(g1))
    if paired:
        keep_ta, send_ta, keep_tb, send_tb = after_core(g_time[0], got_time)
        with jax.named_scope("time_side"):
            side_ta, side_tb = flip_y(after(send_ta, g1)), flip_x(after(send_tb, g1))
        hidden_own, *sends = hidden_after_corner(hidden_rest_a, corner_a, hidden_rest_b, corner_b)
        sends = after(sends, send_ta)
        with jax.named_scope("hidden_line"):
            hidden_moved = [shift_z(v, k) for v, k in zip(sends, (1, 2, 1, 2, 3))]

    got = call(
        space_weights(plan, head_cols, len(w_space)),
        by_patch + g1 + [gains[0:1], shifts[0:1], key_mask, log1, p1, o1] + w_space,
        len(w_space),
        grads + [p_shape],
        n_g,
        weight_scratch + plan.grad_scratch(),
        "space_weights",
        24,
        after=(sends[0], send_ta) if paired else (),
    )
    if paired:
        got, side_ta, side_tb, hidden_moved[:2] = after((got, side_ta, side_tb, hidden_moved[:2]))
    g_space, d_space = got[:n_g], got[n_g]
    vector, *back = call(
        space_backward(plan, head_cols, len(w_space)),
        by_patch + g1 + [time_vec, up_sums, gains[0:1], d_space] + w_space,
        len(w_space),
        [vec_shape] + [unit] * 4,
        0,
        weight_scratch + [qv_held],
        "space_backward",
        16,
    )

    if paired:
        with jax.named_scope("space_core"):
            got_space = flip_core(g_space[1])
        rest_ta, send_ta, rest_tb, send_tb = after_side((keep_ta, side_ta), (keep_tb, side_tb))
        with jax.named_scope("time_corner"):
            corner_ta, corner_tb = flip_x(send_ta), flip_y(send_tb)
        with jax.named_scope("vectors"):
            other = flip_core(vector)
        got_space, other, back, corner_ta, corner_tb, hidden_moved[4] = after(
            (got_space, other, back, corner_ta, corner_tb, hidden_moved[4])
        )

        keep_a, send_a, keep_b, send_b = after_core(g_space[0], got_space)
        with jax.named_scope("space_side"):
            side_a, side_b = flip_y(send_a), flip_x(send_b)
        own_time_sum, *sends = after_corner(rest_ta, corner_ta, rest_tb, corner_tb)
        with jax.named_scope("time_line"):
            time_moved = spread(sends)
        vector, *messages = pack(back[1:], vector, other)
        side_a, side_b, messages, time_moved[:2] = after((side_a, side_b, messages, time_moved[:2]))

        rest_a, send_a, rest_b, send_b = after_side((keep_a, side_a), (keep_b, side_b))
        with jax.named_scope("space_corner"):
            corner_a, corner_b = flip_x(send_a), flip_y(send_b)
        with jax.named_scope("token_grad"):
            moved = [shift_z(v, 4 - k) for k, v in zip((1, 2, 3), after(messages, send_a))]
        with jax.named_scope("finished"):
            far = flip_y(after(finished[2], send_a))
        qkv_time, proj_time = attention_total(own_time_sum, time_moved, head_cols, 2**15)
        corner_a, corner_b, moved, qkv_time, proj_time, far, hidden_moved[2] = after(
            (corner_a, corner_b, moved, qkv_time, proj_time, far, hidden_moved[2])
        )

        own, *sends = after_corner(rest_a, corner_a, rest_b, corner_b)
        with jax.named_scope("space_line"):
            space_moved = spread(sends)
        with jax.named_scope("finished"):
            finished = [finished[0], flip_core(after(finished[1], far)), far, flip_core(far)]
        token_grad, vector = unpack(back[0], vector, moved, patches)
        with jax.named_scope("vectors"):
            vector = vector + flip_y(vector)
            vector = own_vectors(mesh, vector, flip_x(vector))
        hidden_keep, hidden_send = hidden_total(hidden_own, hidden_moved)
        with jax.named_scope("hidden_core"):
            hidden_got = flip_core(hidden_send)
        grad_up, grad_down = hidden_join(hidden_keep, hidden_got)
        qkv_space, proj_space = attention_total(own, space_moved, head_cols, None)
    else:

        def summed(g):
            g = lax.psum_scatter(g.astype(f32), ("shard", "ctx"), scatter_dimension=1, tiled=True)
            return lax.psum_scatter(g, "tp", scatter_dimension=0, tiled=True)[0]

        def apart(total):
            three = total[:, : 3 * head_cols].reshape(-1, 3, head_cols)
            return jnp.swapaxes(three, 0, 1), total[:, 3 * head_cols :].T

        hidden_grad = jnp.concatenate([v[i : i + 1] for i in (0, 1) for v in (first_grads[0], second_grads[0])])
        grad_up, grad_down = summed(hidden_grad[:, :model]), summed(hidden_grad[:, model:])
        qkv_time, proj_time = apart(summed(g_time[0]))
        qkv_space, proj_space = apart(summed(g_space[0]))

    with jax.named_scope("finished"):
        if not paired:
            finished = swap_ctx(*finished)
        finished = bring_back(finished, False, patches, bf16)
    if not paired:
        token_grad = bring_back(swap_z_back(back), True, patches, f32)

    if not paired:
        vector = lax.psum(vector, ("shard", "ctx", "tp"))
        vector = own_vectors(mesh, vector, jnp.zeros_like(vector))
    gains, shifts, biases, qv, hidden = vector
    return (
        finished[None],
        token_grad[None],
        gains,
        shifts,
        qkv_space,
        proj_space,
        qkv_time,
        proj_time,
        grad_up,
        grad_down.T,
        biases,
        qv.reshape(2, 2, -1),
        hidden.reshape(-1),
    )


def solution(mesh):
    return jax.shard_map(
        functools.partial(on_device, mesh),
        mesh=mesh,
        in_specs=(
            P("shard", "ctx", "tp", None),
            P("shard", "ctx", "tp", None),
            P(None, "shard"),
            P(None, "shard"),
            P(None, "shard", "tp"),
            P("tp", "shard"),
            P(None, "shard", "tp"),
            P("tp", "shard"),
            P("shard", "tp"),
            P("tp", "shard"),
            P(None, "shard"),
            P(None, None, "shard"),
            P("shard"),
        ),
        out_specs=(
            P("shard", "ctx", "tp", None),
            P("shard", "ctx", "tp", None),
            P(None, ("shard", "ctx", "tp")),
            P(None, ("shard", "ctx", "tp")),
            P(None, ("shard", "ctx"), "tp"),
            P("tp", ("shard", "ctx")),
            P(None, ("shard", "ctx"), "tp"),
            P("tp", ("shard", "ctx")),
            P(("shard", "ctx"), "tp"),
            P("tp", ("shard", "ctx")),
            P(None, ("shard", "ctx", "tp")),
            P(None, None, ("shard", "ctx", "tp")),
            P(("shard", "ctx", "tp")),
        ),
        check_vma=False,
    )
```

```python
import functools

import jax
import jax.numpy as jnp
from jax import lax
from jax.experimental import pallas as pl
from jax.experimental.pallas import tpu as pltpu
from jax.sharding import PartitionSpec as P

HD = 64
EPS = 1e-06
SCALE = HD ** (-0.5)
SLOT = 16
bf16 = jnp.bfloat16
f32 = jnp.float32
VMEM = pl.BlockSpec(memory_space=pltpu.VMEM)
ANY = pl.BlockSpec(memory_space=pl.ANY)


def nn(a, b):
    return lax.dot_general(a, b, (((1,), (0,)), ((), ())), preferred_element_type=f32)


def nt(a, b):
    return lax.dot_general(a, b, (((1,), (1,)), ((), ())), preferred_element_type=f32)


def tn(a, b):
    return lax.dot_general(a, b, (((0,), (0,)), ((), ())), preferred_element_type=f32)


def turned(a):
    return a.astype(f32).T.astype(bf16)


def row_sum(v):
    return jnp.sum(v.astype(f32), axis=0, keepdims=True)


def standardize(v):
    c = v - jnp.mean(v, axis=-1, keepdims=True)
    r = lax.rsqrt(jnp.mean(c * c, axis=-1, keepdims=True) + EPS)
    return c * r, r


def norm_back(d, q, r, gain):
    e = d * gain
    return r * (e - jnp.mean(e, axis=-1, keepdims=True) - q * jnp.mean(e * q, axis=-1, keepdims=True))


def rows_of(parts):
    return jnp.concatenate([v[...].reshape(-1, v.shape[-1]) for v in parts], axis=0)


def put_rows(refs, value):
    n = value.shape[0] // len(refs)
    for i, r in enumerate(refs):
        r[...] = value[i * n : (i + 1) * n].reshape(r.shape).astype(r.dtype)


def put_ctx(refs, value):
    n = value.shape[0] // 4
    for i, to in enumerate((refs[0], refs[1], refs[2].at[0], refs[2].at[1])):
        to[...] = value[i * n : (i + 1) * n].reshape(to.shape).astype(to.dtype)


def like(shape, dtype=bf16):
    return jax.ShapeDtypeStruct(shape, dtype)


class Take:
    def __init__(self, refs):
        self.refs = list(refs)

    def __call__(self, n):
        got, self.refs = self.refs[:n], self.refs[n:]
        return got


def flip_x(v):
    return lax.ppermute(v, "shard", [(i, i ^ 1) for i in range(2)])


def flip_ctx(v, e):
    return lax.ppermute(v, "ctx", [(i, i ^ e) for i in range(4)])


def flip_core(v):
    return flip_ctx(v, 1)


def flip_y(v):
    return flip_ctx(v, 2)


def shift_z(v, k):
    return lax.ppermute(v, "tp", [(i, (i + k) % 4) for i in range(4)])


def swap_z_out(parts):
    return [parts[0]] + [shift_z(parts[k], k) for k in (1, 2, 3)]


def swap_z_back(parts):
    return [parts[0]] + [shift_z(parts[k], 4 - k) for k in (1, 2, 3)]


def swap_ctx(p0, p1, pair):
    far = flip_y(pair)
    return [p0, flip_core(p1), far, flip_core(far)]


def ctx_parts(refs):
    return [refs[0][...], refs[1][...], refs[2][0], refs[3][1]]


def after(value, *others):
    return lax.optimization_barrier((value, others))[0]


class Plan:
    def __init__(self, mesh, model, wide):
        self.sizes = (mesh.shape["shard"], mesh.shape["ctx"], mesh.shape["tp"])
        self.paired = self.sizes == (2, 4, 4)
        self.model, self.wide, self.blocks = model, wide, self.sizes[2]
        self.hidden = wide // 2 if self.paired else wide

    def ranks(self):
        q = lax.axis_index("ctx")
        return lax.axis_index("shard"), q >> 1, q & 1, lax.axis_index("tp")

    def block(self, r):
        if not self.paired:
            return r
        return lax.rem(lax.axis_index("tp") + r, self.blocks)

    def places(self):
        if not self.paired:
            return [(0, 0, 0, self.model, 0)]
        x, y, c, _ = self.ranks()
        rows = self.model // 8
        every = range(4)
        kinds = [(0, 0, every), (1, 0, every), (0, 1, every), (1, 1, every)]
        out = []
        for core in (0, 1):
            for i, (dx, dy, ks) in enumerate(kinds):
                row = (((x ^ dx) * 2 + (y ^ dy)) * 2 + (c ^ core)) * rows
                for n, k in enumerate(ks):
                    out.append((core * 4 + i, n, pl.multiple_of(row, rows), rows, (4 - k) % 4))
        return out

    def n_loads(self):
        return 32 if self.paired else 1

    def start_loads(self, refs, whole, sems):
        by_slot = [[] for _ in range(self.blocks)]
        for n, (i, k, row, rows, slot) in enumerate(self.places()):
            to = whole.at[pl.ds(row, rows), pl.ds(slot * self.wide, refs[i].shape[-1])]
            by_slot[slot].append(pltpu.make_async_copy(refs[i].at[k], to, sems.at[n]))
        for copies in by_slot:
            for copy in copies:
                copy.start()
        return by_slot

    def start_hidden_loads(self, refs, slots, up, down, sems):
        by_slot = [[], []]
        if self.paired:
            x, y, _, _ = self.ranks()
            rows = self.model // 4
            kinds = [(0, 0, (0, 1)), (1, 0, (0, 1)), (0, 1, (0, 1))]
            kinds += [(1, 1, (0, 1))] if len(refs) == 4 else [(1, 1, (0,)), (1, 1, (1,))]
            places = []
            for ref, (dx, dy, ks) in zip(refs, kinds):
                row = pl.multiple_of(((x ^ dx) * 2 + (y ^ dy)) * rows, rows)
                places += [(ref.at[n], row, k) for n, k in enumerate(ks)]
        else:
            rows = self.model
            places = [(refs[0].at[r], 0, i) for i, r in enumerate(slots)]
        for n, (source, row, i) in enumerate(places):
            for part, whole in enumerate((up, down)):
                to = whole.at[pl.ds(row, rows), pl.ds(i * self.hidden, self.hidden)]
                copy = pltpu.make_async_copy(source.at[part * rows : (part + 1) * rows], to, sems.at[2 * n + part])
                by_slot[i].append(copy)
        for copies in by_slot:
            for copy in copies:
                copy.start()
        return by_slot

    def grad_shapes(self):
        if self.paired:
            return [like((2, 2, 4, self.model // 8, self.wide))] * 2
        return [like((self.blocks, self.model, self.wide))]

    def grad_scratch(self):
        if self.paired:
            held = pltpu.VMEM((4, 2, 2, 2, self.model // 8, self.wide), bf16)
            return [held, pltpu.SemaphoreType.DMA((8,))]
        return [
            pltpu.VMEM((self.blocks, self.model, self.wide), bf16),
            pltpu.SemaphoreType.DMA((self.blocks,)),
        ]

    def hold(self, r, value, held):
        value = value.astype(bf16)
        if not self.paired:
            held[r] = value
            return
        x, y, c, _ = self.ranks()
        rows = self.model // 8
        for i in range(8):
            held[r, (i & 1) ^ c, ((i >> 1) & 1) ^ y, (i >> 2) ^ x] = value[i * rows : (i + 1) * rows]

    def store(self, held, outs, sems):
        copies = []
        for r in range(self.blocks):
            if not self.paired:
                copies.append(pltpu.make_async_copy(held.at[r], outs[0].at[r], sems.at[r]))
                continue
            for core in (1, 0):
                to = outs[core].at[:, :, r]
                copies.append(pltpu.make_async_copy(held.at[r, core], to, sems.at[2 * r + core]))
        for copy in copies:
            copy.start()
        for copy in copies:
            copy.wait()

    def hidden_grad_shapes(self):
        if self.paired:
            return [like((2, self.model // 2, self.hidden))] * 4
        return [like((2, 2 * self.model, self.hidden))]

    def hidden_grad_scratch(self):
        if self.paired:
            held = pltpu.VMEM((2, 2, 2, self.model // 2, self.hidden), bf16)
            return [held, pltpu.SemaphoreType.DMA((4,))]
        return [pltpu.VMEM((2, 2 * self.model, self.hidden), bf16), pltpu.SemaphoreType.DMA((2,))]

    def put_hidden(self, i, part, value, held):
        value = value.astype(bf16)
        if not self.paired:
            held[i, part * self.model : (part + 1) * self.model] = value
            return
        x, y, _, _ = self.ranks()
        rows = self.model // 4
        for n in range(4):
            to = held.at[i, (n & 1) ^ y, (n >> 1) ^ x]
            to[part * rows : (part + 1) * rows] = value[n * rows : (n + 1) * rows]

    def start_hidden(self, i, held, outs, sems):
        if not self.paired:
            copies = [pltpu.make_async_copy(held.at[i], outs[0].at[i], sems.at[i])]
        else:
            copies = []
            for side in (0, 1):
                source = held.at[i, side] if i == 0 else held.at[i, :, side]
                copies.append(pltpu.make_async_copy(source, outs[2 * i + side], sems.at[2 * i + side]))
        for copy in copies:
            copy.start()
        return copies


def call(kernel, ins, n_any, outs, n_any_out, scratch, name, limit, after=(), far=None, wait=()):
    n_in, n_after = len(ins), len(after)

    def run(*refs):
        kernel(*refs[:n_in], *refs[n_in + n_after :])

    ins = list(ins)
    for i, v in enumerate(ins):
        if i >= n_in - n_any or (far is not None and v.size >= far):
            ins[i] = pltpu.with_memory_space_constraint(v, pltpu.HBM)
    outs = [pltpu.HBM(v.shape, v.dtype) if i in wait else v for i, v in enumerate(outs)]
    got = pl.pallas_call(
        run,
        out_shape=outs,
        in_specs=[VMEM] * (n_in - n_any) + [ANY] * (n_any + n_after),
        out_specs=[ANY] * n_any_out + [VMEM] * (len(outs) - n_any_out),
        scratch_shapes=scratch,
        compiler_params=pltpu.CompilerParams(vmem_limit_bytes=limit * 2**20),
        name=name,
    )(*ins, *after)
    return list(got)


def add(u, v):
    return (u.astype(f32) + v.astype(f32)).astype(bf16)


def after_core(keep, got):
    rows, wide = keep.shape[-2:]
    cut = 3

    def kernel(k, g, keep_a, send_a, keep_b, send_b):
        for x in (0, 1):
            keep_a[x] = add(k[0, x, :2], g[0, x, :2])
            send_a[x] = add(k[1, x, :2], g[1, x, :2])
        for y in (0, 1):
            keep_b[y] = add(k[y, 0, 2:], g[y, 0, 2:])
            send_b[y] = add(k[y, 1, 2:], g[y, 1, 2:])

    whole = pl.BlockSpec((2, 2, 4, rows // cut, wide), lambda i: (0, 0, 0, i, 0))
    half = pl.BlockSpec((2, 2, rows // cut, wide), lambda i: (0, 0, i, 0))
    return pl.pallas_call(
        kernel,
        grid=(cut,),
        out_shape=[like((2, 2, rows, wide))] * 4,
        in_specs=[whole] * 2,
        out_specs=[half] * 4,
        compiler_params=pltpu.CompilerParams(vmem_limit_bytes=16 * 2**20),
        name="after_core",
    )(keep, got)


def after_side(*pairs):
    def kernel(*refs):
        n = len(pairs)
        for i in range(n):
            k, g = refs[2 * i], refs[2 * i + 1]
            refs[2 * n + 2 * i][...] = add(k[0], g[0])
            refs[2 * n + 2 * i + 1][...] = add(k[1], g[1])

    ins = [v for pair in pairs for v in pair]
    outs = [like(v.shape[1:]) for v in ins]
    return call(kernel, ins, 0, outs, 0, [], "after_side", 24, wait=range(0, 2 * len(pairs), 2))


def hidden_after_side(pairs):
    def kernel(*refs):
        for i in range(4):
            k, g = refs[2 * i], refs[2 * i + 1]
            rest, send = refs[8 + 2 * (i // 2)], refs[9 + 2 * (i // 2)]
            rest[i % 2] = add(k[0], g[0])
            send[i % 2] = add(k[1], g[1])

    ins = [v for pair in pairs for v in pair]
    return call(kernel, ins, 0, [like(ins[0].shape)] * 4, 0, [], "hidden_after_side", 24)


def after_corner(rest_a, got_a, rest_b, got_b):
    def kernel(ra, ga, rb, gb, own, *sends):
        own[...] = ra[0].astype(f32) + ga[0].astype(f32)
        sends[0][...] = add(ra[1], ga[1])
        sends[1][...] = add(rb[0], gb[0])
        sends[2][...] = add(rb[1], gb[1])

    shape = rest_a.shape[1:]
    outs = [like(shape, f32)] + [like(shape)] * 3
    return call(kernel, [rest_a, got_a, rest_b, got_b], 0, outs, 0, [], "after_corner", 12)


def hidden_after_corner(rest_a, got_a, rest_b, got_b):
    rows = rest_a.shape[1] // 2

    def kernel(ra, ga, rb, gb, own, *sends):
        own[...] = ra[0].astype(f32) + ga[0].astype(f32)
        for part in (0, 1):
            at = slice(part * rows, (part + 1) * rows)
            sends[2 * part][...] = add(ra[1, at], ga[1, at])
            sends[2 * part + 1][...] = add(rb[0, at], gb[0, at])
        sends[4][...] = add(rb[1], gb[1])

    shape = rest_a.shape[1:]
    half = (rows,) + shape[1:]
    outs = [like(shape, f32)] + [like(half)] * 4 + [like(shape)]
    return call(kernel, [rest_a, got_a, rest_b, got_b], 0, outs, 0, [], "hidden_after_corner", 12)


def spread(sends):
    return [shift_z(v, k) for k, v in zip((1, 2, 3), sends)]


def attention_total(own, moved, head_cols, far):
    rows = own.shape[0]
    three = 3 * head_cols

    def kernel(o, a, b, c, qkv, proj):
        total = o[...] + a[...].astype(f32) + b[...].astype(f32) + c[...].astype(f32)
        for t in range(3):
            qkv[t] = total[:, t * head_cols : (t + 1) * head_cols]
        proj[...] = total[:, three:].T

    outs = [like((3, rows, head_cols), f32), like((head_cols, rows), f32)]
    return call(kernel, [own] + moved, 0, outs, 0, [], "attention_total", 8, far=far)


def hidden_total(own, moved):
    rows, wide = own.shape[0] // 4, own.shape[1]

    def kernel(o, up_1, up_2, down_1, down_2, both, keep, send):
        core = lax.axis_index("ctx") & 1
        for part, pair in enumerate(((up_1, up_2), (down_1, down_2))):
            for half in (0, 1):
                at = slice(half * rows, (half + 1) * rows)
                of = slice((2 * part + half) * rows, (2 * part + half + 1) * rows)
                total = o[of] + both[of].astype(f32) + pair[0][at].astype(f32) + pair[1][at].astype(f32)

                @pl.when(core == half)
                def _(total=total, part=part):
                    keep[part] = total

                @pl.when(core != half)
                def _(total=total, part=part):
                    send[part] = total.astype(bf16)

    outs = [like((2, rows, wide), f32), like((2, rows, wide))]
    return call(kernel, [own] + moved, 0, outs, 0, [], "hidden_total", 8)


def hidden_join(keep, got):
    rows, wide = keep.shape[1:]

    def kernel(k, g, up, down):
        core = lax.axis_index("ctx") & 1
        here, there = pl.multiple_of(core * wide, wide), pl.multiple_of((1 - core) * wide, wide)
        for part, out in enumerate((up, down)):
            out[:, pl.ds(here, wide)] = k[part]
            out[:, pl.ds(there, wide)] = g[part].astype(f32)

    return call(kernel, [keep, got], 0, [like((rows, 2 * wide), f32)] * 2, 0, [], "hidden_join", 8)


def lay_out(x, c):
    frames, patches, width = x.shape
    step = -(-patches // 4)

    def kernel(x_ref, c_ref, *refs):
        by_patch, by_frame, held = refs[:4], refs[4:7], refs[7]
        z, q = lax.axis_index("tp"), lax.axis_index("ctx")
        for i, ref in enumerate((x_ref, c_ref)):
            for f in range(4):
                v = ref[f].astype(f32)
                for b in range(4):
                    part = v[b * step : min((b + 1) * step, patches)]
                    pad = jnp.zeros((SLOT - part.shape[0], width), f32)
                    held[i, f, b] = jnp.concatenate([part, pad], axis=0).astype(bf16)
        for s in range(4):
            f = lax.rem(z + s, 4)
            for e in range(4):
                by_patch[s][e * SLOT : (e + 1) * SLOT] = held[0, f, q ^ e]
                to = by_frame[e] if e < 2 else by_frame[2].at[e - 2]
                to[0, s] = held[0, f, q ^ e]
                to[1, s] = held[1, f, q ^ e]

    both = (2, 4, SLOT, width)
    outs = [like((4 * SLOT, width))] * 4 + [like(both)] * 2 + [like((2,) + both)]
    got = call(kernel, [x, c], 0, outs, 0, [pltpu.VMEM((2, 4, 4, SLOT, width), bf16)], "lay_out", 8)
    return got[:4], got[4:]


def put_tokens(values, frames_first, held, out):
    z, q = lax.axis_index("tp"), lax.axis_index("ctx")
    patches, width = out.shape[0], out.shape[-1]
    step = -(-patches // 4)
    for i, v in enumerate(values):
        v = v.reshape(4, SLOT, width).astype(f32)
        if frames_first:
            held[i] = v
        else:
            held[:, i] = v
    for f in range(4):
        s = lax.rem(f + 4 - z, 4)
        rows = [held[s, b ^ q][: min(step, patches - b * step)] for b in range(4)]
        out[:, f] = jnp.concatenate(rows, axis=0).astype(out.dtype)


def bring_back(parts, frames_first, patches, dtype):
    width = parts[0].shape[-1]

    def kernel(*refs):
        ins, out, held = refs[:4], refs[4], refs[5]
        put_tokens([r[...] for r in ins] if frames_first else ctx_parts(ins), frames_first, held, out)

    scratch = [pltpu.VMEM((4, 4, SLOT, width), f32)]
    got = call(kernel, parts, 0, [like((patches, 4, width), dtype)], 0, scratch, "bring_back", 8)
    return jnp.swapaxes(got[0], 0, 1)


def pack(parts, vector, other):
    rows, width = 4 * SLOT, parts[0].shape[-1]
    extra = vector.shape[0]

    def kernel(a, b, c, vec, far, total, *outs):
        v = vec[...] + far[...]
        total[...] = v
        high = v.astype(bf16)
        low = (v - high.astype(f32)).astype(bf16)
        below = jnp.concatenate([high.astype(f32), low.astype(f32)], axis=0).astype(bf16)
        for part, out in zip((a, b, c), outs):
            out[:rows] = part[...].reshape(rows, width)
            out[rows:] = below

    outs = [like(vector.shape, f32)] + [like((rows + 2 * extra, width))] * 3
    return call(kernel, parts + [vector, other], 0, outs, 0, [], "pack", 8)


def own_vectors(mesh, vector, other):
    blocks, model = mesh.shape["tp"], vector.shape[-1]
    many = mesh.size
    size, hidden = model // many, 4 * model // many

    def kernel(vec, far, gains, shifts, biases, qv, up):
        place = (lax.axis_index("shard") * mesh.shape["ctx"] + lax.axis_index("ctx")) * blocks + lax.axis_index("tp")
        total = vec[...] + far[...]
        mine = pltpu.roll(total, lax.rem(model - place * size, model), 1)[:, :size]
        gains[...] = mine[0:3]
        shifts[...] = mine[3:6]
        biases[...] = mine[6:9]
        qv[...] = mine[9:13]
        at = place * hidden
        for row in range(4):

            @pl.when(lax.div(at, model) == row)
            def _(row=row):
                here = total[13 + row : 14 + row]
                up[...] = pltpu.roll(here, lax.rem(model - lax.rem(at, model), model), 1)[:, :hidden]

    outs = [like((3, size), f32)] * 3 + [like((4, size), f32), like((1, hidden), f32)]
    return call(kernel, [vector, other], 0, outs, 0, [], "own_vectors", 4)


def unpack(own, vector, moved, patches):
    rows, width = 4 * SLOT, own.shape[-1]
    extra = vector.shape[0]

    def kernel(*refs):
        own_ref, vec, ins = refs[0], refs[1], refs[2:5]
        out, total, held = refs[5:]
        put_tokens([own_ref[...]] + [r[:rows] for r in ins], True, held, out)
        v = vec[...]
        for r in ins:
            below = r[rows:].astype(f32)
            v = v + (below[:extra] + below[extra:])
        total[...] = v

    scratch = [pltpu.VMEM((4, 4, SLOT, width), f32)]
    outs = [like((patches, 4, width), f32), like(vector.shape, f32)]
    token_grad, total = call(kernel, [own, vector] + moved, 0, outs, 0, scratch, "unpack", 8, far=2**15)
    return jnp.swapaxes(token_grad, 0, 1), total


def to_ctx(parts):
    def kernel(*refs):
        for s in range(4):
            for e in range(4):
                to = refs[4 + e] if e < 2 else refs[6].at[e - 2]
                to[s] = refs[s][e]

    shape = parts[0].shape
    return call(kernel, parts, 0, [like(shape)] * 2 + [like((2,) + shape)], 0, [], "to_ctx", 4)


def to_frames(parts):
    def kernel(*refs):
        for e, v in enumerate(ctx_parts(refs[:4])):
            for s in range(4):
                refs[4 + s][e] = v[s]

    return call(kernel, parts, 0, [like(parts[0].shape)] * 4, 0, [], "to_frames", 4)


def turn_rows(rows):
    a = lax.broadcasted_iota(jnp.int32, (rows, rows), 0)
    b = lax.broadcasted_iota(jnp.int32, (rows, rows), 1)
    bits = SLOT.bit_length() - 1
    return jnp.where(b == ((a & (SLOT - 1)) << bits) + (a >> bits), 1.0, 0.0).astype(bf16)


def masks_of(timed, rows, mask_ref):
    if not timed:
        return [slice(0, rows)], mask_ref[...]
    half = rows // 2
    a = lax.broadcasted_iota(jnp.int32, (half, half), 0)
    b = lax.broadcasted_iota(jnp.int32, (half, half), 1)
    return [slice(0, half), slice(half, rows)], jnp.where((a ^ b) < SLOT, 0.0, -1e30).astype(f32)


def head_slices(p, h, head_cols):
    return [p[:, t * head_cols + h * HD : t * head_cols + (h + 1) * HD] for t in range(3)]


def attention_forward(plan, timed, head_cols, n_w):
    heads = head_cols // HD
    three = 3 * head_cols

    def kernel(*refs):
        take = Take(refs)
        x_refs = take(4)
        b_refs = take(4) if timed else []
        gain, shift, qv, mask_ref, bias_in = take(5)
        next_norm = take(2) if timed else []
        w_refs = take(n_w)
        p_ref, o_ref, log_ref = take(3)
        outs = take(3) if timed else take(4)
        whole, sems = take(2)
        loads = plan.start_loads(w_refs, whole, sems)
        if timed:
            parts = ctx_parts(x_refs)
            swap = turn_rows(log_ref.shape[0])
            x = nn(swap, rows_of([v[0] for v in parts]))
            x = x + nn(swap, rows_of(ctx_parts(b_refs))) + bias_in[0:1]
            outs[0][...] = x
            outs[2][1] = nn(swap, rows_of([v[1] for v in parts])).astype(bf16)
        else:
            x = rows_of(x_refs).astype(f32)
        ranges, mask = masks_of(timed, x.shape[0], mask_ref)
        q, _ = standardize(x)
        n = (q * gain[...] + shift[...]).astype(bf16)
        total = jnp.zeros(x.shape, f32)
        scale = jnp.where(lax.broadcasted_iota(jnp.int32, (1, three), 1) < head_cols, SCALE, 1.0).astype(f32)
        rows = x.shape[0]
        for r in range(plan.blocks):
            at = r * plan.wide
            for copy in loads[r]:
                copy.wait()
            p = ((nn(n, whole[:, at : at + three]) + qv[plan.block(r)]) * scale).astype(bf16)
            p_ref[r] = p
            cells = [[v[m] for v in head_slices(p, h, head_cols)] for h in range(heads) for m in ranges]
            s = jnp.concatenate([nt(qh, kh) + mask for qh, kh, _ in cells], axis=0)
            top = jnp.max(s, axis=-1, keepdims=True)
            e = jnp.exp(s - top)
            total_e = jnp.sum(e, axis=-1, keepdims=True)
            log = top + jnp.log(total_e)
            w = (e / total_e).astype(bf16)
            size = mask.shape[-1]
            o = [nn(w[i * size : (i + 1) * size], vh) for i, (_, _, vh) in enumerate(cells)]
            for h in range(heads):
                log_ref[:, r * heads + h : r * heads + h + 1] = log[h * rows : (h + 1) * rows]
            n_m = len(ranges)
            o = jnp.concatenate(
                [jnp.concatenate(o[h * n_m : (h + 1) * n_m], axis=0) for h in range(heads)], axis=-1
            ).astype(bf16)
            o_ref[r] = o
            total = total + nt(o, whole[:, at + three : at + plan.wide])
        if timed:
            x = x + total + bias_in[1:2]
            outs[1][...] = x
            q, _ = standardize(x)
            outs[2][0] = (q * next_norm[0][...] + next_norm[1][...]).astype(bf16)
        else:
            put_rows(outs, total)

    return kernel


def heads_backward(p, d_o, log, ranges, mask, head_cols):
    heads, n_m, size = head_cols // HD, len(ranges), mask.shape[-1]
    cells = []
    for h in range(heads):
        parts = head_slices(p, h, head_cols) + [d_o[:, h * HD : (h + 1) * HD], log[:, h : h + 1]]
        cells += [[v[m] for v in parts] for m in ranges]
    s = jnp.concatenate([nt(qh, kh) + (mask - lh) for qh, kh, _, _, lh in cells], axis=0)
    d_w = jnp.concatenate([nt(doh, vh) for _, _, vh, doh, _ in cells], axis=0)
    w = jnp.exp(s)
    d_s = (w * (d_w - jnp.sum(d_w * w, axis=-1, keepdims=True))).astype(bf16)
    w = w.astype(bf16)
    at = [slice(i * size, (i + 1) * size) for i in range(len(cells))]
    d_q = [nn(d_s[m], cell[1]) * SCALE for m, cell in zip(at, cells)]
    d_k = [tn(d_s[m], cell[0]) for m, cell in zip(at, cells)]
    d_v = [tn(w[m], cell[3]) for m, cell in zip(at, cells)]
    columns = [jnp.concatenate(v[h * n_m : (h + 1) * n_m], axis=0) for v in (d_q, d_k, d_v) for h in range(heads)]
    return jnp.concatenate(columns, axis=-1).astype(bf16)


def put_qv(vec, layer, qv_held, head_cols):
    for i, t in enumerate((0, 2)):
        row = [qv_held[j][:, t * head_cols : (t + 1) * head_cols] for j in range(qv_held.shape[0])]
        vec[9 + 2 * layer + i : 10 + 2 * layer + i] = jnp.concatenate(row, axis=-1)


def time_backward(plan, head_cols, n_w, n_back):
    heads = head_cols // HD
    three = 3 * head_cols

    def kernel(*refs):
        take = Take(refs)
        x_ref, next_x, pair = take(3)
        back_refs = take(n_back)
        next_gain, gain, log_ref = take(3)
        (p_ref,) = take(1)
        w_refs = take(n_w)
        d_ref, vec, g_out = take(3)
        outs = take(3)
        whole, sems, qv_held = take(3)
        loads = plan.start_loads(w_refs, whole, sems)
        vec[...] = jnp.zeros(vec.shape, f32)
        x = x_ref[...]
        rows = x.shape[0]
        ranges, mask = masks_of(True, rows, None)
        g = pair[1].astype(f32)
        q3, r3 = standardize(next_x[...])
        d = back_refs[0][...].astype(f32)
        for ref in back_refs[1:]:
            d = d + ref[...].astype(f32)
        vec[2:3] = row_sum(d * q3)
        vec[5:6] = row_sum(d)
        vec[8:9] = row_sum(g)
        g = g + norm_back(d, q3, r3, next_gain[...])
        g_b = g.astype(bf16)
        g_out[...] = g_b
        vec[7:8] = row_sum(g_b)
        q, r_x = standardize(x)
        d_n = jnp.zeros(x.shape, f32)
        for r in range(plan.blocks):
            at = r * plan.wide
            for copy in loads[r]:
                copy.wait()
            d_o = nn(g_b, whole[:, at + three : at + plan.wide]).astype(bf16)
            log = log_ref[:, r * heads : (r + 1) * heads]
            d_p = heads_backward(p_ref[r], d_o, log, ranges, mask, head_cols)
            d_ref[r] = d_p
            qv_held[plan.block(r)] = row_sum(d_p)
            d_n = d_n + nt(d_p, whole[:, at : at + three])
        vec[1:2] = row_sum(d_n * q)
        vec[4:5] = row_sum(d_n)
        put_qv(vec, 1, qv_held, head_cols)
        g = g + norm_back(d_n, q, r_x, gain[...])
        put_ctx(outs, nn(turn_rows(rows), g.astype(bf16)))

    return kernel


def time_weights(plan):
    def kernel(*refs):
        take = Take(refs)
        x_ref, g_ref, gain, shift = take(4)
        d_ref, o_ref = take(2)
        grads = take(len(plan.grad_shapes()))
        held, out_sems = take(2)
        q, _ = standardize(x_ref[...])
        n_t = (q * gain[...] + shift[...]).T.astype(bf16)
        g_t = turned(g_ref[...])
        for r in range(plan.blocks):
            block = jnp.concatenate([nn(n_t, d_ref[r]), nn(g_t, o_ref[r])], axis=-1)
            plan.hold(r, block, held)
        plan.store(held, grads, out_sems)

    return kernel


def space_weights(plan, head_cols, n_w):
    heads = head_cols // HD
    three = 3 * head_cols

    def kernel(*refs):
        take = Take(refs)
        x_refs, g_refs = take(4), take(4)
        gain, shift, mask_ref, log_ref = take(4)
        p_ref, o_ref = take(2)
        w_refs = take(n_w)
        grads = take(len(plan.grad_shapes()))
        (d_ref,) = take(1)
        whole, sems, held, out_sems = take(4)
        loads = plan.start_loads(w_refs, whole, sems)
        x = rows_of(x_refs).astype(f32)
        g_b = rows_of(g_refs)
        g_t = turned(g_b)
        ranges, mask = masks_of(False, x.shape[0], mask_ref)
        q, _ = standardize(x)
        n_t = (q * gain[...] + shift[...]).T.astype(bf16)
        for r in range(plan.blocks):
            at = r * plan.wide
            for copy in loads[r]:
                copy.wait()
            d_o = nn(g_b, whole[:, at + three : at + plan.wide]).astype(bf16)
            log = log_ref[:, r * heads : (r + 1) * heads]
            d_p = heads_backward(p_ref[r], d_o, log, ranges, mask, head_cols)
            d_ref[r] = d_p
            block = jnp.concatenate([nn(n_t, d_p), nn(g_t, o_ref[r])], axis=-1)
            plan.hold(r, block, held)
        plan.store(held, grads, out_sems)

    return kernel


def space_backward(plan, head_cols, n_w):
    three = 3 * head_cols

    def kernel(*refs):
        take = Take(refs)
        x_refs, g_refs = take(4), take(4)
        time_vec, up_sums, gain = take(3)
        (d_ref,) = take(1)
        w_refs = take(n_w)
        (vec,) = take(1)
        outs = take(4)
        whole, sems, qv_held = take(3)
        loads = plan.start_loads(w_refs, whole, sems)
        x, g = rows_of(x_refs).astype(f32), rows_of(g_refs).astype(f32)
        vec[...] = time_vec[...]
        for j in range(up_sums.shape[0]):
            vec[13 + j : 14 + j] = up_sums[j]
        vec[6:7] = row_sum(g)
        q, r_x = standardize(x)
        d_n = jnp.zeros(x.shape, f32)
        for r in range(plan.blocks):
            at = r * plan.wide
            for copy in loads[r]:
                copy.wait()
            d_p = d_ref[r]
            qv_held[plan.block(r)] = row_sum(d_p)
            d_n = d_n + nt(d_p, whole[:, at : at + three])
        vec[0:1] = row_sum(d_n * q)
        vec[3:4] = row_sum(d_n)
        put_qv(vec, 0, qv_held, head_cols)
        put_rows(outs, g + norm_back(d_n, q, r_x, gain[...]))

    return kernel


def mlp(plan, slots, n_w, groups, rows, first):
    def kernel(*refs):
        take = Take(refs)
        pairs = take(groups)
        (up_bias,) = take(1)
        before = [] if first else take(2 * groups + 1)
        w_refs = take(n_w)
        grads = take(len(plan.hidden_grad_shapes()))
        outs = take(groups)
        backs = take(groups)
        (up_sums,) = take(1)
        up, down, load_sems, held, out_sems = take(5)
        loads = plan.start_hidden_loads(w_refs, slots, up, down, load_sems)
        n = jnp.concatenate([v[0] for v in pairs], axis=0)
        g = jnp.concatenate([v[1] for v in pairs], axis=0)
        n_t, g_t = turned(n), turned(g)
        if first:
            total = jnp.zeros(n.shape, f32)
            back = jnp.zeros(n.shape, f32)
            up_sums[...] = jnp.zeros(up_sums.shape, f32)
        else:
            total = jnp.concatenate([v[...] for v in before[:groups]], axis=0)
            back = jnp.concatenate([v[...] for v in before[groups : 2 * groups]], axis=0)
            up_sums[...] = before[2 * groups][...]
        side = lax.axis_index("ctx") & 1 if plan.paired else 0
        here = pl.multiple_of(side * plan.hidden, plan.hidden)
        for copies in loads:
            for copy in copies:
                copy.wait()
        places = [plan.block(r) for r in slots]
        u = nn(n, up[...]) + jnp.concatenate([up_bias[at, :, pl.ds(here, plan.hidden)] for at in places], axis=-1)
        half = 0.5 * (1.0 + lax.erf(u * (0.5**0.5)))
        z = (u * half).astype(bf16)
        slope = half + u * (jnp.exp(-0.5 * u * u) * 0.3989422804014327)
        d_u = (nn(g, down[...]) * slope).astype(bf16)
        up_grad, down_grad = nn(n_t, d_u), nn(g_t, z)
        sums = row_sum(d_u)
        stores = []
        for i, at in enumerate(places):
            cols = slice(i * plan.hidden, (i + 1) * plan.hidden)
            plan.put_hidden(i, 0, up_grad[:, cols], held)
            plan.put_hidden(i, 1, down_grad[:, cols], held)
            stores += plan.start_hidden(i, held, grads, out_sems)
            up_sums[at, :, pl.ds(here, plan.hidden)] = sums[:, cols]
        total = total + nt(z, down[...])
        back = back + nt(d_u, up[...])
        for i in range(groups):
            outs[i][...] = total[i * rows : (i + 1) * rows].astype(outs[i].dtype)
            backs[i][...] = back[i * rows : (i + 1) * rows].astype(backs[i].dtype)
        for copy in stores:
            copy.wait()

    return kernel


def on_device(
    mesh,
    tokens,
    cotangent,
    norm_gains,
    norm_shifts,
    qkv_spatial,
    proj_spatial,
    qkv_temporal,
    proj_temporal,
    up_weight,
    down_weight,
    out_bias,
    qv_bias,
    up_bias,
):
    shards, _, blocks = mesh.shape["shard"], mesh.shape["ctx"], mesh.shape["tp"]
    patches, model = tokens.shape[2:]
    head_cols = qkv_spatial.shape[2]
    wide = 4 * head_cols
    rows = 16 * SLOT
    plan = Plan(mesh, model, wide)
    paired = plan.paired
    x_rank, z_rank = lax.axis_index("shard"), lax.axis_index("tp")
    q_rank = lax.axis_index("ctx")

    def cut(v, axis, size, at):
        return lax.dynamic_slice_in_dim(v, at * size, size, axis)

    def joined(qkv, proj):
        if paired:
            part = model // 8
            qkv, proj = cut(qkv, 1, part, q_rank), cut(proj, 1, part, q_rank)
        return jnp.concatenate([qkv[0], qkv[1], qkv[2], proj.T], axis=1)

    own_space = joined(qkv_spatial, proj_spatial)
    own_time = joined(qkv_temporal, proj_temporal)
    own_up, own_down = up_weight, down_weight
    if paired:
        part = model // 4
        own_up = cut(cut(own_up, 0, part, q_rank >> 1), 1, plan.hidden, q_rank & 1)
        own_down = cut(cut(own_down, 0, plan.hidden, q_rank & 1), 1, part, q_rank >> 1)
    own_down = own_down.T
    part = norm_gains.shape[1]
    small = [norm_gains, norm_shifts, out_bias, qv_bias.reshape(-1, part), up_bias.reshape(-1, part)]
    small = jnp.concatenate(small, axis=0)
    msg_patch, msg_frame = lay_out(*after((tokens[0], cotangent[0]), own_space))
    own_hidden = jnp.concatenate([own_up, own_down], axis=0)

    if paired:

        def line(own, m):
            with jax.named_scope(f"line{m}"):
                return [own] + [shift_z(own, k) for k in (1, 2, 3)]

        def sides(a, m):
            with jax.named_scope(f"side{m}"):
                return a, flip_x(a), flip_y(a)

        def cores(parts, m):
            with jax.named_scope(f"core{m}"):
                return [flip_core(v) for v in parts]

        l0 = line(own_space, 0)
        with jax.named_scope("small"):
            other = flip_x(small)
        with jax.named_scope("frames"):
            frames = swap_ctx(*msg_frame)
        l0, other, frames[2], own_time, own_hidden = after((l0, other, frames[2], own_time, own_hidden))

        a0, x0, y0 = sides(jnp.stack(l0), 0)
        l1 = line(own_time, 1)
        x0, y0, l1 = after((x0, y0, l1))

        a1, x1, y1 = sides(jnp.stack(l1), 1)
        with jax.named_scope("line2"):
            l2 = shift_z(after(own_hidden, l1), 2)
        core0 = cores(after([a0, x0], l1), 0)
        x1, y1, l2, core0 = after((x1, y1, l2, core0))

        with jax.named_scope("corner0"):
            c0 = flip_x(after(y0, x1))
        with jax.named_scope("corner1"):
            c1 = flip_y(x1)
        with jax.named_scope("patches"):
            by_patch = swap_z_out(after(list(msg_patch), l2))
        c0, c1, by_patch = after((c0, c1, by_patch))

        a2, x2, y2 = sides(jnp.stack(after([own_hidden, l2], c0)), 2)
        core0 += cores([y0, c0], 0)
        with jax.named_scope("line3"):
            own = after(own_hidden, core0)
            l3 = [shift_z(own, 3), shift_z(own, 1)]
        w_space = [a0, x0, y0, c0] + core0
        first = jnp.where(x_rank == 0, small, other)
        second = jnp.where(x_rank == 0, other, small)
        small = jnp.stack([first, second])
    else:

        def gathered(v):
            v = lax.all_gather(v, "shard", axis=0, tiled=True)
            return [lax.all_gather(v, "tp", axis=1, tiled=True)[None]]

        w_space, w_time = gathered(own_space), gathered(own_time)
        w_hidden = lax.all_gather(own_hidden.reshape(2, -1, wide), "shard", axis=1, tiled=True)
        w_first = w_second = [lax.all_gather(w_hidden.reshape(1, 2 * model, wide), "tp", axis=0, tiled=True)]
        small = lax.all_gather(small, "shard", axis=0, tiled=False)
        frames = swap_ctx(*msg_frame)
        by_patch = swap_z_out(msg_patch)

    small = small.astype(f32)
    vectors = jnp.swapaxes(small[:, :13], 0, 1).reshape(13, model)
    gains, shifts, biases = vectors[0:3], vectors[3:6], vectors[6:9]
    qv = vectors[9:13].reshape(2, 2, blocks, head_cols)
    qv = jnp.concatenate([qv[:, 0], jnp.zeros_like(qv[:, 0]), qv[:, 1]], axis=-1)[:, :, None]
    up_b = small[:, 13:].reshape(blocks, 1, -1)

    step = -(-patches // 4)
    slot = jnp.arange(SLOT)[None, :]
    block = (jnp.arange(4) ^ q_rank)[:, None]
    valid = (slot < step) & (block * step + slot < patches)
    key_mask = jnp.where(valid, 0.0, -1e30).astype(f32).reshape(1, 4 * SLOT)
    key_mask = jnp.tile(key_mask, (1, 4))

    weight_scratch = [
        pltpu.VMEM((model, blocks * wide), bf16),
        pltpu.SemaphoreType.DMA((plan.n_loads(),)),
    ]
    p_shape = like((blocks, rows, 3 * head_cols))
    o_shape = like((blocks, rows, head_cols))
    log_shape = like((rows, 128), f32)
    full = like((rows, model), f32)
    unit = like((4, SLOT, model))

    p1, o1, log1, *branch = call(
        attention_forward(plan, False, head_cols, len(w_space)),
        by_patch + [gains[0:1], shifts[0:1], qv[0], key_mask, biases[0:2]] + w_space,
        len(w_space),
        [p_shape, o_shape, log_shape] + [unit] * 4,
        0,
        weight_scratch,
        "space_forward",
        20,
        wait=(0, 1, 2),
    )
    if paired:
        x2, y2, l3, branch = after((x2, y2, l3, branch))
        a3, x3, y3 = sides(jnp.stack(l3), 3)
    with jax.named_scope("branch_z"):
        branch = swap_z_back(branch)
    if paired:
        x3, y3, branch = after((x3, y3, branch))
        with jax.named_scope("corner2"):
            c2 = flip_x(after(y2, x3))
    with jax.named_scope("branch_ctx"):
        near, beside, beyond = to_ctx(branch)
        far = flip_y(beyond)
    if paired:
        core1 = cores(after([a1, x1, y1, c1], far), 1)
        with jax.named_scope("corner3"):
            c3 = [flip_x(y3[:1]), flip_y(after(x3[1:], far))]
        w_time = [a1, x1, y1, c1] + core1
    with jax.named_scope("branch_ctx"):
        branch = [near, flip_core(beside), far, flip_core(far)]

    p2, o2, log2, mid, stream, pair = call(
        attention_forward(plan, True, head_cols, len(w_time)),
        frames
        + branch
        + [gains[1:2], shifts[1:2], qv[1], key_mask, biases[0:2], gains[2:3], shifts[2:3]]
        + w_time,
        len(w_time),
        [p_shape, o_shape, log_shape, full, full, like((2, rows, model))],
        0,
        weight_scratch,
        "time_forward",
        20,
        wait=(0, 1, 2, 3, 4),
    )
    pairs = [pair]
    if paired:
        pair, c2, c3[1] = after((pair, c2, c3[1]))
        w_first, w_second = [a2, x2, y2, c2], [a3, x3, y3, *c3]
        pairs = [pair]
        with jax.named_scope("pair_core"):
            pairs.append(flip_core(pair))

    groups = len(pairs)
    hidden_whole = pltpu.VMEM((model, 2 * plan.hidden), bf16)
    hidden_scratch = [hidden_whole, hidden_whole, pltpu.SemaphoreType.DMA((16,))]
    hidden_scratch += plan.hidden_grad_scratch()
    hidden_grads = plan.hidden_grad_shapes()
    n_g = len(hidden_grads)
    up_shape = like((blocks, 1, wide), f32)
    got = call(
        mlp(plan, (0, 2), len(w_first), groups, rows, True),
        pairs + [up_b] + w_first,
        len(w_first),
        hidden_grads + [full] * (2 * groups) + [up_shape],
        n_g,
        hidden_scratch,
        "mlp_first",
        26,
    )
    first_grads, partial = got[:n_g], got[n_g:]
    got = call(
        mlp(plan, (1, 3), len(w_second), groups, rows, False),
        pairs + [up_b] + partial + w_second,
        len(w_second),
        hidden_grads + ([full] + [like((rows, model))] * (groups - 1)) * 2 + [up_shape],
        n_g,
        hidden_scratch,
        "mlp_second",
        26,
    )
    second_grads, results, backs, up_sums = got[:n_g], got[n_g : n_g + groups], got[n_g + groups : -1], got[-1]
    if paired:
        with jax.named_scope("hidden_side"):
            first_moved = [flip_y(first_grads[1]), flip_x(first_grads[3])]
            second_moved = [flip_y(second_grads[1]), flip_x(second_grads[3])]
        with jax.named_scope("back_core"):
            backs = [backs[0], flip_core(backs[1])]

    grads = plan.grad_shapes()
    n_g = len(grads)
    vec_shape = like((24, model), f32)
    qv_held = pltpu.VMEM((blocks, 1, 3 * head_cols), f32)
    d_time, time_vec, time_g, *g1 = call(
        time_backward(plan, head_cols, len(w_time), groups),
        [mid, stream, pair] + backs + [gains[2:3], gains[1:2], log2, p2] + w_time,
        len(w_time),
        [p_shape, vec_shape, like((rows, model))] + [unit] * 2 + [like((2,) + unit.shape)],
        0,
        weight_scratch + [qv_held],
        "time_backward",
        20,
    )
    if paired:
        g1, first_moved = after((g1, first_moved))
    with jax.named_scope("g1_ctx"):
        far = flip_y(g1[2])
    g_time = call(
        time_weights(plan),
        [mid, time_g, gains[1:2], shifts[1:2], d_time, o2],
        0,
        grads,
        n_g,
        plan.grad_scratch(),
        "time_weights",
        16,
    )
    if paired:
        g_time, far, second_moved = after((g_time, far, second_moved))
    with jax.named_scope("g1_ctx"):
        g1 = [g1[0], flip_core(g1[1]), far, flip_core(far)]
    with jax.named_scope("finished"):
        if paired:
            results = [results[0], flip_core(after(results[1], far))]

        def finish(*refs):
            total = refs[0][...] + refs[1][...] + refs[2][...]
            for ref in refs[3 : 2 + groups]:
                total = total + ref[...].astype(f32)
            put_ctx(refs[2 + groups :], nn(turn_rows(total.shape[0]), total.astype(bf16)))

        outs = [unit] * 2 + [like((2,) + unit.shape)]
        finished = call(finish, [biases[2:3], stream] + list(results), 0, outs, 0, [], "finish", 8)
    if paired:
        with jax.named_scope("time_core"):
            got_time = flip_core(g_time[1])
        pairs = [(first_grads[0], first_moved[0]), (second_grads[0], second_moved[0])]
        pairs += [(first_grads[2], first_moved[1]), (second_grads[2], second_moved[1])]
        hidden_rest_a, send_a, hidden_rest_b, send_b = hidden_after_side(pairs)
        with jax.named_scope("hidden_corner"):
            corner_a, corner_b = flip_x(send_a), flip_y(send_b)
    with jax.named_scope("g1_z"):
        g1 = swap_z_out(to_frames(g1))
    if paired:
        keep_ta, send_ta, keep_tb, send_tb = after_core(g_time[0], got_time)
        with jax.named_scope("time_side"):
            side_ta, side_tb = flip_y(after(send_ta, g1)), flip_x(after(send_tb, g1))
        hidden_own, *sends = hidden_after_corner(hidden_rest_a, corner_a, hidden_rest_b, corner_b)
        sends = after(sends, send_ta)
        with jax.named_scope("hidden_line"):
            hidden_moved = [shift_z(v, k) for v, k in zip(sends, (1, 2, 1, 2, 3))]

    got = call(
        space_weights(plan, head_cols, len(w_space)),
        by_patch + g1 + [gains[0:1], shifts[0:1], key_mask, log1, p1, o1] + w_space,
        len(w_space),
        grads + [p_shape],
        n_g,
        weight_scratch + plan.grad_scratch(),
        "space_weights",
        24,
        after=(sends[0], send_ta) if paired else (),
    )
    if paired:
        got, side_ta, side_tb, hidden_moved[:2] = after((got, side_ta, side_tb, hidden_moved[:2]))
    g_space, d_space = got[:n_g], got[n_g]
    vector, *back = call(
        space_backward(plan, head_cols, len(w_space)),
        by_patch + g1 + [time_vec, up_sums, gains[0:1], d_space] + w_space,
        len(w_space),
        [vec_shape] + [unit] * 4,
        0,
        weight_scratch + [qv_held],
        "space_backward",
        16,
    )

    if paired:
        with jax.named_scope("space_core"):
            got_space = flip_core(g_space[1])
        rest_ta, send_ta, rest_tb, send_tb = after_side((keep_ta, side_ta), (keep_tb, side_tb))
        with jax.named_scope("time_corner"):
            corner_ta, corner_tb = flip_x(send_ta), flip_y(send_tb)
        with jax.named_scope("vectors"):
            other = flip_core(vector)
        got_space, other, back, corner_ta, corner_tb, hidden_moved[4] = after(
            (got_space, other, back, corner_ta, corner_tb, hidden_moved[4])
        )

        keep_a, send_a, keep_b, send_b = after_core(g_space[0], got_space)
        with jax.named_scope("space_side"):
            side_a, side_b = flip_y(send_a), flip_x(send_b)
        own_time_sum, *sends = after_corner(rest_ta, corner_ta, rest_tb, corner_tb)
        with jax.named_scope("time_line"):
            time_moved = spread(sends)
        vector, *messages = pack(back[1:], vector, other)
        side_a, side_b, messages, time_moved[:2] = after((side_a, side_b, messages, time_moved[:2]))

        rest_a, send_a, rest_b, send_b = after_side((keep_a, side_a), (keep_b, side_b))
        with jax.named_scope("space_corner"):
            corner_a, corner_b = flip_x(send_a), flip_y(send_b)
        with jax.named_scope("token_grad"):
            moved = [shift_z(v, 4 - k) for k, v in zip((1, 2, 3), after(messages, send_a))]
        with jax.named_scope("finished"):
            far = flip_y(after(finished[2], send_a))
        qkv_time, proj_time = attention_total(own_time_sum, time_moved, head_cols, 2**15)
        corner_a, corner_b, moved, qkv_time, proj_time, far, hidden_moved[2] = after(
            (corner_a, corner_b, moved, qkv_time, proj_time, far, hidden_moved[2])
        )

        own, *sends = after_corner(rest_a, corner_a, rest_b, corner_b)
        with jax.named_scope("space_line"):
            space_moved = spread(sends)
        with jax.named_scope("finished"):
            finished = [finished[0], flip_core(after(finished[1], far)), far, flip_core(far)]
        token_grad, vector = unpack(back[0], vector, moved, patches)
        with jax.named_scope("vectors"):
            vector = vector + flip_y(vector)
            vector = own_vectors(mesh, vector, flip_x(vector))
        hidden_keep, hidden_send = hidden_total(hidden_own, hidden_moved)
        with jax.named_scope("hidden_core"):
            hidden_got = flip_core(hidden_send)
        grad_up, grad_down = hidden_join(hidden_keep, hidden_got)
        qkv_space, proj_space = attention_total(own, space_moved, head_cols, None)
    else:

        def summed(g):
            g = lax.psum_scatter(g.astype(f32), ("shard", "ctx"), scatter_dimension=1, tiled=True)
            return lax.psum_scatter(g, "tp", scatter_dimension=0, tiled=True)[0]

        def apart(total):
            three = total[:, : 3 * head_cols].reshape(-1, 3, head_cols)
            return jnp.swapaxes(three, 0, 1), total[:, 3 * head_cols :].T

        hidden_grad = jnp.concatenate([v[i : i + 1] for i in (0, 1) for v in (first_grads[0], second_grads[0])])
        grad_up, grad_down = summed(hidden_grad[:, :model]), summed(hidden_grad[:, model:])
        qkv_time, proj_time = apart(summed(g_time[0]))
        qkv_space, proj_space = apart(summed(g_space[0]))

    with jax.named_scope("finished"):
        if not paired:
            finished = swap_ctx(*finished)
        finished = bring_back(finished, False, patches, bf16)
    if not paired:
        token_grad = bring_back(swap_z_back(back), True, patches, f32)

    if not paired:
        vector = lax.psum(vector, ("shard", "ctx", "tp"))
        vector = own_vectors(mesh, vector, jnp.zeros_like(vector))
    gains, shifts, biases, qv, hidden = vector
    return (
        finished[None],
        token_grad[None],
        gains,
        shifts,
        qkv_space,
        proj_space,
        qkv_time,
        proj_time,
        grad_up,
        grad_down.T,
        biases,
        qv.reshape(2, 2, -1),
        hidden.reshape(-1),
    )


def solution(mesh):
    return jax.shard_map(
        functools.partial(on_device, mesh),
        mesh=mesh,
        in_specs=(
            P("shard", "ctx", "tp", None),
            P("shard", "ctx", "tp", None),
            P(None, "shard"),
            P(None, "shard"),
            P(None, "shard", "tp"),
            P("tp", "shard"),
            P(None, "shard", "tp"),
            P("tp", "shard"),
            P("shard", "tp"),
            P("tp", "shard"),
            P(None, "shard"),
            P(None, None, "shard"),
            P("shard"),
        ),
        out_specs=(
            P("shard", "ctx", "tp", None),
            P("shard", "ctx", "tp", None),
            P(None, ("shard", "ctx", "tp")),
            P(None, ("shard", "ctx", "tp")),
            P(None, ("shard", "ctx"), "tp"),
            P("tp", ("shard", "ctx")),
            P(None, ("shard", "ctx"), "tp"),
            P("tp", ("shard", "ctx")),
            P(("shard", "ctx"), "tp"),
            P("tp", ("shard", "ctx")),
            P(None, ("shard", "ctx", "tp")),
            P(None, None, ("shard", "ctx", "tp")),
            P(("shard", "ctx", "tp")),
        ),
        check_vma=False,
    )
```

```python
import functools

import jax
import jax.numpy as jnp
from jax import lax
from jax.experimental import pallas as pl
from jax.experimental.pallas import tpu as pltpu
from jax.sharding import PartitionSpec as P

HD = 64
EPS = 1e-06
SCALE = HD ** (-0.5)
SLOT = 16
bf16 = jnp.bfloat16
f32 = jnp.float32
VMEM = pl.BlockSpec(memory_space=pltpu.VMEM)
ANY = pl.BlockSpec(memory_space=pl.ANY)


def nn(a, b):
    return lax.dot_general(a, b, (((1,), (0,)), ((), ())), preferred_element_type=f32)


def nt(a, b):
    return lax.dot_general(a, b, (((1,), (1,)), ((), ())), preferred_element_type=f32)


def tn(a, b):
    return lax.dot_general(a, b, (((0,), (0,)), ((), ())), preferred_element_type=f32)


def turned(a):
    return a.astype(f32).T.astype(bf16)


def row_sum(v):
    return jnp.sum(v.astype(f32), axis=0, keepdims=True)


def standardize(v):
    c = v - jnp.mean(v, axis=-1, keepdims=True)
    r = lax.rsqrt(jnp.mean(c * c, axis=-1, keepdims=True) + EPS)
    return c * r, r


def norm_back(d, q, r, gain):
    e = d * gain
    return r * (e - jnp.mean(e, axis=-1, keepdims=True) - q * jnp.mean(e * q, axis=-1, keepdims=True))


def rows_of(parts):
    return jnp.concatenate([v[...].reshape(-1, v.shape[-1]) for v in parts], axis=0)


def put_rows(refs, value):
    n = value.shape[0] // len(refs)
    for i, r in enumerate(refs):
        r[...] = value[i * n : (i + 1) * n].reshape(r.shape).astype(r.dtype)


def put_ctx(refs, value):
    n = value.shape[0] // 4
    for i, to in enumerate((refs[0], refs[1], refs[2].at[0], refs[2].at[1])):
        to[...] = value[i * n : (i + 1) * n].reshape(to.shape).astype(to.dtype)


def like(shape, dtype=bf16):
    return jax.ShapeDtypeStruct(shape, dtype)


class Take:
    def __init__(self, refs):
        self.refs = list(refs)

    def __call__(self, n):
        got, self.refs = self.refs[:n], self.refs[n:]
        return got


def flip_x(v):
    return lax.ppermute(v, "shard", [(i, i ^ 1) for i in range(2)])


def flip_ctx(v, e):
    return lax.ppermute(v, "ctx", [(i, i ^ e) for i in range(4)])


def flip_core(v):
    return flip_ctx(v, 1)


def flip_y(v):
    return flip_ctx(v, 2)


def shift_z(v, k):
    return lax.ppermute(v, "tp", [(i, (i + k) % 4) for i in range(4)])


def swap_z_out(parts):
    return [parts[0]] + [shift_z(parts[k], k) for k in (1, 2, 3)]


def swap_z_back(parts):
    return [parts[0]] + [shift_z(parts[k], 4 - k) for k in (1, 2, 3)]


def swap_ctx(p0, p1, pair):
    far = flip_y(pair)
    return [p0, flip_core(p1), far, flip_core(far)]


def ctx_parts(refs):
    return [refs[0][...], refs[1][...], refs[2][0], refs[3][1]]


def after(value, *others):
    return lax.optimization_barrier((value, others))[0]


class Plan:
    def __init__(self, mesh, model, wide):
        self.sizes = (mesh.shape["shard"], mesh.shape["ctx"], mesh.shape["tp"])
        self.paired = self.sizes == (2, 4, 4)
        self.model, self.wide, self.blocks = model, wide, self.sizes[2]
        self.hidden = wide // 2 if self.paired else wide

    def ranks(self):
        q = lax.axis_index("ctx")
        return lax.axis_index("shard"), q >> 1, q & 1, lax.axis_index("tp")

    def block(self, r):
        if not self.paired:
            return r
        return lax.rem(lax.axis_index("tp") + r, self.blocks)

    def places(self):
        if not self.paired:
            return [(0, 0, 0, self.model, 0)]
        x, y, c, _ = self.ranks()
        rows = self.model // 8
        every = range(4)
        kinds = [(0, 0, every), (1, 0, every), (0, 1, every), (1, 1, every)]
        out = []
        for core in (0, 1):
            for i, (dx, dy, ks) in enumerate(kinds):
                row = (((x ^ dx) * 2 + (y ^ dy)) * 2 + (c ^ core)) * rows
                for n, k in enumerate(ks):
                    out.append((core * 4 + i, n, pl.multiple_of(row, rows), rows, (4 - k) % 4))
        return out

    def n_loads(self):
        return 32 if self.paired else 1

    def start_loads(self, refs, whole, sems):
        by_slot = [[] for _ in range(self.blocks)]
        for n, (i, k, row, rows, slot) in enumerate(self.places()):
            to = whole.at[pl.ds(row, rows), pl.ds(slot * self.wide, refs[i].shape[-1])]
            by_slot[slot].append(pltpu.make_async_copy(refs[i].at[k], to, sems.at[n]))
        for copies in by_slot:
            for copy in copies:
                copy.start()
        return by_slot

    def start_hidden_loads(self, refs, slots, up, down, sems):
        by_slot = [[], []]
        if self.paired:
            x, y, _, _ = self.ranks()
            rows = self.model // 4
            kinds = [(0, 0, (0, 1)), (1, 0, (0, 1)), (0, 1, (0, 1))]
            kinds += [(1, 1, (0, 1))] if len(refs) == 4 else [(1, 1, (0,)), (1, 1, (1,))]
            places = []
            for ref, (dx, dy, ks) in zip(refs, kinds):
                row = pl.multiple_of(((x ^ dx) * 2 + (y ^ dy)) * rows, rows)
                places += [(ref.at[n], row, k) for n, k in enumerate(ks)]
        else:
            rows = self.model
            places = [(refs[0].at[r], 0, i) for i, r in enumerate(slots)]
        for n, (source, row, i) in enumerate(places):
            for part, whole in enumerate((up, down)):
                to = whole.at[pl.ds(row, rows), pl.ds(i * self.hidden, self.hidden)]
                copy = pltpu.make_async_copy(source.at[part * rows : (part + 1) * rows], to, sems.at[2 * n + part])
                by_slot[i].append(copy)
        for copies in by_slot:
            for copy in copies:
                copy.start()
        return by_slot

    def grad_shapes(self):
        if self.paired:
            return [like((2, 2, 4, self.model // 8, self.wide))] * 2
        return [like((self.blocks, self.model, self.wide))]

    def grad_scratch(self):
        if self.paired:
            held = pltpu.VMEM((4, 2, 2, 2, self.model // 8, self.wide), bf16)
            return [held, pltpu.SemaphoreType.DMA((8,))]
        return [
            pltpu.VMEM((self.blocks, self.model, self.wide), bf16),
            pltpu.SemaphoreType.DMA((self.blocks,)),
        ]

    def hold(self, r, value, held):
        value = value.astype(bf16)
        if not self.paired:
            held[r] = value
            return
        x, y, c, _ = self.ranks()
        rows = self.model // 8
        for i in range(8):
            held[r, (i & 1) ^ c, ((i >> 1) & 1) ^ y, (i >> 2) ^ x] = value[i * rows : (i + 1) * rows]

    def store(self, held, outs, sems):
        copies = []
        for r in range(self.blocks):
            if not self.paired:
                copies.append(pltpu.make_async_copy(held.at[r], outs[0].at[r], sems.at[r]))
                continue
            for core in (1, 0):
                to = outs[core].at[:, :, r]
                copies.append(pltpu.make_async_copy(held.at[r, core], to, sems.at[2 * r + core]))
        for copy in copies:
            copy.start()
        for copy in copies:
            copy.wait()

    def hidden_grad_shapes(self):
        if self.paired:
            return [like((2, self.model // 2, self.hidden))] * 4
        return [like((2, 2 * self.model, self.hidden))]

    def hidden_grad_scratch(self):
        if self.paired:
            held = pltpu.VMEM((2, 2, 2, self.model // 2, self.hidden), bf16)
            return [held, pltpu.SemaphoreType.DMA((4,))]
        return [pltpu.VMEM((2, 2 * self.model, self.hidden), bf16), pltpu.SemaphoreType.DMA((2,))]

    def put_hidden(self, i, part, value, held):
        value = value.astype(bf16)
        if not self.paired:
            held[i, part * self.model : (part + 1) * self.model] = value
            return
        x, y, _, _ = self.ranks()
        rows = self.model // 4
        for n in range(4):
            to = held.at[i, (n & 1) ^ y, (n >> 1) ^ x]
            to[part * rows : (part + 1) * rows] = value[n * rows : (n + 1) * rows]

    def start_hidden(self, i, held, outs, sems):
        if not self.paired:
            copies = [pltpu.make_async_copy(held.at[i], outs[0].at[i], sems.at[i])]
        else:
            copies = []
            for side in (0, 1):
                source = held.at[i, side] if i == 0 else held.at[i, :, side]
                copies.append(pltpu.make_async_copy(source, outs[2 * i + side], sems.at[2 * i + side]))
        for copy in copies:
            copy.start()
        return copies


def call(kernel, ins, n_any, outs, n_any_out, scratch, name, limit, after=(), far=None, wait=()):
    n_in, n_after = len(ins), len(after)

    def run(*refs):
        kernel(*refs[:n_in], *refs[n_in + n_after :])

    ins = list(ins)
    for i, v in enumerate(ins):
        if i >= n_in - n_any or (far is not None and v.size >= far):
            ins[i] = pltpu.with_memory_space_constraint(v, pltpu.HBM)
    outs = [pltpu.HBM(v.shape, v.dtype) if i in wait else v for i, v in enumerate(outs)]
    got = pl.pallas_call(
        run,
        out_shape=outs,
        in_specs=[VMEM] * (n_in - n_any) + [ANY] * (n_any + n_after),
        out_specs=[ANY] * n_any_out + [VMEM] * (len(outs) - n_any_out),
        scratch_shapes=scratch,
        compiler_params=pltpu.CompilerParams(vmem_limit_bytes=limit * 2**20),
        name=name,
    )(*ins, *after)
    return list(got)


def add(u, v):
    return (u.astype(f32) + v.astype(f32)).astype(bf16)


def after_core(keep, got):
    rows, wide = keep.shape[-2:]
    cut = 3

    def kernel(k, g, keep_a, send_a, keep_b, send_b):
        for x in (0, 1):
            keep_a[x] = add(k[0, x, :2], g[0, x, :2])
            send_a[x] = add(k[1, x, :2], g[1, x, :2])
        for y in (0, 1):
            keep_b[y] = add(k[y, 0, 2:], g[y, 0, 2:])
            send_b[y] = add(k[y, 1, 2:], g[y, 1, 2:])

    whole = pl.BlockSpec((2, 2, 4, rows // cut, wide), lambda i: (0, 0, 0, i, 0))
    half = pl.BlockSpec((2, 2, rows // cut, wide), lambda i: (0, 0, i, 0))
    return pl.pallas_call(
        kernel,
        grid=(cut,),
        out_shape=[like((2, 2, rows, wide))] * 4,
        in_specs=[whole] * 2,
        out_specs=[half] * 4,
        compiler_params=pltpu.CompilerParams(vmem_limit_bytes=16 * 2**20),
        name="after_core",
    )(keep, got)


def after_side(*pairs):
    def kernel(*refs):
        n = len(pairs)
        for i in range(n):
            k, g = refs[2 * i], refs[2 * i + 1]
            refs[2 * n + 2 * i][...] = add(k[0], g[0])
            refs[2 * n + 2 * i + 1][...] = add(k[1], g[1])

    ins = [v for pair in pairs for v in pair]
    outs = [like(v.shape[1:]) for v in ins]
    return call(kernel, ins, 0, outs, 0, [], "after_side", 24)


def hidden_after_side(pairs):
    def kernel(*refs):
        for i in range(4):
            k, g = refs[2 * i], refs[2 * i + 1]
            rest, send = refs[8 + 2 * (i // 2)], refs[9 + 2 * (i // 2)]
            rest[i % 2] = add(k[0], g[0])
            send[i % 2] = add(k[1], g[1])

    ins = [v for pair in pairs for v in pair]
    return call(kernel, ins, 0, [like(ins[0].shape)] * 4, 0, [], "hidden_after_side", 24)


def after_corner(rest_a, got_a, rest_b, got_b):
    def kernel(ra, ga, rb, gb, own, *sends):
        own[...] = ra[0].astype(f32) + ga[0].astype(f32)
        sends[0][...] = add(ra[1], ga[1])
        sends[1][...] = add(rb[0], gb[0])
        sends[2][...] = add(rb[1], gb[1])

    shape = rest_a.shape[1:]
    outs = [like(shape, f32)] + [like(shape)] * 3
    return call(kernel, [rest_a, got_a, rest_b, got_b], 0, outs, 0, [], "after_corner", 12)


def hidden_after_corner(rest_a, got_a, rest_b, got_b):
    rows = rest_a.shape[1] // 2

    def kernel(ra, ga, rb, gb, own, *sends):
        own[...] = ra[0].astype(f32) + ga[0].astype(f32)
        for part in (0, 1):
            at = slice(part * rows, (part + 1) * rows)
            sends[2 * part][...] = add(ra[1, at], ga[1, at])
            sends[2 * part + 1][...] = add(rb[0, at], gb[0, at])
        sends[4][...] = add(rb[1], gb[1])

    shape = rest_a.shape[1:]
    half = (rows,) + shape[1:]
    outs = [like(shape, f32)] + [like(half)] * 4 + [like(shape)]
    return call(kernel, [rest_a, got_a, rest_b, got_b], 0, outs, 0, [], "hidden_after_corner", 12)


def spread(sends):
    return [shift_z(v, k) for k, v in zip((1, 2, 3), sends)]


def attention_total(own, moved, head_cols, far):
    rows = own.shape[0]
    three = 3 * head_cols

    def kernel(o, a, b, c, qkv, proj):
        total = o[...] + a[...].astype(f32) + b[...].astype(f32) + c[...].astype(f32)
        for t in range(3):
            qkv[t] = total[:, t * head_cols : (t + 1) * head_cols]
        proj[...] = total[:, three:].T

    outs = [like((3, rows, head_cols), f32), like((head_cols, rows), f32)]
    return call(kernel, [own] + moved, 0, outs, 0, [], "attention_total", 8, far=far)


def hidden_total(own, moved):
    rows, wide = own.shape[0] // 4, own.shape[1]

    def kernel(o, up_1, up_2, down_1, down_2, both, keep, send):
        core = lax.axis_index("ctx") & 1
        for part, pair in enumerate(((up_1, up_2), (down_1, down_2))):
            for half in (0, 1):
                at = slice(half * rows, (half + 1) * rows)
                of = slice((2 * part + half) * rows, (2 * part + half + 1) * rows)
                total = o[of] + both[of].astype(f32) + pair[0][at].astype(f32) + pair[1][at].astype(f32)

                @pl.when(core == half)
                def _(total=total, part=part):
                    keep[part] = total

                @pl.when(core != half)
                def _(total=total, part=part):
                    send[part] = total.astype(bf16)

    outs = [like((2, rows, wide), f32), like((2, rows, wide))]
    return call(kernel, [own] + moved, 0, outs, 0, [], "hidden_total", 8)


def hidden_join(keep, got):
    rows, wide = keep.shape[1:]

    def kernel(k, g, up, down):
        core = lax.axis_index("ctx") & 1
        here, there = pl.multiple_of(core * wide, wide), pl.multiple_of((1 - core) * wide, wide)
        for part, out in enumerate((up, down)):
            out[:, pl.ds(here, wide)] = k[part]
            out[:, pl.ds(there, wide)] = g[part].astype(f32)

    return call(kernel, [keep, got], 0, [like((rows, 2 * wide), f32)] * 2, 0, [], "hidden_join", 8)


def lay_out(x, c):
    frames, patches, width = x.shape
    step = -(-patches // 4)

    def kernel(x_ref, c_ref, *refs):
        by_patch, by_frame, held = refs[:4], refs[4:7], refs[7]
        z, q = lax.axis_index("tp"), lax.axis_index("ctx")
        for i, ref in enumerate((x_ref, c_ref)):
            for f in range(4):
                v = ref[f].astype(f32)
                for b in range(4):
                    part = v[b * step : min((b + 1) * step, patches)]
                    pad = jnp.zeros((SLOT - part.shape[0], width), f32)
                    held[i, f, b] = jnp.concatenate([part, pad], axis=0).astype(bf16)
        for s in range(4):
            f = lax.rem(z + s, 4)
            for e in range(4):
                by_patch[s][e * SLOT : (e + 1) * SLOT] = held[0, f, q ^ e]
                to = by_frame[e] if e < 2 else by_frame[2].at[e - 2]
                to[0, s] = held[0, f, q ^ e]
                to[1, s] = held[1, f, q ^ e]

    both = (2, 4, SLOT, width)
    outs = [like((4 * SLOT, width))] * 4 + [like(both)] * 2 + [like((2,) + both)]
    got = call(kernel, [x, c], 0, outs, 0, [pltpu.VMEM((2, 4, 4, SLOT, width), bf16)], "lay_out", 8)
    return got[:4], got[4:]


def put_tokens(values, frames_first, held, out):
    z, q = lax.axis_index("tp"), lax.axis_index("ctx")
    patches, width = out.shape[0], out.shape[-1]
    step = -(-patches // 4)
    for i, v in enumerate(values):
        v = v.reshape(4, SLOT, width).astype(f32)
        if frames_first:
            held[i] = v
        else:
            held[:, i] = v
    for f in range(4):
        s = lax.rem(f + 4 - z, 4)
        rows = [held[s, b ^ q][: min(step, patches - b * step)] for b in range(4)]
        out[:, f] = jnp.concatenate(rows, axis=0).astype(out.dtype)


def bring_back(parts, frames_first, patches, dtype):
    width = parts[0].shape[-1]

    def kernel(*refs):
        ins, out, held = refs[:4], refs[4], refs[5]
        put_tokens([r[...] for r in ins] if frames_first else ctx_parts(ins), frames_first, held, out)

    scratch = [pltpu.VMEM((4, 4, SLOT, width), f32)]
    got = call(kernel, parts, 0, [like((patches, 4, width), dtype)], 0, scratch, "bring_back", 8)
    return jnp.swapaxes(got[0], 0, 1)


def pack(parts, vector, other):
    rows, width = 4 * SLOT, parts[0].shape[-1]
    extra = vector.shape[0]

    def kernel(a, b, c, vec, far, total, *outs):
        v = vec[...] + far[...]
        total[...] = v
        high = v.astype(bf16)
        low = (v - high.astype(f32)).astype(bf16)
        below = jnp.concatenate([high.astype(f32), low.astype(f32)], axis=0).astype(bf16)
        for part, out in zip((a, b, c), outs):
            out[:rows] = part[...].reshape(rows, width)
            out[rows:] = below

    outs = [like(vector.shape, f32)] + [like((rows + 2 * extra, width))] * 3
    return call(kernel, parts + [vector, other], 0, outs, 0, [], "pack", 8)


def own_vectors(mesh, vector, other):
    blocks, model = mesh.shape["tp"], vector.shape[-1]
    many = mesh.size
    size, hidden = model // many, 4 * model // many

    def kernel(vec, far, gains, shifts, biases, qv, up):
        place = (lax.axis_index("shard") * mesh.shape["ctx"] + lax.axis_index("ctx")) * blocks + lax.axis_index("tp")
        total = vec[...] + far[...]
        mine = pltpu.roll(total, lax.rem(model - place * size, model), 1)[:, :size]
        gains[...] = mine[0:3]
        shifts[...] = mine[3:6]
        biases[...] = mine[6:9]
        qv[...] = mine[9:13]
        at = place * hidden
        for row in range(4):

            @pl.when(lax.div(at, model) == row)
            def _(row=row):
                here = total[13 + row : 14 + row]
                up[...] = pltpu.roll(here, lax.rem(model - lax.rem(at, model), model), 1)[:, :hidden]

    outs = [like((3, size), f32)] * 3 + [like((4, size), f32), like((1, hidden), f32)]
    return call(kernel, [vector, other], 0, outs, 0, [], "own_vectors", 4)


def unpack(own, vector, moved, patches):
    rows, width = 4 * SLOT, own.shape[-1]
    extra = vector.shape[0]

    def kernel(*refs):
        own_ref, vec, ins = refs[0], refs[1], refs[2:5]
        out, total, held = refs[5:]
        put_tokens([own_ref[...]] + [r[:rows] for r in ins], True, held, out)
        v = vec[...]
        for r in ins:
            below = r[rows:].astype(f32)
            v = v + (below[:extra] + below[extra:])
        total[...] = v

    scratch = [pltpu.VMEM((4, 4, SLOT, width), f32)]
    outs = [like((patches, 4, width), f32), like(vector.shape, f32)]
    token_grad, total = call(kernel, [own, vector] + moved, 0, outs, 0, scratch, "unpack", 8, far=2**15)
    return jnp.swapaxes(token_grad, 0, 1), total


def to_ctx(parts):
    def kernel(*refs):
        for s in range(4):
            for e in range(4):
                to = refs[4 + e] if e < 2 else refs[6].at[e - 2]
                to[s] = refs[s][e]

    shape = parts[0].shape
    return call(kernel, parts, 0, [like(shape)] * 2 + [like((2,) + shape)], 0, [], "to_ctx", 4)


def to_frames(parts):
    def kernel(*refs):
        for e, v in enumerate(ctx_parts(refs[:4])):
            for s in range(4):
                refs[4 + s][e] = v[s]

    return call(kernel, parts, 0, [like(parts[0].shape)] * 4, 0, [], "to_frames", 4)


def turn_rows(rows):
    a = lax.broadcasted_iota(jnp.int32, (rows, rows), 0)
    b = lax.broadcasted_iota(jnp.int32, (rows, rows), 1)
    bits = SLOT.bit_length() - 1
    return jnp.where(b == ((a & (SLOT - 1)) << bits) + (a >> bits), 1.0, 0.0).astype(bf16)


def masks_of(timed, rows, mask_ref):
    if not timed:
        return [slice(0, rows)], mask_ref[...]
    half = rows // 2
    a = lax.broadcasted_iota(jnp.int32, (half, half), 0)
    b = lax.broadcasted_iota(jnp.int32, (half, half), 1)
    return [slice(0, half), slice(half, rows)], jnp.where((a ^ b) < SLOT, 0.0, -1e30).astype(f32)


def head_slices(p, h, head_cols):
    return [p[:, t * head_cols + h * HD : t * head_cols + (h + 1) * HD] for t in range(3)]


def attention_forward(plan, timed, head_cols, n_w):
    heads = head_cols // HD
    three = 3 * head_cols

    def kernel(*refs):
        take = Take(refs)
        x_refs = take(4)
        b_refs = take(4) if timed else []
        gain, shift, qv, mask_ref, bias_in = take(5)
        next_norm = take(2) if timed else []
        w_refs = take(n_w)
        p_ref, o_ref, log_ref = take(3)
        outs = take(3) if timed else take(4)
        whole, sems = take(2)
        loads = plan.start_loads(w_refs, whole, sems)
        if timed:
            parts = ctx_parts(x_refs)
            swap = turn_rows(log_ref.shape[0])
            x = nn(swap, rows_of([v[0] for v in parts]))
            x = x + nn(swap, rows_of(ctx_parts(b_refs))) + bias_in[0:1]
            outs[0][...] = x
            outs[2][1] = nn(swap, rows_of([v[1] for v in parts])).astype(bf16)
        else:
            x = rows_of(x_refs).astype(f32)
        ranges, mask = masks_of(timed, x.shape[0], mask_ref)
        q, _ = standardize(x)
        n = (q * gain[...] + shift[...]).astype(bf16)
        total = jnp.zeros(x.shape, f32)
        scale = jnp.where(lax.broadcasted_iota(jnp.int32, (1, three), 1) < head_cols, SCALE, 1.0).astype(f32)
        rows = x.shape[0]
        for r in range(plan.blocks):
            at = r * plan.wide
            for copy in loads[r]:
                copy.wait()
            p = ((nn(n, whole[:, at : at + three]) + qv[plan.block(r)]) * scale).astype(bf16)
            p_ref[r] = p
            cells = [[v[m] for v in head_slices(p, h, head_cols)] for h in range(heads) for m in ranges]
            s = jnp.concatenate([nt(qh, kh) + mask for qh, kh, _ in cells], axis=0)
            top = jnp.max(s, axis=-1, keepdims=True)
            e = jnp.exp(s - top)
            total_e = jnp.sum(e, axis=-1, keepdims=True)
            log = top + jnp.log(total_e)
            w = (e / total_e).astype(bf16)
            size = mask.shape[-1]
            o = [nn(w[i * size : (i + 1) * size], vh) for i, (_, _, vh) in enumerate(cells)]
            for h in range(heads):
                log_ref[:, r * heads + h : r * heads + h + 1] = log[h * rows : (h + 1) * rows]
            n_m = len(ranges)
            o = jnp.concatenate(
                [jnp.concatenate(o[h * n_m : (h + 1) * n_m], axis=0) for h in range(heads)], axis=-1
            ).astype(bf16)
            o_ref[r] = o
            total = total + nt(o, whole[:, at + three : at + plan.wide])
        if timed:
            x = x + total + bias_in[1:2]
            outs[1][...] = x
            q, _ = standardize(x)
            outs[2][0] = (q * next_norm[0][...] + next_norm[1][...]).astype(bf16)
        else:
            put_rows(outs, total)

    return kernel


def heads_backward(p, d_o, log, ranges, mask, head_cols):
    heads, n_m, size = head_cols // HD, len(ranges), mask.shape[-1]
    cells = []
    for h in range(heads):
        parts = head_slices(p, h, head_cols) + [d_o[:, h * HD : (h + 1) * HD], log[:, h : h + 1]]
        cells += [[v[m] for v in parts] for m in ranges]
    s = jnp.concatenate([nt(qh, kh) + (mask - lh) for qh, kh, _, _, lh in cells], axis=0)
    d_w = jnp.concatenate([nt(doh, vh) for _, _, vh, doh, _ in cells], axis=0)
    w = jnp.exp(s)
    d_s = (w * (d_w - jnp.sum(d_w * w, axis=-1, keepdims=True))).astype(bf16)
    w = w.astype(bf16)
    at = [slice(i * size, (i + 1) * size) for i in range(len(cells))]
    d_q = [nn(d_s[m], cell[1]) * SCALE for m, cell in zip(at, cells)]
    d_k = [tn(d_s[m], cell[0]) for m, cell in zip(at, cells)]
    d_v = [tn(w[m], cell[3]) for m, cell in zip(at, cells)]
    columns = [jnp.concatenate(v[h * n_m : (h + 1) * n_m], axis=0) for v in (d_q, d_k, d_v) for h in range(heads)]
    return jnp.concatenate(columns, axis=-1).astype(bf16)


def put_qv(vec, layer, qv_held, head_cols):
    for i, t in enumerate((0, 2)):
        row = [qv_held[j][:, t * head_cols : (t + 1) * head_cols] for j in range(qv_held.shape[0])]
        vec[9 + 2 * layer + i : 10 + 2 * layer + i] = jnp.concatenate(row, axis=-1)


def time_backward(plan, head_cols, n_w, n_back):
    heads = head_cols // HD
    three = 3 * head_cols

    def kernel(*refs):
        take = Take(refs)
        x_ref, next_x, pair = take(3)
        back_refs = take(n_back)
        next_gain, gain, log_ref = take(3)
        (p_ref,) = take(1)
        w_refs = take(n_w)
        d_ref, vec, g_out = take(3)
        outs = take(3)
        whole, sems, qv_held = take(3)
        loads = plan.start_loads(w_refs, whole, sems)
        vec[...] = jnp.zeros(vec.shape, f32)
        x = x_ref[...]
        rows = x.shape[0]
        ranges, mask = masks_of(True, rows, None)
        g = pair[1].astype(f32)
        q3, r3 = standardize(next_x[...])
        d = back_refs[0][...].astype(f32)
        for ref in back_refs[1:]:
            d = d + ref[...].astype(f32)
        vec[2:3] = row_sum(d * q3)
        vec[5:6] = row_sum(d)
        vec[8:9] = row_sum(g)
        g = g + norm_back(d, q3, r3, next_gain[...])
        g_b = g.astype(bf16)
        g_out[...] = g_b
        vec[7:8] = row_sum(g_b)
        q, r_x = standardize(x)
        d_n = jnp.zeros(x.shape, f32)
        for r in range(plan.blocks):
            at = r * plan.wide
            for copy in loads[r]:
                copy.wait()
            d_o = nn(g_b, whole[:, at + three : at + plan.wide]).astype(bf16)
            log = log_ref[:, r * heads : (r + 1) * heads]
            d_p = heads_backward(p_ref[r], d_o, log, ranges, mask, head_cols)
            d_ref[r] = d_p
            qv_held[plan.block(r)] = row_sum(d_p)
            d_n = d_n + nt(d_p, whole[:, at : at + three])
        vec[1:2] = row_sum(d_n * q)
        vec[4:5] = row_sum(d_n)
        put_qv(vec, 1, qv_held, head_cols)
        g = g + norm_back(d_n, q, r_x, gain[...])
        put_ctx(outs, nn(turn_rows(rows), g.astype(bf16)))

    return kernel


def time_weights(plan):
    def kernel(*refs):
        take = Take(refs)
        x_ref, g_ref, gain, shift = take(4)
        d_ref, o_ref = take(2)
        grads = take(len(plan.grad_shapes()))
        held, out_sems = take(2)
        q, _ = standardize(x_ref[...])
        n_t = (q * gain[...] + shift[...]).T.astype(bf16)
        g_t = turned(g_ref[...])
        for r in range(plan.blocks):
            block = jnp.concatenate([nn(n_t, d_ref[r]), nn(g_t, o_ref[r])], axis=-1)
            plan.hold(r, block, held)
        plan.store(held, grads, out_sems)

    return kernel


def space_weights(plan, head_cols, n_w):
    heads = head_cols // HD
    three = 3 * head_cols

    def kernel(*refs):
        take = Take(refs)
        x_refs, g_refs = take(4), take(4)
        gain, shift, mask_ref, log_ref = take(4)
        p_ref, o_ref = take(2)
        w_refs = take(n_w)
        grads = take(len(plan.grad_shapes()))
        (d_ref,) = take(1)
        whole, sems, held, out_sems = take(4)
        loads = plan.start_loads(w_refs, whole, sems)
        x = rows_of(x_refs).astype(f32)
        g_b = rows_of(g_refs)
        g_t = turned(g_b)
        ranges, mask = masks_of(False, x.shape[0], mask_ref)
        q, _ = standardize(x)
        n_t = (q * gain[...] + shift[...]).T.astype(bf16)
        for r in range(plan.blocks):
            at = r * plan.wide
            for copy in loads[r]:
                copy.wait()
            d_o = nn(g_b, whole[:, at + three : at + plan.wide]).astype(bf16)
            log = log_ref[:, r * heads : (r + 1) * heads]
            d_p = heads_backward(p_ref[r], d_o, log, ranges, mask, head_cols)
            d_ref[r] = d_p
            block = jnp.concatenate([nn(n_t, d_p), nn(g_t, o_ref[r])], axis=-1)
            plan.hold(r, block, held)
        plan.store(held, grads, out_sems)

    return kernel


def space_backward(plan, head_cols, n_w):
    three = 3 * head_cols

    def kernel(*refs):
        take = Take(refs)
        x_refs, g_refs = take(4), take(4)
        time_vec, up_sums, gain = take(3)
        (d_ref,) = take(1)
        w_refs = take(n_w)
        (vec,) = take(1)
        outs = take(4)
        whole, sems, qv_held = take(3)
        loads = plan.start_loads(w_refs, whole, sems)
        x, g = rows_of(x_refs).astype(f32), rows_of(g_refs).astype(f32)
        vec[...] = time_vec[...]
        for j in range(up_sums.shape[0]):
            vec[13 + j : 14 + j] = up_sums[j]
        vec[6:7] = row_sum(g)
        q, r_x = standardize(x)
        d_n = jnp.zeros(x.shape, f32)
        for r in range(plan.blocks):
            at = r * plan.wide
            for copy in loads[r]:
                copy.wait()
            d_p = d_ref[r]
            qv_held[plan.block(r)] = row_sum(d_p)
            d_n = d_n + nt(d_p, whole[:, at : at + three])
        vec[0:1] = row_sum(d_n * q)
        vec[3:4] = row_sum(d_n)
        put_qv(vec, 0, qv_held, head_cols)
        put_rows(outs, g + norm_back(d_n, q, r_x, gain[...]))

    return kernel


def mlp(plan, slots, n_w, groups, rows, first):
    def kernel(*refs):
        take = Take(refs)
        pairs = take(groups)
        (up_bias,) = take(1)
        before = [] if first else take(2 * groups + 1)
        w_refs = take(n_w)
        grads = take(len(plan.hidden_grad_shapes()))
        outs = take(groups)
        backs = take(groups)
        (up_sums,) = take(1)
        up, down, load_sems, held, out_sems = take(5)
        loads = plan.start_hidden_loads(w_refs, slots, up, down, load_sems)
        n = jnp.concatenate([v[0] for v in pairs], axis=0)
        g = jnp.concatenate([v[1] for v in pairs], axis=0)
        n_t, g_t = turned(n), turned(g)
        if first:
            total = jnp.zeros(n.shape, f32)
            back = jnp.zeros(n.shape, f32)
            up_sums[...] = jnp.zeros(up_sums.shape, f32)
        else:
            total = jnp.concatenate([v[...] for v in before[:groups]], axis=0)
            back = jnp.concatenate([v[...] for v in before[groups : 2 * groups]], axis=0)
            up_sums[...] = before[2 * groups][...]
        side = lax.axis_index("ctx") & 1 if plan.paired else 0
        here = pl.multiple_of(side * plan.hidden, plan.hidden)
        for copies in loads:
            for copy in copies:
                copy.wait()
        places = [plan.block(r) for r in slots]
        u = nn(n, up[...]) + jnp.concatenate([up_bias[at, :, pl.ds(here, plan.hidden)] for at in places], axis=-1)
        half = 0.5 * (1.0 + lax.erf(u * (0.5**0.5)))
        z = (u * half).astype(bf16)
        slope = half + u * (jnp.exp(-0.5 * u * u) * 0.3989422804014327)
        d_u = (nn(g, down[...]) * slope).astype(bf16)
        up_grad, down_grad = nn(n_t, d_u), nn(g_t, z)
        sums = row_sum(d_u)
        stores = []
        for i, at in enumerate(places):
            cols = slice(i * plan.hidden, (i + 1) * plan.hidden)
            plan.put_hidden(i, 0, up_grad[:, cols], held)
            plan.put_hidden(i, 1, down_grad[:, cols], held)
            stores += plan.start_hidden(i, held, grads, out_sems)
            up_sums[at, :, pl.ds(here, plan.hidden)] = sums[:, cols]
        total = total + nt(z, down[...])
        back = back + nt(d_u, up[...])
        for i in range(groups):
            outs[i][...] = total[i * rows : (i + 1) * rows].astype(outs[i].dtype)
            backs[i][...] = back[i * rows : (i + 1) * rows].astype(backs[i].dtype)
        for copy in stores:
            copy.wait()

    return kernel


def on_device(
    mesh,
    tokens,
    cotangent,
    norm_gains,
    norm_shifts,
    qkv_spatial,
    proj_spatial,
    qkv_temporal,
    proj_temporal,
    up_weight,
    down_weight,
    out_bias,
    qv_bias,
    up_bias,
):
    shards, _, blocks = mesh.shape["shard"], mesh.shape["ctx"], mesh.shape["tp"]
    patches, model = tokens.shape[2:]
    head_cols = qkv_spatial.shape[2]
    wide = 4 * head_cols
    rows = 16 * SLOT
    plan = Plan(mesh, model, wide)
    paired = plan.paired
    x_rank, z_rank = lax.axis_index("shard"), lax.axis_index("tp")
    q_rank = lax.axis_index("ctx")

    def cut(v, axis, size, at):
        return lax.dynamic_slice_in_dim(v, at * size, size, axis)

    def joined(qkv, proj):
        if paired:
            part = model // 8
            qkv, proj = cut(qkv, 1, part, q_rank), cut(proj, 1, part, q_rank)
        return jnp.concatenate([qkv[0], qkv[1], qkv[2], proj.T], axis=1)

    own_space = joined(qkv_spatial, proj_spatial)
    own_time = joined(qkv_temporal, proj_temporal)
    own_up, own_down = up_weight, down_weight
    if paired:
        part = model // 4
        own_up = cut(cut(own_up, 0, part, q_rank >> 1), 1, plan.hidden, q_rank & 1)
        own_down = cut(cut(own_down, 0, plan.hidden, q_rank & 1), 1, part, q_rank >> 1)
    own_down = own_down.T
    part = norm_gains.shape[1]
    small = [norm_gains, norm_shifts, out_bias, qv_bias.reshape(-1, part), up_bias.reshape(-1, part)]
    small = jnp.concatenate(small, axis=0)
    msg_patch, msg_frame = lay_out(*after((tokens[0], cotangent[0]), own_space))
    own_hidden = jnp.concatenate([own_up, own_down], axis=0)

    if paired:

        def line(own, m):
            with jax.named_scope(f"line{m}"):
                return [own] + [shift_z(own, k) for k in (1, 2, 3)]

        def sides(a, m):
            with jax.named_scope(f"side{m}"):
                return a, flip_x(a), flip_y(a)

        def cores(parts, m):
            with jax.named_scope(f"core{m}"):
                return [flip_core(v) for v in parts]

        l0 = line(own_space, 0)
        with jax.named_scope("small"):
            other = flip_x(small)
        with jax.named_scope("frames"):
            frames = swap_ctx(*msg_frame)
        l0, other, frames[2], own_time, own_hidden = after((l0, other, frames[2], own_time, own_hidden))

        a0, x0, y0 = sides(jnp.stack(l0), 0)
        l1 = line(own_time, 1)
        x0, y0, l1 = after((x0, y0, l1))

        a1, x1, y1 = sides(jnp.stack(l1), 1)
        with jax.named_scope("line2"):
            l2 = shift_z(after(own_hidden, l1), 2)
        core0 = cores(after([a0, x0], l1), 0)
        x1, y1, l2 = after((x1, y1, l2))

        with jax.named_scope("corner0"):
            c0 = flip_x(after(y0, x1))
        with jax.named_scope("corner1"):
            c1 = flip_y(x1)
        with jax.named_scope("patches"):
            by_patch = swap_z_out(after(list(msg_patch), l2))
        c0, c1, by_patch = after((c0, c1, by_patch))

        a2, x2, y2 = sides(jnp.stack(after([own_hidden, l2], c0)), 2)
        core0 += cores([y0, c0], 0)
        with jax.named_scope("line3"):
            own = after(own_hidden, core0)
            l3 = [shift_z(own, 3), shift_z(own, 1)]
        w_space = [a0, x0, y0, c0] + core0
        first = jnp.where(x_rank == 0, small, other)
        second = jnp.where(x_rank == 0, other, small)
        small = jnp.stack([first, second])
    else:

        def gathered(v):
            v = lax.all_gather(v, "shard", axis=0, tiled=True)
            return [lax.all_gather(v, "tp", axis=1, tiled=True)[None]]

        w_space, w_time = gathered(own_space), gathered(own_time)
        w_hidden = lax.all_gather(own_hidden.reshape(2, -1, wide), "shard", axis=1, tiled=True)
        w_first = w_second = [lax.all_gather(w_hidden.reshape(1, 2 * model, wide), "tp", axis=0, tiled=True)]
        small = lax.all_gather(small, "shard", axis=0, tiled=False)
        frames = swap_ctx(*msg_frame)
        by_patch = swap_z_out(msg_patch)

    small = small.astype(f32)
    vectors = jnp.swapaxes(small[:, :13], 0, 1).reshape(13, model)
    gains, shifts, biases = vectors[0:3], vectors[3:6], vectors[6:9]
    qv = vectors[9:13].reshape(2, 2, blocks, head_cols)
    qv = jnp.concatenate([qv[:, 0], jnp.zeros_like(qv[:, 0]), qv[:, 1]], axis=-1)[:, :, None]
    up_b = small[:, 13:].reshape(blocks, 1, -1)

    step = -(-patches // 4)
    slot = jnp.arange(SLOT)[None, :]
    block = (jnp.arange(4) ^ q_rank)[:, None]
    valid = (slot < step) & (block * step + slot < patches)
    key_mask = jnp.where(valid, 0.0, -1e30).astype(f32).reshape(1, 4 * SLOT)
    key_mask = jnp.tile(key_mask, (1, 4))

    weight_scratch = [
        pltpu.VMEM((model, blocks * wide), bf16),
        pltpu.SemaphoreType.DMA((plan.n_loads(),)),
    ]
    p_shape = like((blocks, rows, 3 * head_cols))
    o_shape = like((blocks, rows, head_cols))
    log_shape = like((rows, 128), f32)
    full = like((rows, model), f32)
    unit = like((4, SLOT, model))

    p1, o1, log1, *branch = call(
        attention_forward(plan, False, head_cols, len(w_space)),
        by_patch + [gains[0:1], shifts[0:1], qv[0], key_mask, biases[0:2]] + w_space,
        len(w_space),
        [p_shape, o_shape, log_shape] + [unit] * 4,
        0,
        weight_scratch,
        "space_forward",
        20,
        wait=(0, 1, 2),
    )
    if paired:
        x2, y2, l3, branch = after((x2, y2, l3, branch))
        a3, x3, y3 = sides(jnp.stack(l3), 3)
    with jax.named_scope("branch_z"):
        branch = swap_z_back(branch)
    if paired:
        x3, y3, branch = after((x3, y3, branch))
        with jax.named_scope("corner2"):
            c2 = flip_x(after(y2, x3))
    with jax.named_scope("branch_ctx"):
        near, beside, beyond = to_ctx(branch)
        far = flip_y(beyond)
    if paired:
        core1 = cores(after([a1, x1, y1, c1], far), 1)
        with jax.named_scope("corner3"):
            c3 = [flip_x(y3[:1]), flip_y(after(x3[1:], far))]
        w_time = [a1, x1, y1, c1] + core1
    with jax.named_scope("branch_ctx"):
        branch = [near, flip_core(beside), far, flip_core(far)]

    p2, o2, log2, mid, stream, pair = call(
        attention_forward(plan, True, head_cols, len(w_time)),
        frames
        + branch
        + [gains[1:2], shifts[1:2], qv[1], key_mask, biases[0:2], gains[2:3], shifts[2:3]]
        + w_time,
        len(w_time),
        [p_shape, o_shape, log_shape, full, full, like((2, rows, model))],
        0,
        weight_scratch,
        "time_forward",
        20,
        wait=(0, 1, 2, 3, 4),
    )
    pairs = [pair]
    if paired:
        pair, c2, c3[1] = after((pair, c2, c3[1]))
        w_first, w_second = [a2, x2, y2, c2], [a3, x3, y3, *c3]
        pairs = [pair]
        with jax.named_scope("pair_core"):
            pairs.append(flip_core(pair))

    groups = len(pairs)
    hidden_whole = pltpu.VMEM((model, 2 * plan.hidden), bf16)
    hidden_scratch = [hidden_whole, hidden_whole, pltpu.SemaphoreType.DMA((16,))]
    hidden_scratch += plan.hidden_grad_scratch()
    hidden_grads = plan.hidden_grad_shapes()
    n_g = len(hidden_grads)
    up_shape = like((blocks, 1, wide), f32)
    got = call(
        mlp(plan, (0, 2), len(w_first), groups, rows, True),
        pairs + [up_b] + w_first,
        len(w_first),
        hidden_grads + [full] * (2 * groups) + [up_shape],
        n_g,
        hidden_scratch,
        "mlp_first",
        26,
    )
    first_grads, partial = got[:n_g], got[n_g:]
    got = call(
        mlp(plan, (1, 3), len(w_second), groups, rows, False),
        pairs + [up_b] + partial + w_second,
        len(w_second),
        hidden_grads + ([full] + [like((rows, model))] * (groups - 1)) * 2 + [up_shape],
        n_g,
        hidden_scratch,
        "mlp_second",
        26,
    )
    second_grads, results, backs, up_sums = got[:n_g], got[n_g : n_g + groups], got[n_g + groups : -1], got[-1]
    if paired:
        with jax.named_scope("hidden_side"):
            first_moved = [flip_y(first_grads[1]), flip_x(first_grads[3])]
            second_moved = [flip_y(second_grads[1]), flip_x(second_grads[3])]
        with jax.named_scope("back_core"):
            backs = [backs[0], flip_core(backs[1])]

    grads = plan.grad_shapes()
    n_g = len(grads)
    vec_shape = like((24, model), f32)
    qv_held = pltpu.VMEM((blocks, 1, 3 * head_cols), f32)
    d_time, time_vec, time_g, *g1 = call(
        time_backward(plan, head_cols, len(w_time), groups),
        [mid, stream, pair] + backs + [gains[2:3], gains[1:2], log2, p2] + w_time,
        len(w_time),
        [p_shape, vec_shape, like((rows, model))] + [unit] * 2 + [like((2,) + unit.shape)],
        0,
        weight_scratch + [qv_held],
        "time_backward",
        20,
    )
    if paired:
        g1, first_moved = after((g1, first_moved))
    with jax.named_scope("g1_ctx"):
        far = flip_y(g1[2])
    g_time = call(
        time_weights(plan),
        [mid, time_g, gains[1:2], shifts[1:2], d_time, o2],
        0,
        grads,
        n_g,
        plan.grad_scratch(),
        "time_weights",
        16,
    )
    if paired:
        g_time, far, second_moved = after((g_time, far, second_moved))
    with jax.named_scope("g1_ctx"):
        g1 = [g1[0], flip_core(g1[1]), far, flip_core(far)]
    with jax.named_scope("finished"):
        if paired:
            results = [results[0], flip_core(after(results[1], far))]

        def finish(*refs):
            total = refs[0][...] + refs[1][...] + refs[2][...]
            for ref in refs[3 : 2 + groups]:
                total = total + ref[...].astype(f32)
            put_ctx(refs[2 + groups :], nn(turn_rows(total.shape[0]), total.astype(bf16)))

        outs = [unit] * 2 + [like((2,) + unit.shape)]
        finished = call(finish, [biases[2:3], stream] + list(results), 0, outs, 0, [], "finish", 8)
    if paired:
        with jax.named_scope("time_core"):
            got_time = flip_core(g_time[1])
        pairs = [(first_grads[0], first_moved[0]), (second_grads[0], second_moved[0])]
        pairs += [(first_grads[2], first_moved[1]), (second_grads[2], second_moved[1])]
        hidden_rest_a, send_a, hidden_rest_b, send_b = hidden_after_side(pairs)
        with jax.named_scope("hidden_corner"):
            corner_a, corner_b = flip_x(send_a), flip_y(send_b)
    with jax.named_scope("g1_z"):
        g1 = swap_z_out(to_frames(g1))
    if paired:
        keep_ta, send_ta, keep_tb, send_tb = after_core(g_time[0], got_time)
        with jax.named_scope("time_side"):
            side_ta, side_tb = flip_y(after(send_ta, g1)), flip_x(after(send_tb, g1))
        hidden_own, *sends = hidden_after_corner(hidden_rest_a, corner_a, hidden_rest_b, corner_b)
        sends = after(sends, send_ta)
        with jax.named_scope("hidden_line"):
            hidden_moved = [shift_z(v, k) for v, k in zip(sends, (1, 2, 1, 2, 3))]

    got = call(
        space_weights(plan, head_cols, len(w_space)),
        by_patch + g1 + [gains[0:1], shifts[0:1], key_mask, log1, p1, o1] + w_space,
        len(w_space),
        grads + [p_shape],
        n_g,
        weight_scratch + plan.grad_scratch(),
        "space_weights",
        24,
        after=(sends[0], send_ta) if paired else (),
    )
    if paired:
        got, side_ta, side_tb, hidden_moved[:2] = after((got, side_ta, side_tb, hidden_moved[:2]))
    g_space, d_space = got[:n_g], got[n_g]
    vector, *back = call(
        space_backward(plan, head_cols, len(w_space)),
        by_patch + g1 + [time_vec, up_sums, gains[0:1], d_space] + w_space,
        len(w_space),
        [vec_shape] + [unit] * 4,
        0,
        weight_scratch + [qv_held],
        "space_backward",
        16,
    )

    if paired:
        with jax.named_scope("space_core"):
            got_space = flip_core(g_space[1])
        rest_ta, send_ta, rest_tb, send_tb = after_side((keep_ta, side_ta), (keep_tb, side_tb))
        with jax.named_scope("time_corner"):
            corner_ta, corner_tb = flip_x(send_ta), flip_y(send_tb)
        with jax.named_scope("vectors"):
            other = flip_core(vector)
        got_space, other, back, corner_ta, corner_tb, hidden_moved[4] = after(
            (got_space, other, back, corner_ta, corner_tb, hidden_moved[4])
        )

        keep_a, send_a, keep_b, send_b = after_core(g_space[0], got_space)
        with jax.named_scope("space_side"):
            side_a, side_b = flip_y(send_a), flip_x(send_b)
        own_time_sum, *sends = after_corner(rest_ta, corner_ta, rest_tb, corner_tb)
        with jax.named_scope("time_line"):
            time_moved = spread(sends)
        vector, *messages = pack(back[1:], vector, other)
        side_a, side_b, messages, time_moved[:2] = after((side_a, side_b, messages, time_moved[:2]))

        rest_a, send_a, rest_b, send_b = after_side((keep_a, side_a), (keep_b, side_b))
        with jax.named_scope("space_corner"):
            corner_a, corner_b = flip_x(send_a), flip_y(send_b)
        with jax.named_scope("token_grad"):
            moved = [shift_z(v, 4 - k) for k, v in zip((1, 2, 3), after(messages, send_a))]
        with jax.named_scope("finished"):
            far = flip_y(after(finished[2], send_a))
        qkv_time, proj_time = attention_total(own_time_sum, time_moved, head_cols, 2**15)
        corner_a, corner_b, moved, far, hidden_moved[2] = after(
            (corner_a, corner_b, moved, far, hidden_moved[2])
        )

        own, *sends = after_corner(rest_a, corner_a, rest_b, corner_b)
        with jax.named_scope("space_line"):
            space_moved = spread(sends)
        with jax.named_scope("finished"):
            finished = [finished[0], flip_core(after(finished[1], far)), far, flip_core(far)]
        token_grad, vector = unpack(back[0], vector, moved, patches)
        with jax.named_scope("vectors"):
            vector = vector + flip_y(vector)
            vector = own_vectors(mesh, vector, flip_x(vector))
        hidden_keep, hidden_send = hidden_total(hidden_own, hidden_moved)
        with jax.named_scope("hidden_core"):
            hidden_got = flip_core(hidden_send)
        grad_up, grad_down = hidden_join(hidden_keep, hidden_got)
        qkv_space, proj_space = attention_total(own, space_moved, head_cols, None)
    else:

        def summed(g):
            g = lax.psum_scatter(g.astype(f32), ("shard", "ctx"), scatter_dimension=1, tiled=True)
            return lax.psum_scatter(g, "tp", scatter_dimension=0, tiled=True)[0]

        def apart(total):
            three = total[:, : 3 * head_cols].reshape(-1, 3, head_cols)
            return jnp.swapaxes(three, 0, 1), total[:, 3 * head_cols :].T

        hidden_grad = jnp.concatenate([v[i : i + 1] for i in (0, 1) for v in (first_grads[0], second_grads[0])])
        grad_up, grad_down = summed(hidden_grad[:, :model]), summed(hidden_grad[:, model:])
        qkv_time, proj_time = apart(summed(g_time[0]))
        qkv_space, proj_space = apart(summed(g_space[0]))

    with jax.named_scope("finished"):
        if not paired:
            finished = swap_ctx(*finished)
        finished = bring_back(finished, False, patches, bf16)
    if not paired:
        token_grad = bring_back(swap_z_back(back), True, patches, f32)

    if not paired:
        vector = lax.psum(vector, ("shard", "ctx", "tp"))
        vector = own_vectors(mesh, vector, jnp.zeros_like(vector))
    gains, shifts, biases, qv, hidden = vector
    return (
        finished[None],
        token_grad[None],
        gains,
        shifts,
        qkv_space,
        proj_space,
        qkv_time,
        proj_time,
        grad_up,
        grad_down.T,
        biases,
        qv.reshape(2, 2, -1),
        hidden.reshape(-1),
    )


def solution(mesh):
    return jax.shard_map(
        functools.partial(on_device, mesh),
        mesh=mesh,
        in_specs=(
            P("shard", "ctx", "tp", None),
            P("shard", "ctx", "tp", None),
            P(None, "shard"),
            P(None, "shard"),
            P(None, "shard", "tp"),
            P("tp", "shard"),
            P(None, "shard", "tp"),
            P("tp", "shard"),
            P("shard", "tp"),
            P("tp", "shard"),
            P(None, "shard"),
            P(None, None, "shard"),
            P("shard"),
        ),
        out_specs=(
            P("shard", "ctx", "tp", None),
            P("shard", "ctx", "tp", None),
            P(None, ("shard", "ctx", "tp")),
            P(None, ("shard", "ctx", "tp")),
            P(None, ("shard", "ctx"), "tp"),
            P("tp", ("shard", "ctx")),
            P(None, ("shard", "ctx"), "tp"),
            P("tp", ("shard", "ctx")),
            P(("shard", "ctx"), "tp"),
            P("tp", ("shard", "ctx")),
            P(None, ("shard", "ctx", "tp")),
            P(None, None, ("shard", "ctx", "tp")),
            P(("shard", "ctx", "tp")),
        ),
        check_vma=False,
    )
```

```python
import functools

import jax
import jax.numpy as jnp
from jax import lax
from jax.experimental import pallas as pl
from jax.experimental.pallas import tpu as pltpu
from jax.sharding import PartitionSpec as P

HD = 64
EPS = 1e-06
SCALE = HD ** (-0.5)
SLOT = 16
bf16 = jnp.bfloat16
f32 = jnp.float32
VMEM = pl.BlockSpec(memory_space=pltpu.VMEM)
ANY = pl.BlockSpec(memory_space=pl.ANY)


def nn(a, b):
    return lax.dot_general(a, b, (((1,), (0,)), ((), ())), preferred_element_type=f32)


def nt(a, b):
    return lax.dot_general(a, b, (((1,), (1,)), ((), ())), preferred_element_type=f32)


def tn(a, b):
    return lax.dot_general(a, b, (((0,), (0,)), ((), ())), preferred_element_type=f32)


def turned(a):
    return a.astype(f32).T.astype(bf16)


def row_sum(v):
    return jnp.sum(v.astype(f32), axis=0, keepdims=True)


def standardize(v):
    c = v - jnp.mean(v, axis=-1, keepdims=True)
    r = lax.rsqrt(jnp.mean(c * c, axis=-1, keepdims=True) + EPS)
    return c * r, r


def norm_back(d, q, r, gain):
    e = d * gain
    return r * (e - jnp.mean(e, axis=-1, keepdims=True) - q * jnp.mean(e * q, axis=-1, keepdims=True))


def rows_of(parts):
    return jnp.concatenate([v[...].reshape(-1, v.shape[-1]) for v in parts], axis=0)


def put_rows(refs, value):
    n = value.shape[0] // len(refs)
    for i, r in enumerate(refs):
        r[...] = value[i * n : (i + 1) * n].reshape(r.shape).astype(r.dtype)


def put_ctx(refs, value):
    n = value.shape[0] // 4
    for i, to in enumerate((refs[0], refs[1], refs[2].at[0], refs[2].at[1])):
        to[...] = value[i * n : (i + 1) * n].reshape(to.shape).astype(to.dtype)


def like(shape, dtype=bf16):
    return jax.ShapeDtypeStruct(shape, dtype)


class Take:
    def __init__(self, refs):
        self.refs = list(refs)

    def __call__(self, n):
        got, self.refs = self.refs[:n], self.refs[n:]
        return got


def flip_x(v):
    return lax.ppermute(v, "shard", [(i, i ^ 1) for i in range(2)])


def flip_ctx(v, e):
    return lax.ppermute(v, "ctx", [(i, i ^ e) for i in range(4)])


def flip_core(v):
    return flip_ctx(v, 1)


def flip_y(v):
    return flip_ctx(v, 2)


def shift_z(v, k):
    return lax.ppermute(v, "tp", [(i, (i + k) % 4) for i in range(4)])


def swap_z_out(parts):
    return [parts[0]] + [shift_z(parts[k], k) for k in (1, 2, 3)]


def swap_z_back(parts):
    return [parts[0]] + [shift_z(parts[k], 4 - k) for k in (1, 2, 3)]


def swap_ctx(p0, p1, pair):
    far = flip_y(pair)
    return [p0, flip_core(p1), far, flip_core(far)]


def ctx_parts(refs):
    return [refs[0][...], refs[1][...], refs[2][0], refs[3][1]]


def after(value, *others):
    return lax.optimization_barrier((value, others))[0]


class Plan:
    def __init__(self, mesh, model, wide):
        self.sizes = (mesh.shape["shard"], mesh.shape["ctx"], mesh.shape["tp"])
        self.paired = self.sizes == (2, 4, 4)
        self.model, self.wide, self.blocks = model, wide, self.sizes[2]
        self.hidden = wide // 2 if self.paired else wide

    def ranks(self):
        q = lax.axis_index("ctx")
        return lax.axis_index("shard"), q >> 1, q & 1, lax.axis_index("tp")

    def block(self, r):
        if not self.paired:
            return r
        return lax.rem(lax.axis_index("tp") + r, self.blocks)

    def places(self):
        if not self.paired:
            return [(0, 0, 0, self.model, 0)]
        x, y, c, _ = self.ranks()
        rows = self.model // 8
        every = range(4)
        kinds = [(0, 0, every), (1, 0, every), (0, 1, every), (1, 1, every)]
        out = []
        for core in (0, 1):
            for i, (dx, dy, ks) in enumerate(kinds):
                row = (((x ^ dx) * 2 + (y ^ dy)) * 2 + (c ^ core)) * rows
                for n, k in enumerate(ks):
                    out.append((core * 4 + i, n, pl.multiple_of(row, rows), rows, (4 - k) % 4))
        return out

    def n_loads(self):
        return 32 if self.paired else 1

    def start_loads(self, refs, whole, sems):
        by_slot = [[] for _ in range(self.blocks)]
        for n, (i, k, row, rows, slot) in enumerate(self.places()):
            to = whole.at[pl.ds(row, rows), pl.ds(slot * self.wide, refs[i].shape[-1])]
            by_slot[slot].append(pltpu.make_async_copy(refs[i].at[k], to, sems.at[n]))
        for copies in by_slot:
            for copy in copies:
                copy.start()
        return by_slot

    def start_hidden_loads(self, refs, slots, up, down, sems):
        by_slot = [[], []]
        if self.paired:
            x, y, _, _ = self.ranks()
            rows = self.model // 4
            kinds = [(0, 0, (0, 1)), (1, 0, (0, 1)), (0, 1, (0, 1))]
            kinds += [(1, 1, (0, 1))] if len(refs) == 4 else [(1, 1, (0,)), (1, 1, (1,))]
            places = []
            for ref, (dx, dy, ks) in zip(refs, kinds):
                row = pl.multiple_of(((x ^ dx) * 2 + (y ^ dy)) * rows, rows)
                places += [(ref.at[n], row, k) for n, k in enumerate(ks)]
        else:
            rows = self.model
            places = [(refs[0].at[r], 0, i) for i, r in enumerate(slots)]
        for n, (source, row, i) in enumerate(places):
            for part, whole in enumerate((up, down)):
                to = whole.at[pl.ds(row, rows), pl.ds(i * self.hidden, self.hidden)]
                copy = pltpu.make_async_copy(source.at[part * rows : (part + 1) * rows], to, sems.at[2 * n + part])
                by_slot[i].append(copy)
        for copies in by_slot:
            for copy in copies:
                copy.start()
        return by_slot

    def grad_shapes(self):
        if self.paired:
            return [like((2, 2, 4, self.model // 8, self.wide))] * 2
        return [like((self.blocks, self.model, self.wide))]

    def grad_scratch(self):
        if self.paired:
            held = pltpu.VMEM((4, 2, 2, 2, self.model // 8, self.wide), bf16)
            return [held, pltpu.SemaphoreType.DMA((8,))]
        return [
            pltpu.VMEM((self.blocks, self.model, self.wide), bf16),
            pltpu.SemaphoreType.DMA((self.blocks,)),
        ]

    def hold(self, r, value, held):
        value = value.astype(bf16)
        if not self.paired:
            held[r] = value
            return
        x, y, c, _ = self.ranks()
        rows = self.model // 8
        for i in range(8):
            held[r, (i & 1) ^ c, ((i >> 1) & 1) ^ y, (i >> 2) ^ x] = value[i * rows : (i + 1) * rows]

    def store(self, held, outs, sems):
        copies = []
        for r in range(self.blocks):
            if not self.paired:
                copies.append(pltpu.make_async_copy(held.at[r], outs[0].at[r], sems.at[r]))
                continue
            for core in (1, 0):
                to = outs[core].at[:, :, r]
                copies.append(pltpu.make_async_copy(held.at[r, core], to, sems.at[2 * r + core]))
        for copy in copies:
            copy.start()
        for copy in copies:
            copy.wait()

    def hidden_grad_shapes(self):
        if self.paired:
            return [like((2, self.model // 2, self.hidden))] * 4
        return [like((2, 2 * self.model, self.hidden))]

    def hidden_grad_scratch(self):
        if self.paired:
            held = pltpu.VMEM((2, 2, 2, self.model // 2, self.hidden), bf16)
            return [held, pltpu.SemaphoreType.DMA((4,))]
        return [pltpu.VMEM((2, 2 * self.model, self.hidden), bf16), pltpu.SemaphoreType.DMA((2,))]

    def put_hidden(self, i, part, value, held):
        value = value.astype(bf16)
        if not self.paired:
            held[i, part * self.model : (part + 1) * self.model] = value
            return
        x, y, _, _ = self.ranks()
        rows = self.model // 4
        for n in range(4):
            to = held.at[i, (n & 1) ^ y, (n >> 1) ^ x]
            to[part * rows : (part + 1) * rows] = value[n * rows : (n + 1) * rows]

    def start_hidden(self, i, held, outs, sems):
        if not self.paired:
            copies = [pltpu.make_async_copy(held.at[i], outs[0].at[i], sems.at[i])]
        else:
            copies = []
            for side in (0, 1):
                source = held.at[i, side] if i == 0 else held.at[i, :, side]
                copies.append(pltpu.make_async_copy(source, outs[2 * i + side], sems.at[2 * i + side]))
        for copy in copies:
            copy.start()
        return copies


def call(kernel, ins, n_any, outs, n_any_out, scratch, name, limit, after=(), far=None, wait=()):
    n_in, n_after = len(ins), len(after)

    def run(*refs):
        kernel(*refs[:n_in], *refs[n_in + n_after :])

    ins = list(ins)
    for i, v in enumerate(ins):
        if i >= n_in - n_any or (far is not None and v.size >= far):
            ins[i] = pltpu.with_memory_space_constraint(v, pltpu.HBM)
    outs = [pltpu.HBM(v.shape, v.dtype) if i in wait else v for i, v in enumerate(outs)]
    got = pl.pallas_call(
        run,
        out_shape=outs,
        in_specs=[VMEM] * (n_in - n_any) + [ANY] * (n_any + n_after),
        out_specs=[ANY] * n_any_out + [VMEM] * (len(outs) - n_any_out),
        scratch_shapes=scratch,
        compiler_params=pltpu.CompilerParams(vmem_limit_bytes=limit * 2**20),
        name=name,
    )(*ins, *after)
    return list(got)


def add(u, v):
    return (u.astype(f32) + v.astype(f32)).astype(bf16)


def after_core(keep, got):
    rows, wide = keep.shape[-2:]
    cut = 3

    def kernel(k, g, keep_a, send_a, keep_b, send_b):
        for x in (0, 1):
            keep_a[x] = add(k[0, x, :2], g[0, x, :2])
            send_a[x] = add(k[1, x, :2], g[1, x, :2])
        for y in (0, 1):
            keep_b[y] = add(k[y, 0, 2:], g[y, 0, 2:])
            send_b[y] = add(k[y, 1, 2:], g[y, 1, 2:])

    whole = pl.BlockSpec((2, 2, 4, rows // cut, wide), lambda i: (0, 0, 0, i, 0))
    half = pl.BlockSpec((2, 2, rows // cut, wide), lambda i: (0, 0, i, 0))
    return pl.pallas_call(
        kernel,
        grid=(cut,),
        out_shape=[like((2, 2, rows, wide))] * 4,
        in_specs=[whole] * 2,
        out_specs=[half] * 4,
        compiler_params=pltpu.CompilerParams(vmem_limit_bytes=16 * 2**20),
        name="after_core",
    )(keep, got)


def after_side(*pairs):
    def kernel(*refs):
        n = len(pairs)
        for i in range(n):
            k, g = refs[2 * i], refs[2 * i + 1]
            refs[2 * n + 2 * i][...] = add(k[0], g[0])
            refs[2 * n + 2 * i + 1][...] = add(k[1], g[1])

    ins = [v for pair in pairs for v in pair]
    outs = [like(v.shape[1:]) for v in ins]
    return call(kernel, ins, 0, outs, 0, [], "after_side", 24)


def hidden_after_side(pairs):
    def kernel(*refs):
        for i in range(4):
            k, g = refs[2 * i], refs[2 * i + 1]
            rest, send = refs[8 + 2 * (i // 2)], refs[9 + 2 * (i // 2)]
            rest[i % 2] = add(k[0], g[0])
            send[i % 2] = add(k[1], g[1])

    ins = [v for pair in pairs for v in pair]
    return call(kernel, ins, 0, [like(ins[0].shape)] * 4, 0, [], "hidden_after_side", 24)


def after_corner(rest_a, got_a, rest_b, got_b):
    def kernel(ra, ga, rb, gb, own, *sends):
        own[...] = ra[0].astype(f32) + ga[0].astype(f32)
        sends[0][...] = add(ra[1], ga[1])
        sends[1][...] = add(rb[0], gb[0])
        sends[2][...] = add(rb[1], gb[1])

    shape = rest_a.shape[1:]
    outs = [like(shape, f32)] + [like(shape)] * 3
    return call(kernel, [rest_a, got_a, rest_b, got_b], 0, outs, 0, [], "after_corner", 12)


def hidden_after_corner(rest_a, got_a, rest_b, got_b):
    rows = rest_a.shape[1] // 2

    def kernel(ra, ga, rb, gb, own, *sends):
        own[...] = ra[0].astype(f32) + ga[0].astype(f32)
        for part in (0, 1):
            at = slice(part * rows, (part + 1) * rows)
            sends[2 * part][...] = add(ra[1, at], ga[1, at])
            sends[2 * part + 1][...] = add(rb[0, at], gb[0, at])
        sends[4][...] = add(rb[1], gb[1])

    shape = rest_a.shape[1:]
    half = (rows,) + shape[1:]
    outs = [like(shape, f32)] + [like(half)] * 4 + [like(shape)]
    return call(kernel, [rest_a, got_a, rest_b, got_b], 0, outs, 0, [], "hidden_after_corner", 12)


def spread(sends):
    return [shift_z(v, k) for k, v in zip((1, 2, 3), sends)]


def attention_total(own, moved, head_cols, far):
    rows = own.shape[0]
    three = 3 * head_cols

    def kernel(o, a, b, c, qkv, proj):
        total = o[...] + a[...].astype(f32) + b[...].astype(f32) + c[...].astype(f32)
        for t in range(3):
            qkv[t] = total[:, t * head_cols : (t + 1) * head_cols]
        proj[...] = total[:, three:].T

    outs = [like((3, rows, head_cols), f32), like((head_cols, rows), f32)]
    return call(kernel, [own] + moved, 0, outs, 0, [], "attention_total", 8, far=far)


def hidden_total(own, moved):
    rows, wide = own.shape[0] // 4, own.shape[1]

    def kernel(o, up_1, up_2, down_1, down_2, both, keep, send):
        core = lax.axis_index("ctx") & 1
        for part, pair in enumerate(((up_1, up_2), (down_1, down_2))):
            for half in (0, 1):
                at = slice(half * rows, (half + 1) * rows)
                of = slice((2 * part + half) * rows, (2 * part + half + 1) * rows)
                total = o[of] + both[of].astype(f32) + pair[0][at].astype(f32) + pair[1][at].astype(f32)

                @pl.when(core == half)
                def _(total=total, part=part):
                    keep[part] = total

                @pl.when(core != half)
                def _(total=total, part=part):
                    send[part] = total.astype(bf16)

    outs = [like((2, rows, wide), f32), like((2, rows, wide))]
    return call(kernel, [own] + moved, 0, outs, 0, [], "hidden_total", 8)


def hidden_join(keep, got):
    rows, wide = keep.shape[1:]

    def kernel(k, g, up, down):
        core = lax.axis_index("ctx") & 1
        here, there = pl.multiple_of(core * wide, wide), pl.multiple_of((1 - core) * wide, wide)
        for part, out in enumerate((up, down)):
            out[:, pl.ds(here, wide)] = k[part]
            out[:, pl.ds(there, wide)] = g[part].astype(f32)

    return call(kernel, [keep, got], 0, [like((rows, 2 * wide), f32)] * 2, 0, [], "hidden_join", 8)


def lay_out(x, c):
    frames, patches, width = x.shape
    step = -(-patches // 4)

    def kernel(x_ref, c_ref, *refs):
        by_patch, by_frame, held = refs[:4], refs[4:7], refs[7]
        z, q = lax.axis_index("tp"), lax.axis_index("ctx")
        for i, ref in enumerate((x_ref, c_ref)):
            for f in range(4):
                v = ref[f].astype(f32)
                for b in range(4):
                    part = v[b * step : min((b + 1) * step, patches)]
                    pad = jnp.zeros((SLOT - part.shape[0], width), f32)
                    held[i, f, b] = jnp.concatenate([part, pad], axis=0).astype(bf16)
        for s in range(4):
            f = lax.rem(z + s, 4)
            for e in range(4):
                by_patch[s][e * SLOT : (e + 1) * SLOT] = held[0, f, q ^ e]
                to = by_frame[e] if e < 2 else by_frame[2].at[e - 2]
                to[0, s] = held[0, f, q ^ e]
                to[1, s] = held[1, f, q ^ e]

    both = (2, 4, SLOT, width)
    outs = [like((4 * SLOT, width))] * 4 + [like(both)] * 2 + [like((2,) + both)]
    got = call(kernel, [x, c], 0, outs, 0, [pltpu.VMEM((2, 4, 4, SLOT, width), bf16)], "lay_out", 8)
    return got[:4], got[4:]


def put_tokens(values, frames_first, held, out):
    z, q = lax.axis_index("tp"), lax.axis_index("ctx")
    patches, width = out.shape[0], out.shape[-1]
    step = -(-patches // 4)
    for i, v in enumerate(values):
        v = v.reshape(4, SLOT, width).astype(f32)
        if frames_first:
            held[i] = v
        else:
            held[:, i] = v
    for f in range(4):
        s = lax.rem(f + 4 - z, 4)
        rows = [held[s, b ^ q][: min(step, patches - b * step)] for b in range(4)]
        out[:, f] = jnp.concatenate(rows, axis=0).astype(out.dtype)


def bring_back(parts, frames_first, patches, dtype):
    width = parts[0].shape[-1]

    def kernel(*refs):
        ins, out, held = refs[:4], refs[4], refs[5]
        put_tokens([r[...] for r in ins] if frames_first else ctx_parts(ins), frames_first, held, out)

    scratch = [pltpu.VMEM((4, 4, SLOT, width), f32)]
    got = call(kernel, parts, 0, [like((patches, 4, width), dtype)], 0, scratch, "bring_back", 8)
    return jnp.swapaxes(got[0], 0, 1)


def pack(parts, vector, other):
    rows, width = 4 * SLOT, parts[0].shape[-1]
    extra = vector.shape[0]

    def kernel(a, b, c, vec, far, total, *outs):
        v = vec[...] + far[...]
        total[...] = v
        high = v.astype(bf16)
        low = (v - high.astype(f32)).astype(bf16)
        below = jnp.concatenate([high.astype(f32), low.astype(f32)], axis=0).astype(bf16)
        for part, out in zip((a, b, c), outs):
            out[:rows] = part[...].reshape(rows, width)
            out[rows:] = below

    outs = [like(vector.shape, f32)] + [like((rows + 2 * extra, width))] * 3
    return call(kernel, parts + [vector, other], 0, outs, 0, [], "pack", 8)


def own_vectors(mesh, vector, other):
    blocks, model = mesh.shape["tp"], vector.shape[-1]
    many = mesh.size
    size, hidden = model // many, 4 * model // many

    def kernel(vec, far, gains, shifts, biases, qv, up):
        place = (lax.axis_index("shard") * mesh.shape["ctx"] + lax.axis_index("ctx")) * blocks + lax.axis_index("tp")
        total = vec[...] + far[...]
        mine = pltpu.roll(total, lax.rem(model - place * size, model), 1)[:, :size]
        gains[...] = mine[0:3]
        shifts[...] = mine[3:6]
        biases[...] = mine[6:9]
        qv[...] = mine[9:13]
        at = place * hidden
        for row in range(4):

            @pl.when(lax.div(at, model) == row)
            def _(row=row):
                here = total[13 + row : 14 + row]
                up[...] = pltpu.roll(here, lax.rem(model - lax.rem(at, model), model), 1)[:, :hidden]

    outs = [like((3, size), f32)] * 3 + [like((4, size), f32), like((1, hidden), f32)]
    return call(kernel, [vector, other], 0, outs, 0, [], "own_vectors", 4)


def unpack(own, vector, moved, patches):
    rows, width = 4 * SLOT, own.shape[-1]
    extra = vector.shape[0]

    def kernel(*refs):
        own_ref, vec, ins = refs[0], refs[1], refs[2:5]
        out, total, held = refs[5:]
        put_tokens([own_ref[...]] + [r[:rows] for r in ins], True, held, out)
        v = vec[...]
        for r in ins:
            below = r[rows:].astype(f32)
            v = v + (below[:extra] + below[extra:])
        total[...] = v

    scratch = [pltpu.VMEM((4, 4, SLOT, width), f32)]
    outs = [like((patches, 4, width), f32), like(vector.shape, f32)]
    token_grad, total = call(kernel, [own, vector] + moved, 0, outs, 0, scratch, "unpack", 8, far=2**15)
    return jnp.swapaxes(token_grad, 0, 1), total


def to_ctx(parts):
    def kernel(*refs):
        for s in range(4):
            for e in range(4):
                to = refs[4 + e] if e < 2 else refs[6].at[e - 2]
                to[s] = refs[s][e]

    shape = parts[0].shape
    return call(kernel, parts, 0, [like(shape)] * 2 + [like((2,) + shape)], 0, [], "to_ctx", 4)


def to_frames(parts):
    def kernel(*refs):
        for e, v in enumerate(ctx_parts(refs[:4])):
            for s in range(4):
                refs[4 + s][e] = v[s]

    return call(kernel, parts, 0, [like(parts[0].shape)] * 4, 0, [], "to_frames", 4)


def turn_rows(rows, columns):
    a = lax.broadcasted_iota(jnp.int32, (rows, columns), 0)
    b = lax.broadcasted_iota(jnp.int32, (rows, columns), 1)
    bits = SLOT.bit_length() - 1
    return jnp.where(b == ((a & (SLOT - 1)) << bits) + (a >> bits), 1.0, 0.0).astype(bf16)


def masks_of(timed, rows, mask_ref):
    if not timed:
        return [slice(0, rows)], mask_ref[...]
    half = 8 * SLOT
    a = lax.broadcasted_iota(jnp.int32, (half, half), 0)
    b = lax.broadcasted_iota(jnp.int32, (half, half), 1)
    return [slice(0, half), slice(half, 2 * half)], jnp.where((a ^ b) < SLOT, 0.0, -1e30).astype(f32)


def filled(v, ranges):
    missing = ranges[-1].stop - v.shape[0]
    return jnp.concatenate([v, jnp.zeros((missing, v.shape[1]), v.dtype)], axis=0) if missing else v


def head_slices(p, h, head_cols):
    return [p[:, t * head_cols + h * HD : t * head_cols + (h + 1) * HD] for t in range(3)]


def attention_forward(plan, timed, head_cols, n_w):
    heads = head_cols // HD
    three = 3 * head_cols

    def kernel(*refs):
        take = Take(refs)
        x_refs = take(4)
        b_refs = take(4) if timed else []
        gain, shift, qv, mask_ref, bias_in = take(5)
        next_norm = take(2) if timed else []
        w_refs = take(n_w)
        p_ref, o_ref, log_ref = take(3)
        outs = take(3) if timed else take(4)
        whole, sems = take(2)
        loads = plan.start_loads(w_refs, whole, sems)
        if timed:
            parts = ctx_parts(x_refs)
            swap = turn_rows(log_ref.shape[0], 16 * SLOT)
            x = nn(swap, rows_of([v[0] for v in parts]))
            x = x + nn(swap, rows_of(ctx_parts(b_refs))) + bias_in[0:1]
            outs[0][...] = x
            outs[2][1] = nn(swap, rows_of([v[1] for v in parts])).astype(bf16)
        else:
            x = rows_of(x_refs).astype(f32)
        ranges, mask = masks_of(timed, x.shape[0], mask_ref)
        q, _ = standardize(x)
        n = (q * gain[...] + shift[...]).astype(bf16)
        total = jnp.zeros(x.shape, f32)
        scale = jnp.where(lax.broadcasted_iota(jnp.int32, (1, three), 1) < head_cols, SCALE, 1.0).astype(f32)
        for r in range(plan.blocks):
            at = r * plan.wide
            for copy in loads[r]:
                copy.wait()
            p = ((nn(n, whole[:, at : at + three]) + qv[plan.block(r)]) * scale).astype(bf16)
            p_ref[r] = p
            wide_p, end, rows = filled(p, ranges), ranges[-1].stop, x.shape[0]
            cells = [[v[m] for v in head_slices(wide_p, h, head_cols)] for h in range(heads) for m in ranges]
            s = jnp.concatenate([nt(qh, kh) + mask for qh, kh, _ in cells], axis=0)
            top = jnp.max(s, axis=-1, keepdims=True)
            e = jnp.exp(s - top)
            total_e = jnp.sum(e, axis=-1, keepdims=True)
            log = top + jnp.log(total_e)
            w = (e / total_e).astype(bf16)
            size = mask.shape[-1]
            o = [nn(w[i * size : (i + 1) * size], vh) for i, (_, _, vh) in enumerate(cells)]
            for h in range(heads):
                log_ref[:, r * heads + h : r * heads + h + 1] = log[h * end : h * end + rows]
            n_m = len(ranges)
            o = jnp.concatenate(
                [jnp.concatenate(o[h * n_m : (h + 1) * n_m], axis=0) for h in range(heads)], axis=-1
            ).astype(bf16)[:rows]
            o_ref[r] = o
            total = total + nt(o, whole[:, at + three : at + plan.wide])
        if timed:
            x = x + total + bias_in[1:2]
            outs[1][...] = x
            q, _ = standardize(x)
            outs[2][0] = (q * next_norm[0][...] + next_norm[1][...]).astype(bf16)
        else:
            put_rows(outs, total)

    return kernel


def heads_backward(p, d_o, log, ranges, mask, head_cols):
    rows = p.shape[0]
    p, d_o, log = filled(p, ranges), filled(d_o, ranges), filled(log, ranges)
    heads, n_m, size = head_cols // HD, len(ranges), mask.shape[-1]
    cells = []
    for h in range(heads):
        parts = head_slices(p, h, head_cols) + [d_o[:, h * HD : (h + 1) * HD], log[:, h : h + 1]]
        cells += [[v[m] for v in parts] for m in ranges]
    s = jnp.concatenate([nt(qh, kh) + (mask - lh) for qh, kh, _, _, lh in cells], axis=0)
    d_w = jnp.concatenate([nt(doh, vh) for _, _, vh, doh, _ in cells], axis=0)
    w = jnp.exp(s)
    d_s = (w * (d_w - jnp.sum(d_w * w, axis=-1, keepdims=True))).astype(bf16)
    w = w.astype(bf16)
    at = [slice(i * size, (i + 1) * size) for i in range(len(cells))]
    d_q = [nn(d_s[m], cell[1]) * SCALE for m, cell in zip(at, cells)]
    d_k = [tn(d_s[m], cell[0]) for m, cell in zip(at, cells)]
    d_v = [tn(w[m], cell[3]) for m, cell in zip(at, cells)]
    columns = [jnp.concatenate(v[h * n_m : (h + 1) * n_m], axis=0) for v in (d_q, d_k, d_v) for h in range(heads)]
    return jnp.concatenate(columns, axis=-1).astype(bf16)[:rows]


def put_qv(vec, layer, qv_held, head_cols):
    for i, t in enumerate((0, 2)):
        row = [qv_held[j][:, t * head_cols : (t + 1) * head_cols] for j in range(qv_held.shape[0])]
        vec[9 + 2 * layer + i : 10 + 2 * layer + i] = jnp.concatenate(row, axis=-1)


def time_backward(plan, head_cols, n_w, n_back):
    heads = head_cols // HD
    three = 3 * head_cols

    def kernel(*refs):
        take = Take(refs)
        x_ref, next_x, pair = take(3)
        back_refs = take(n_back)
        next_gain, gain, log_ref = take(3)
        (p_ref,) = take(1)
        w_refs = take(n_w)
        d_ref, vec, g_out = take(3)
        outs = take(3)
        whole, sems, qv_held = take(3)
        loads = plan.start_loads(w_refs, whole, sems)
        vec[...] = jnp.zeros(vec.shape, f32)
        x = x_ref[...]
        rows = x.shape[0]
        ranges, mask = masks_of(True, rows, None)
        g = pair[1].astype(f32)
        q3, r3 = standardize(next_x[...])
        d = back_refs[0][...].astype(f32)
        for ref in back_refs[1:]:
            d = d + ref[...].astype(f32)
        vec[2:3] = row_sum(d * q3)
        vec[5:6] = row_sum(d)
        vec[8:9] = row_sum(g)
        g = g + norm_back(d, q3, r3, next_gain[...])
        g_b = g.astype(bf16)
        g_out[...] = g_b
        vec[7:8] = row_sum(g_b)
        q, r_x = standardize(x)
        d_n = jnp.zeros(x.shape, f32)
        for r in range(plan.blocks):
            at = r * plan.wide
            for copy in loads[r]:
                copy.wait()
            d_o = nn(g_b, whole[:, at + three : at + plan.wide]).astype(bf16)
            log = log_ref[:, r * heads : (r + 1) * heads]
            d_p = heads_backward(p_ref[r], d_o, log, ranges, mask, head_cols)
            d_ref[r] = d_p
            qv_held[plan.block(r)] = row_sum(d_p)
            d_n = d_n + nt(d_p, whole[:, at : at + three])
        vec[1:2] = row_sum(d_n * q)
        vec[4:5] = row_sum(d_n)
        put_qv(vec, 1, qv_held, head_cols)
        g = g + norm_back(d_n, q, r_x, gain[...])
        put_ctx(outs, nn(turn_rows(16 * SLOT, rows), g.astype(bf16)))

    return kernel


def time_weights(plan):
    def kernel(*refs):
        take = Take(refs)
        x_ref, g_ref, gain, shift = take(4)
        d_ref, o_ref = take(2)
        grads = take(len(plan.grad_shapes()))
        held, out_sems = take(2)
        q, _ = standardize(x_ref[...])
        n_t = (q * gain[...] + shift[...]).T.astype(bf16)
        g_t = turned(g_ref[...])
        for r in range(plan.blocks):
            block = jnp.concatenate([nn(n_t, d_ref[r]), nn(g_t, o_ref[r])], axis=-1)
            plan.hold(r, block, held)
        plan.store(held, grads, out_sems)

    return kernel


def space_weights(plan, head_cols, n_w):
    heads = head_cols // HD
    three = 3 * head_cols

    def kernel(*refs):
        take = Take(refs)
        x_refs, g_refs = take(4), take(4)
        gain, shift, mask_ref, log_ref = take(4)
        p_ref, o_ref = take(2)
        w_refs = take(n_w)
        grads = take(len(plan.grad_shapes()))
        (d_ref,) = take(1)
        whole, sems, held, out_sems = take(4)
        loads = plan.start_loads(w_refs, whole, sems)
        x = rows_of(x_refs).astype(f32)
        g_b = rows_of(g_refs)
        g_t = turned(g_b)
        ranges, mask = masks_of(False, x.shape[0], mask_ref)
        q, _ = standardize(x)
        n_t = (q * gain[...] + shift[...]).T.astype(bf16)
        for r in range(plan.blocks):
            at = r * plan.wide
            for copy in loads[r]:
                copy.wait()
            d_o = nn(g_b, whole[:, at + three : at + plan.wide]).astype(bf16)
            log = log_ref[:, r * heads : (r + 1) * heads]
            d_p = heads_backward(p_ref[r], d_o, log, ranges, mask, head_cols)
            d_ref[r] = d_p
            block = jnp.concatenate([nn(n_t, d_p), nn(g_t, o_ref[r])], axis=-1)
            plan.hold(r, block, held)
        plan.store(held, grads, out_sems)

    return kernel


def space_backward(plan, head_cols, n_w):
    three = 3 * head_cols

    def kernel(*refs):
        take = Take(refs)
        x_refs, g_refs = take(4), take(4)
        time_vec, up_sums, gain = take(3)
        (d_ref,) = take(1)
        w_refs = take(n_w)
        (vec,) = take(1)
        outs = take(4)
        whole, sems, qv_held = take(3)
        loads = plan.start_loads(w_refs, whole, sems)
        x, g = rows_of(x_refs).astype(f32), rows_of(g_refs).astype(f32)
        vec[...] = time_vec[...]
        for j in range(up_sums.shape[0]):
            vec[13 + j : 14 + j] = up_sums[j]
        vec[6:7] = row_sum(g)
        q, r_x = standardize(x)
        d_n = jnp.zeros(x.shape, f32)
        for r in range(plan.blocks):
            at = r * plan.wide
            for copy in loads[r]:
                copy.wait()
            d_p = d_ref[r]
            qv_held[plan.block(r)] = row_sum(d_p)
            d_n = d_n + nt(d_p, whole[:, at : at + three])
        vec[0:1] = row_sum(d_n * q)
        vec[3:4] = row_sum(d_n)
        put_qv(vec, 0, qv_held, head_cols)
        put_rows(outs, g + norm_back(d_n, q, r_x, gain[...]))

    return kernel


def mlp(plan, slots, n_w, groups, rows, first):
    def kernel(*refs):
        take = Take(refs)
        pairs = take(groups)
        (up_bias,) = take(1)
        before = [] if first else take(2 * groups + 1)
        w_refs = take(n_w)
        grads = take(len(plan.hidden_grad_shapes()))
        outs = take(groups)
        backs = take(groups)
        (up_sums,) = take(1)
        up, down, load_sems, held, out_sems = take(5)
        loads = plan.start_hidden_loads(w_refs, slots, up, down, load_sems)
        n = jnp.concatenate([v[0] for v in pairs], axis=0)
        g = jnp.concatenate([v[1] for v in pairs], axis=0)
        n_t, g_t = turned(n), turned(g)
        if first:
            total = jnp.zeros(n.shape, f32)
            back = jnp.zeros(n.shape, f32)
            up_sums[...] = jnp.zeros(up_sums.shape, f32)
        else:
            total = jnp.concatenate([v[...] for v in before[:groups]], axis=0)
            back = jnp.concatenate([v[...] for v in before[groups : 2 * groups]], axis=0)
            up_sums[...] = before[2 * groups][...]
        side = lax.axis_index("ctx") & 1 if plan.paired else 0
        here = pl.multiple_of(side * plan.hidden, plan.hidden)
        for copies in loads:
            for copy in copies:
                copy.wait()
        places = [plan.block(r) for r in slots]
        u = nn(n, up[...]) + jnp.concatenate([up_bias[at, :, pl.ds(here, plan.hidden)] for at in places], axis=-1)
        half = 0.5 * (1.0 + lax.erf(u * (0.5**0.5)))
        z = (u * half).astype(bf16)
        slope = half + u * (jnp.exp(-0.5 * u * u) * 0.3989422804014327)
        d_u = (nn(g, down[...]) * slope).astype(bf16)
        up_grad, down_grad = nn(n_t, d_u), nn(g_t, z)
        sums = row_sum(d_u)
        stores = []
        for i, at in enumerate(places):
            cols = slice(i * plan.hidden, (i + 1) * plan.hidden)
            plan.put_hidden(i, 0, up_grad[:, cols], held)
            plan.put_hidden(i, 1, down_grad[:, cols], held)
            stores += plan.start_hidden(i, held, grads, out_sems)
            up_sums[at, :, pl.ds(here, plan.hidden)] = sums[:, cols]
        total = total + nt(z, down[...])
        back = back + nt(d_u, up[...])
        for i in range(groups):
            outs[i][...] = total[i * rows : (i + 1) * rows].astype(outs[i].dtype)
            backs[i][...] = back[i * rows : (i + 1) * rows].astype(backs[i].dtype)
        for copy in stores:
            copy.wait()

    return kernel


def on_device(
    mesh,
    tokens,
    cotangent,
    norm_gains,
    norm_shifts,
    qkv_spatial,
    proj_spatial,
    qkv_temporal,
    proj_temporal,
    up_weight,
    down_weight,
    out_bias,
    qv_bias,
    up_bias,
):
    shards, _, blocks = mesh.shape["shard"], mesh.shape["ctx"], mesh.shape["tp"]
    patches, model = tokens.shape[2:]
    head_cols = qkv_spatial.shape[2]
    wide = 4 * head_cols
    rows = 16 * SLOT
    plan = Plan(mesh, model, wide)
    paired = plan.paired
    x_rank, z_rank = lax.axis_index("shard"), lax.axis_index("tp")
    q_rank = lax.axis_index("ctx")

    def cut(v, axis, size, at):
        return lax.dynamic_slice_in_dim(v, at * size, size, axis)

    def joined(qkv, proj):
        if paired:
            part = model // 8
            qkv, proj = cut(qkv, 1, part, q_rank), cut(proj, 1, part, q_rank)
        return jnp.concatenate([qkv[0], qkv[1], qkv[2], proj.T], axis=1)

    own_space = joined(qkv_spatial, proj_spatial)
    own_time = joined(qkv_temporal, proj_temporal)
    own_up, own_down = up_weight, down_weight
    if paired:
        part = model // 4
        own_up = cut(cut(own_up, 0, part, q_rank >> 1), 1, plan.hidden, q_rank & 1)
        own_down = cut(cut(own_down, 0, plan.hidden, q_rank & 1), 1, part, q_rank >> 1)
    own_down = own_down.T
    part = norm_gains.shape[1]
    small = [norm_gains, norm_shifts, out_bias, qv_bias.reshape(-1, part), up_bias.reshape(-1, part)]
    small = jnp.concatenate(small, axis=0)
    msg_patch, msg_frame = lay_out(*after((tokens[0], cotangent[0]), own_space))
    own_hidden = jnp.concatenate([own_up, own_down], axis=0)

    if paired:

        def line(own, m):
            with jax.named_scope(f"line{m}"):
                return [own] + [shift_z(own, k) for k in (1, 2, 3)]

        def sides(a, m):
            with jax.named_scope(f"side{m}"):
                return a, flip_x(a), flip_y(a)

        def cores(parts, m):
            with jax.named_scope(f"core{m}"):
                return [flip_core(v) for v in parts]

        l0 = line(own_space, 0)
        with jax.named_scope("small"):
            other = flip_x(small)
        with jax.named_scope("frames"):
            frames = swap_ctx(*msg_frame)
        l0, other, frames[2], own_time, own_hidden = after((l0, other, frames[2], own_time, own_hidden))

        a0, x0, y0 = sides(jnp.stack(l0), 0)
        l1 = line(own_time, 1)
        x0, y0, l1 = after((x0, y0, l1))

        a1, x1, y1 = sides(jnp.stack(l1), 1)
        with jax.named_scope("line2"):
            l2 = shift_z(after(own_hidden, l1), 2)
        core0 = cores(after([a0, x0], l1), 0)
        x1, y1, l2 = after((x1, y1, l2))

        with jax.named_scope("corner0"):
            c0 = flip_x(after(y0, x1))
        with jax.named_scope("corner1"):
            c1 = flip_y(x1)
        with jax.named_scope("patches"):
            by_patch = swap_z_out(after(list(msg_patch), l2))
        c0, c1, by_patch = after((c0, c1, by_patch))

        a2, x2, y2 = sides(jnp.stack(after([own_hidden, l2], c0)), 2)
        core0 += cores([y0, c0], 0)
        with jax.named_scope("line3"):
            own = after(own_hidden, core0)
            l3 = [shift_z(own, 3), shift_z(own, 1)]
        w_space = [a0, x0, y0, c0] + core0
        first = jnp.where(x_rank == 0, small, other)
        second = jnp.where(x_rank == 0, other, small)
        small = jnp.stack([first, second])
    else:

        def gathered(v):
            v = lax.all_gather(v, "shard", axis=0, tiled=True)
            return [lax.all_gather(v, "tp", axis=1, tiled=True)[None]]

        w_space, w_time = gathered(own_space), gathered(own_time)
        w_hidden = lax.all_gather(own_hidden.reshape(2, -1, wide), "shard", axis=1, tiled=True)
        w_first = w_second = [lax.all_gather(w_hidden.reshape(1, 2 * model, wide), "tp", axis=0, tiled=True)]
        small = lax.all_gather(small, "shard", axis=0, tiled=False)
        frames = swap_ctx(*msg_frame)
        by_patch = swap_z_out(msg_patch)

    small = small.astype(f32)
    vectors = jnp.swapaxes(small[:, :13], 0, 1).reshape(13, model)
    gains, shifts, biases = vectors[0:3], vectors[3:6], vectors[6:9]
    qv = vectors[9:13].reshape(2, 2, blocks, head_cols)
    qv = jnp.concatenate([qv[:, 0], jnp.zeros_like(qv[:, 0]), qv[:, 1]], axis=-1)[:, :, None]
    up_b = small[:, 13:].reshape(blocks, 1, -1)

    step = -(-patches // 4)
    slot = jnp.arange(SLOT)[None, :]
    block = (jnp.arange(4) ^ q_rank)[:, None]
    valid = (slot < step) & (block * step + slot < patches)
    key_mask = jnp.where(valid, 0.0, -1e30).astype(f32).reshape(1, 4 * SLOT)
    key_mask = jnp.tile(key_mask, (1, 4))

    weight_scratch = [
        pltpu.VMEM((model, blocks * wide), bf16),
        pltpu.SemaphoreType.DMA((plan.n_loads(),)),
    ]
    p_shape = like((blocks, rows, 3 * head_cols))
    o_shape = like((blocks, rows, head_cols))
    log_shape = like((rows, 128), f32)
    full = like((rows, model), f32)
    unit = like((4, SLOT, model))
    time_rows = 16 * step
    p_time, o_time = like((blocks, time_rows, 3 * head_cols)), like((blocks, time_rows, head_cols))
    full_time = like((time_rows, model), f32)

    p1, o1, log1, *branch = call(
        attention_forward(plan, False, head_cols, len(w_space)),
        by_patch + [gains[0:1], shifts[0:1], qv[0], key_mask, biases[0:2]] + w_space,
        len(w_space),
        [p_shape, o_shape, log_shape] + [unit] * 4,
        0,
        weight_scratch,
        "space_forward",
        20,
        wait=(0, 1, 2),
    )
    if paired:
        x2, y2, l3, branch = after((x2, y2, l3, branch))
        a3, x3, y3 = sides(jnp.stack(l3), 3)
    with jax.named_scope("branch_z"):
        branch = swap_z_back(branch)
    if paired:
        x3, y3, branch = after((x3, y3, branch))
        with jax.named_scope("corner2"):
            c2 = flip_x(after(y2, x3))
    with jax.named_scope("branch_ctx"):
        near, beside, beyond = to_ctx(branch)
        far = flip_y(beyond)
    if paired:
        core1 = cores(after([a1, x1, y1, c1], far), 1)
        with jax.named_scope("corner3"):
            c3 = [flip_x(y3[:1]), flip_y(after(x3[1:], far))]
        w_time = [a1, x1, y1, c1] + core1
    with jax.named_scope("branch_ctx"):
        branch = [near, flip_core(beside), far, flip_core(far)]

    p2, o2, log2, mid, stream, pair = call(
        attention_forward(plan, True, head_cols, len(w_time)),
        frames
        + branch
        + [gains[1:2], shifts[1:2], qv[1], key_mask, biases[0:2], gains[2:3], shifts[2:3]]
        + w_time,
        len(w_time),
        [p_time, o_time, like((time_rows, 128), f32), full_time, full_time, like((2, time_rows, model))],
        0,
        weight_scratch,
        "time_forward",
        20,
        wait=(0, 1, 2, 3, 4),
    )
    pairs = [pair]
    if paired:
        pair, c2, c3[1] = after((pair, c2, c3[1]))
        w_first, w_second = [a2, x2, y2, c2], [a3, x3, y3, *c3]
        pairs = [pair]
        with jax.named_scope("pair_core"):
            pairs.append(flip_core(pair))

    groups = len(pairs)
    hidden_whole = pltpu.VMEM((model, 2 * plan.hidden), bf16)
    hidden_scratch = [hidden_whole, hidden_whole, pltpu.SemaphoreType.DMA((16,))]
    hidden_scratch += plan.hidden_grad_scratch()
    hidden_grads = plan.hidden_grad_shapes()
    n_g = len(hidden_grads)
    up_shape = like((blocks, 1, wide), f32)
    got = call(
        mlp(plan, (0, 2), len(w_first), groups, time_rows, True),
        pairs + [up_b] + w_first,
        len(w_first),
        hidden_grads + [full_time] * (2 * groups) + [up_shape],
        n_g,
        hidden_scratch,
        "mlp_first",
        26,
    )
    first_grads, partial = got[:n_g], got[n_g:]
    got = call(
        mlp(plan, (1, 3), len(w_second), groups, time_rows, False),
        pairs + [up_b] + partial + w_second,
        len(w_second),
        hidden_grads + ([full_time] + [like((time_rows, model))] * (groups - 1)) * 2 + [up_shape],
        n_g,
        hidden_scratch,
        "mlp_second",
        26,
    )
    second_grads, results, backs, up_sums = got[:n_g], got[n_g : n_g + groups], got[n_g + groups : -1], got[-1]
    if paired:
        with jax.named_scope("hidden_side"):
            first_moved = [flip_y(first_grads[1]), flip_x(first_grads[3])]
            second_moved = [flip_y(second_grads[1]), flip_x(second_grads[3])]
        with jax.named_scope("back_core"):
            backs = [backs[0], flip_core(backs[1])]

    grads = plan.grad_shapes()
    n_g = len(grads)
    vec_shape = like((24, model), f32)
    qv_held = pltpu.VMEM((blocks, 1, 3 * head_cols), f32)
    d_time, time_vec, time_g, *g1 = call(
        time_backward(plan, head_cols, len(w_time), groups),
        [mid, stream, pair] + backs + [gains[2:3], gains[1:2], log2, p2] + w_time,
        len(w_time),
        [p_time, vec_shape, like((time_rows, model))] + [unit] * 2 + [like((2,) + unit.shape)],
        0,
        weight_scratch + [qv_held],
        "time_backward",
        20,
    )
    if paired:
        g1, first_moved = after((g1, first_moved))
    with jax.named_scope("g1_ctx"):
        far = flip_y(g1[2])
    g_time = call(
        time_weights(plan),
        [mid, time_g, gains[1:2], shifts[1:2], d_time, o2],
        0,
        grads,
        n_g,
        plan.grad_scratch(),
        "time_weights",
        16,
    )
    if paired:
        g_time, far, second_moved = after((g_time, far, second_moved))
    with jax.named_scope("g1_ctx"):
        g1 = [g1[0], flip_core(g1[1]), far, flip_core(far)]
    with jax.named_scope("finished"):
        if paired:
            results = [results[0], flip_core(after(results[1], far))]

        def finish(*refs):
            total = refs[0][...] + refs[1][...] + refs[2][...]
            for ref in refs[3 : 2 + groups]:
                total = total + ref[...].astype(f32)
            put_ctx(refs[2 + groups :], nn(turn_rows(16 * SLOT, total.shape[0]), total.astype(bf16)))

        outs = [unit] * 2 + [like((2,) + unit.shape)]
        finished = call(finish, [biases[2:3], stream] + list(results), 0, outs, 0, [], "finish", 8)
    if paired:
        with jax.named_scope("time_core"):
            got_time = flip_core(g_time[1])
        pairs = [(first_grads[0], first_moved[0]), (second_grads[0], second_moved[0])]
        pairs += [(first_grads[2], first_moved[1]), (second_grads[2], second_moved[1])]
        hidden_rest_a, send_a, hidden_rest_b, send_b = hidden_after_side(pairs)
        with jax.named_scope("hidden_corner"):
            corner_a, corner_b = flip_x(send_a), flip_y(send_b)
    with jax.named_scope("g1_z"):
        g1 = swap_z_out(to_frames(g1))
    if paired:
        keep_ta, send_ta, keep_tb, send_tb = after_core(g_time[0], got_time)
        with jax.named_scope("time_side"):
            side_ta, side_tb = flip_y(after(send_ta, g1)), flip_x(after(send_tb, g1))
        hidden_own, *sends = hidden_after_corner(hidden_rest_a, corner_a, hidden_rest_b, corner_b)
        sends = after(sends, send_ta)
        with jax.named_scope("hidden_line"):
            hidden_moved = [shift_z(v, k) for v, k in zip(sends, (1, 2, 1, 2, 3))]

    got = call(
        space_weights(plan, head_cols, len(w_space)),
        by_patch + g1 + [gains[0:1], shifts[0:1], key_mask, log1, p1, o1] + w_space,
        len(w_space),
        grads + [p_shape],
        n_g,
        weight_scratch + plan.grad_scratch(),
        "space_weights",
        24,
        after=(sends[0], send_ta) if paired else (),
    )
    if paired:
        got, side_ta, side_tb, hidden_moved[:2] = after((got, side_ta, side_tb, hidden_moved[:2]))
    g_space, d_space = got[:n_g], got[n_g]
    vector, *back = call(
        space_backward(plan, head_cols, len(w_space)),
        by_patch + g1 + [time_vec, up_sums, gains[0:1], d_space] + w_space,
        len(w_space),
        [vec_shape] + [unit] * 4,
        0,
        weight_scratch + [qv_held],
        "space_backward",
        16,
    )

    if paired:
        with jax.named_scope("space_core"):
            got_space = flip_core(g_space[1])
        rest_ta, send_ta, rest_tb, send_tb = after_side((keep_ta, side_ta), (keep_tb, side_tb))
        with jax.named_scope("time_corner"):
            corner_ta, corner_tb = flip_x(send_ta), flip_y(send_tb)
        with jax.named_scope("vectors"):
            other = flip_core(vector)
        got_space, other, back, corner_ta, corner_tb, hidden_moved[4] = after(
            (got_space, other, back, corner_ta, corner_tb, hidden_moved[4])
        )

        keep_a, send_a, keep_b, send_b = after_core(g_space[0], got_space)
        with jax.named_scope("space_side"):
            side_a, side_b = flip_y(send_a), flip_x(send_b)
        own_time_sum, *sends = after_corner(rest_ta, corner_ta, rest_tb, corner_tb)
        with jax.named_scope("time_line"):
            time_moved = spread(sends)
        vector, *messages = pack(back[1:], vector, other)
        side_a, side_b, messages, time_moved[:2] = after((side_a, side_b, messages, time_moved[:2]))

        rest_a, send_a, rest_b, send_b = after_side((keep_a, side_a), (keep_b, side_b))
        with jax.named_scope("space_corner"):
            corner_a, corner_b = flip_x(send_a), flip_y(send_b)
        with jax.named_scope("token_grad"):
            moved = [shift_z(v, 4 - k) for k, v in zip((1, 2, 3), after(messages, send_a))]
        with jax.named_scope("finished"):
            far = flip_y(after(finished[2], send_a))
        qkv_time, proj_time = attention_total(own_time_sum, time_moved, head_cols, 2**15)
        corner_a, corner_b, moved, far, hidden_moved[2] = after(
            (corner_a, corner_b, moved, far, hidden_moved[2])
        )

        own, *sends = after_corner(rest_a, corner_a, rest_b, corner_b)
        with jax.named_scope("space_line"):
            space_moved = spread(sends)
        with jax.named_scope("finished"):
            finished = [finished[0], flip_core(after(finished[1], far)), far, flip_core(far)]
        token_grad, vector = unpack(back[0], vector, moved, patches)
        with jax.named_scope("vectors"):
            vector = vector + flip_y(vector)
            vector = own_vectors(mesh, vector, flip_x(vector))
        hidden_keep, hidden_send = hidden_total(hidden_own, hidden_moved)
        with jax.named_scope("hidden_core"):
            hidden_got = flip_core(hidden_send)
        grad_up, grad_down = hidden_join(hidden_keep, hidden_got)
        qkv_space, proj_space = attention_total(own, space_moved, head_cols, None)
    else:

        def summed(g):
            g = lax.psum_scatter(g.astype(f32), ("shard", "ctx"), scatter_dimension=1, tiled=True)
            return lax.psum_scatter(g, "tp", scatter_dimension=0, tiled=True)[0]

        def apart(total):
            three = total[:, : 3 * head_cols].reshape(-1, 3, head_cols)
            return jnp.swapaxes(three, 0, 1), total[:, 3 * head_cols :].T

        hidden_grad = jnp.concatenate([v[i : i + 1] for i in (0, 1) for v in (first_grads[0], second_grads[0])])
        grad_up, grad_down = summed(hidden_grad[:, :model]), summed(hidden_grad[:, model:])
        qkv_time, proj_time = apart(summed(g_time[0]))
        qkv_space, proj_space = apart(summed(g_space[0]))

    with jax.named_scope("finished"):
        if not paired:
            finished = swap_ctx(*finished)
        finished = bring_back(finished, False, patches, bf16)
    if not paired:
        token_grad = bring_back(swap_z_back(back), True, patches, f32)

    if not paired:
        vector = lax.psum(vector, ("shard", "ctx", "tp"))
        vector = own_vectors(mesh, vector, jnp.zeros_like(vector))
    gains, shifts, biases, qv, hidden = vector
    return (
        finished[None],
        token_grad[None],
        gains,
        shifts,
        qkv_space,
        proj_space,
        qkv_time,
        proj_time,
        grad_up,
        grad_down.T,
        biases,
        qv.reshape(2, 2, -1),
        hidden.reshape(-1),
    )


def solution(mesh):
    return jax.shard_map(
        functools.partial(on_device, mesh),
        mesh=mesh,
        in_specs=(
            P("shard", "ctx", "tp", None),
            P("shard", "ctx", "tp", None),
            P(None, "shard"),
            P(None, "shard"),
            P(None, "shard", "tp"),
            P("tp", "shard"),
            P(None, "shard", "tp"),
            P("tp", "shard"),
            P("shard", "tp"),
            P("tp", "shard"),
            P(None, "shard"),
            P(None, None, "shard"),
            P("shard"),
        ),
        out_specs=(
            P("shard", "ctx", "tp", None),
            P("shard", "ctx", "tp", None),
            P(None, ("shard", "ctx", "tp")),
            P(None, ("shard", "ctx", "tp")),
            P(None, ("shard", "ctx"), "tp"),
            P("tp", ("shard", "ctx")),
            P(None, ("shard", "ctx"), "tp"),
            P("tp", ("shard", "ctx")),
            P(("shard", "ctx"), "tp"),
            P("tp", ("shard", "ctx")),
            P(None, ("shard", "ctx", "tp")),
            P(None, None, ("shard", "ctx", "tp")),
            P(("shard", "ctx", "tp")),
        ),
        check_vma=False,
    )
```
